32 devices in a mesh: dp: 8 (over z, core), tensor: 4 (over y, x).
Axes of the slice: x: 2, y: 2, z: 4, core: 2. Of those that a mesh axis runs over, the one named last changes fastest.
Arguments:
- hidden_in: bfloat16 [8192, 2048], P(('dp', 'tensor')), may hold values from -6 to 6
- grad_out: bfloat16 [8192, 2048], P(('dp', 'tensor')), may hold values from -6 to 6
- mix_gain: float32 [2048], replicated, may hold values from 0.5 to 1.5
- w_query: float32 [2048, 2048], P('dp', 'tensor'), may hold values from -0.125 to 0.125
- w_key: float32 [2048, 2048], P('dp', 'tensor'), may hold values from -0.125 to 0.125
- w_value: float32 [2048, 4096], P('dp', 'tensor'), may hold values from -0.125 to 0.125
- conv_query: float32 [4, 2048], P(None, ('tensor', 'dp')), may hold values from -0.5 to 0.5
- conv_key: float32 [4, 2048], P(None, ('tensor', 'dp')), may hold values from -0.5 to 0.5
- conv_value: float32 [4, 4096], P(None, ('tensor', 'dp')), may hold values from -0.5 to 0.5
- w_decay: float32 [2048, 16], P('dp', 'tensor'), may hold values from -0.125 to 0.125
- w_beta: float32 [2048, 16], P('dp', 'tensor'), may hold values from -0.125 to 0.125
- log_rate: float32 [16], replicated
- decay_bias: float32 [16], replicated, may hold values from -1.5 to 0.5
- w_outgate: float32 [2048, 4096], P('dp', 'tensor'), may hold values from -0.125 to 0.125
- head_gain: float32 [256], replicated, may hold values from 0.5 to 1.5
- w_output: float32 [4096, 2048], P('tensor', 'dp'), may hold values from -0.125 to 0.125
- ffn_gain: float32 [2048], replicated, may hold values from 0.5 to 1.5
- w_gate: float32 [2048, 5632], P('dp', 'tensor'), may hold values from -0.125 to 0.125
- w_up: float32 [2048, 5632], P('dp', 'tensor'), may hold values from -0.125 to 0.125
- w_down: float32 [5632, 2048], P('tensor', 'dp'), may hold values from -0.109375 to 0.109375
Outputs:
- hidden_out: bfloat16 [8192, 2048], P(('dp', 'tensor'))
- grad_in: bfloat16 [8192, 2048], P(('dp', 'tensor'))
- grad_mix_gain: float32 [2048], replicated
- grad_w_query: float32 [2048, 2048], P('dp', 'tensor')
- grad_w_key: float32 [2048, 2048], P('dp', 'tensor')
- grad_w_value: float32 [2048, 4096], P('dp', 'tensor')
- grad_conv_query: float32 [4, 2048], P(None, ('tensor', 'dp'))
- grad_conv_key: float32 [4, 2048], P(None, ('tensor', 'dp'))
- grad_conv_value: float32 [4, 4096], P(None, ('tensor', 'dp'))
- grad_w_decay: float32 [2048, 16], P('dp', 'tensor')
- grad_w_beta: float32 [2048, 16], P('dp', 'tensor')
- grad_log_rate: float32 [16], replicated
- grad_decay_bias: float32 [16], replicated
- grad_w_outgate: float32 [2048, 4096], P('dp', 'tensor')
- grad_head_gain: float32 [256], replicated
- grad_w_output: float32 [4096, 2048], P('tensor', 'dp')
- grad_ffn_gain: float32 [2048], replicated
- grad_w_gate: float32 [2048, 5632], P('dp', 'tensor')
- grad_w_up: float32 [2048, 5632], P('dp', 'tensor')
- grad_w_down: float32 [5632, 2048], P('tensor', 'dp')
The draws below stay inside these ranges and needn't reach their ends.
All inputs are finite; a program needn't handle non-finite values.
Results may differ from the reference program's by a relative error of at most 0.02.
Values may be sent and summed in bfloat16 or wider, within the bound.
No kernel may reach another device: no remote copies, remote signals or barrier semaphores. Data moves between devices by JAX's collectives and lax.ppermute only.
A program may use at most 320 MiB of HBM per device.

```python
import jax
import jax.numpy as jnp
from jax import lax

D = 2048
HEADS = 16
DV = 256
FF = 5632
CONV = 4
GROUP = 64
SEQ = 1024
TOKENS = 8192
KEYS = 2048
VALS = 4096


def draw_log_rate(key, part):
    fraction = jax.random.uniform(key, (HEADS,), jnp.float32)
    low_end = jnp.log(0.5 / SEQ)
    high_end = jnp.log(0.05)
    return (low_end + (high_end - low_end) * fraction).astype(jnp.float32)


def steps_of(stream_key, shape, split, least, top_value):
    factor_of, own = 1.0, jax.random.fold_in(stream_key, 6)
    for axis_at, blocks in split:
        draws = jnp.exp(jax.random.uniform(jax.random.fold_in(own, axis_at), (blocks,), jnp.float32, least / len(split), top_value / len(split)))
        factor_of = factor_of * jnp.repeat(draws, shape[axis_at] // blocks).reshape([-1 if axis == axis_at else 1 for axis in range(len(shape))])
    return factor_of


def normal_values(own_key, shape, scale, reach, pieces=(), kind=jnp.bfloat16):
    drawn = jax.random.normal(own_key, shape, jnp.float32) * scale
    if len(pieces) > 0:
        drawn = steps_of(own_key, shape, pieces, -0.22, 0.18) * drawn
    return jnp.clip(drawn, min=-reach, max=reach).astype(kind)


def setup_inputs(seed: int = 0) -> dict:
    seeds = jax.random.split(jax.random.key(seed), 21)
    return {
        "hidden_in": normal_values(seeds[0], (TOKENS, D), 1.0, 6.0, ((0, 32),)),
        "grad_out": normal_values(seeds[1], (TOKENS, D), 1.0, 6.0, ((0, 32),)),
        "mix_gain": jnp.clip(1.0 + 0.1 * jax.random.normal(seeds[2], (D,), jnp.float32), 0.5, 1.5),
        "w_query": normal_values(seeds[3], (D, KEYS), D ** -0.5, 0.125, ((0, 8), (1, 4)), jnp.float32),
        "w_key": normal_values(seeds[4], (D, KEYS), D ** -0.5, 0.125, ((0, 8), (1, 4)), jnp.float32),
        "w_value": normal_values(seeds[5], (D, VALS), D ** -0.5, 0.125, ((0, 8), (1, 4)), jnp.float32),
        "conv_query": jnp.clip(jax.random.uniform(seeds[6], (CONV, KEYS), jnp.float32, -0.5, 0.5) * steps_of(seeds[6], (CONV, KEYS), ((1, 32),), -0.4, 0.0), -0.5, 0.5),
        "conv_key": jnp.clip(jax.random.uniform(seeds[7], (CONV, KEYS), jnp.float32, -0.5, 0.5) * steps_of(seeds[7], (CONV, KEYS), ((1, 32),), -0.4, 0.0), -0.5, 0.5),
        "conv_value": jnp.clip(jax.random.uniform(seeds[8], (CONV, VALS), jnp.float32, -0.5, 0.5) * steps_of(seeds[8], (CONV, VALS), ((1, 32),), -0.4, 0.0), -0.5, 0.5),
        "w_decay": normal_values(seeds[9], (D, HEADS), D ** -0.5, 0.125, ((0, 8), (1, 4)), jnp.float32),
        "w_beta": normal_values(seeds[10], (D, HEADS), D ** -0.5, 0.125, ((0, 8), (1, 4)), jnp.float32),
        "log_rate": draw_log_rate(jax.random.fold_in(seeds[20], 71), 0),
        "decay_bias": jnp.clip(jax.random.uniform(seeds[12], (HEADS,), jnp.float32, -1.5, 0.5), -1.5, 0.5),
        "w_outgate": normal_values(seeds[13], (D, VALS), D ** -0.5, 0.125, ((0, 8), (1, 4)), jnp.float32),
        "head_gain": jnp.clip(1.0 + 0.1 * jax.random.normal(seeds[14], (DV,), jnp.float32), 0.5, 1.5),
        "w_output": normal_values(seeds[15], (VALS, D), (VALS // 2) ** -0.5, 0.125, ((0, 4), (1, 8)), jnp.float32),
        "ffn_gain": jnp.clip(1.0 + 0.1 * jax.random.normal(seeds[16], (D,), jnp.float32), 0.5, 1.5),
        "w_gate": normal_values(seeds[17], (D, FF), D ** -0.5, 0.125, ((0, 8), (1, 4)), jnp.float32),
        "w_up": normal_values(seeds[18], (D, FF), D ** -0.5, 0.125, ((0, 8), (1, 4)), jnp.float32),
        "w_down": normal_values(seeds[19], (FF, D), (FF // 2) ** -0.5, 0.109375, ((0, 4), (1, 8)), jnp.float32),
    }


@jax.custom_vjp
def low(v):
    return lax.optimization_barrier(v.astype(jnp.bfloat16)).astype(jnp.float32)

@jax.custom_vjp
def low_back(v):
    return v

def low_keep(v):
    return (low(v), None)

def low_pass(kept, grad):
    return (grad,)

def back_keep(v):
    return (v, None)

def back_low(kept, grad):
    return (low(grad),)
low.defvjp(low_keep, low_pass)
low_back.defvjp(back_keep, back_low)
highest_precision = lax.Precision.HIGHEST

def matmul(matrix_a, matrix_b):
    return jnp.dot(matrix_a.astype(jnp.float32), matrix_b.astype(jnp.float32), precision=highest_precision, preferred_element_type=jnp.float32)

def rms_norm(values, gain_vec):
    return values * lax.rsqrt(lax.optimization_barrier(jnp.mean(values * values, -1, keepdims=True)) + 1e-05) * gain_vec

def unit_norm(values):
    return values * lax.rsqrt(lax.optimization_barrier(jnp.sum(values * values, -1, keepdims=True)) + 1e-06)

def conv_silu(projected, kernel):
    tap_count = kernel.shape[0]
    row_count = projected.shape[0]
    padded = jnp.pad(projected, ((tap_count - 1, 0), (0, 0)))
    running = padded[0:row_count] * kernel[0]
    for offset in range(1, tap_count):
        running = running + padded[offset:offset + row_count] * kernel[offset]
    return jax.nn.silu(running)

def group_step(carried_state, block_in):
    query_rows, key_matrix_rows, value_rows, log_gates, write_rate = block_in
    tri_size = query_rows.shape[1]
    cumulative_decay_sum = jnp.cumsum(log_gates, axis=-1)
    differ = cumulative_decay_sum[:, :, None] - cumulative_decay_sum[:, None, :]
    positions = jnp.arange(tri_size)
    inclusive = positions[:, None] >= positions[None, :]
    strictly = positions[:, None] > positions[None, :]
    relative = jnp.where(inclusive, jnp.exp(jnp.minimum(differ, 0.0)), 0.0)
    key_key = jnp.einsum('hck,hdk->hcd', key_matrix_rows, key_matrix_rows, precision=highest_precision)
    lower_part = jnp.where(strictly, write_rate[:, :, None] * relative * key_key, 0.0)
    system = lower_part + jnp.eye(tri_size, dtype=jnp.float32)
    start_decay = jnp.exp(cumulative_decay_sum)
    state_contribution = jnp.einsum('zrg,zgl->zrl', key_matrix_rows, carried_state, precision=highest_precision)
    right_side = write_rate[..., None] * (value_rows - start_decay[..., None] * state_contribution)
    delta_updates = jax.scipy.linalg.solve_triangular(system, right_side, lower=True, unit_diagonal=True)
    query_key = jnp.einsum('hck,hdk->hcd', query_rows, key_matrix_rows, precision=highest_precision)
    state_readout = jnp.einsum('zrg,zgl->zrl', query_rows, carried_state, precision=highest_precision)
    outputs = start_decay[..., None] * state_readout + jnp.einsum('hcd,hdv->hcv', relative * query_key, delta_updates, precision=highest_precision)
    decay_to_final = jnp.exp(cumulative_decay_sum[:, -1:] - cumulative_decay_sum)
    following_state = jnp.exp(cumulative_decay_sum[:, -1])[:, None, None] * carried_state + jnp.einsum('pgs,pgd->psd', key_matrix_rows * decay_to_final[..., None], delta_updates, precision=highest_precision)
    return (following_state, outputs)

def delta_rule(query_rows, key_matrix_rows, value_rows, log_gates, write_rate):
    seq_rows, head_count, key_size = query_rows.shape
    value_size = value_rows.shape[2]
    blocks = seq_rows // GROUP

    def to_blocks(tensor_in):
        reshaped = tensor_in.reshape((blocks, GROUP) + tensor_in.shape[1:])
        return jnp.swapaxes(reshaped, 1, 2)
    initial = jnp.zeros((head_count, key_size, value_size), jnp.float32)
    final_state, outputs = lax.scan(jax.checkpoint(group_step), initial, (to_blocks(query_rows), to_blocks(key_matrix_rows), to_blocks(value_rows), to_blocks(log_gates), to_blocks(write_rate)))
    return jnp.swapaxes(outputs, 1, 2).reshape(seq_rows, head_count, value_size)

def mixer_core(proj_query, proj_key, proj_value, proj_outgate, proj_decay, proj_beta, kernel_query, kernel_key, kernel_value, rate_log, rate_bias, norm_gain):
    seq_rows, head_count = proj_decay.shape
    query_rows = conv_silu(proj_query, kernel_query).reshape(seq_rows, head_count, -1)
    query_rows = unit_norm(query_rows) * query_rows.shape[-1] ** (-0.5)
    key_matrix_rows = unit_norm(conv_silu(proj_key, kernel_key).reshape(seq_rows, head_count, -1))
    value_rows = conv_silu(proj_value, kernel_value).reshape(seq_rows, head_count, -1)
    write_rate = jax.nn.sigmoid(proj_beta)
    log_gates = -jnp.exp(rate_log) * jax.nn.softplus(proj_decay + rate_bias)
    mixed = delta_rule(query_rows, key_matrix_rows, value_rows, log_gates, write_rate)
    mixed = rms_norm(mixed, norm_gain)
    return mixed.reshape(seq_rows, -1) * jax.nn.silu(proj_outgate)

def forward(hidden_in, mix_gain, w_query, w_key, w_value, conv_query, conv_key, conv_value, w_decay, w_beta, log_rate, decay_bias, w_outgate, head_gain, w_output, ffn_gain, w_gate, w_up, w_down):
    low_query = low(w_query)
    low_key = low(w_key)
    low_value = low(w_value)
    low_conv_q = low(conv_query)
    low_conv_k = low(conv_key)
    low_conv_v = low(conv_value)
    low_decay = low(w_decay)
    low_beta = low(w_beta)
    low_outgate = low(w_outgate)
    low_output = low(w_output)
    low_gate = low(w_gate)
    low_up = low(w_up)
    low_down = low(w_down)

    def one_sequence(rows_in):
        normed = low(rms_norm(rows_in, mix_gain))
        proj_query = low_back(matmul(normed, low_query))
        proj_key = low_back(matmul(normed, low_key))
        proj_value = low_back(matmul(normed, low_value))
        proj_outgate = low_back(matmul(normed, low_outgate))
        proj_decay = low_back(matmul(normed, low_decay))
        proj_beta = low_back(matmul(normed, low_beta))
        mixed = low(mixer_core(proj_query, proj_key, proj_value, proj_outgate, proj_decay, proj_beta, low_conv_q, low_conv_k, low_conv_v, log_rate, decay_bias, head_gain))
        middle = rows_in + low_back(matmul(mixed, low_output))
        ffn_in = low(rms_norm(middle, ffn_gain))
        gate_pre = low_back(matmul(ffn_in, low_gate))
        up_pre = low_back(matmul(ffn_in, low_up))
        activ = low(jax.nn.silu(gate_pre) * up_pre)
        return middle + matmul(activ, low_down)
    sequences = hidden_in.reshape(-1, SEQ, hidden_in.shape[1])
    return lax.map(jax.checkpoint(one_sequence), sequences).reshape(hidden_in.shape)

def reference(hidden_in, grad_out, mix_gain, w_query, w_key, w_value, conv_query, conv_key, conv_value, w_decay, w_beta, log_rate, decay_bias, w_outgate, head_gain, w_output, ffn_gain, w_gate, w_up, w_down):
    primals = (hidden_in.astype(jnp.float32), mix_gain, w_query, w_key, w_value, conv_query, conv_key, conv_value, w_decay, w_beta, log_rate, decay_bias, w_outgate, head_gain, w_output, ffn_gain, w_gate, w_up, w_down)
    result, pullback = jax.vjp(forward, *primals)
    grads = pullback(grad_out.astype(jnp.float32))
    return (result.astype(jnp.bfloat16), grads[0].astype(jnp.bfloat16), grads[1], grads[2], grads[3], grads[4], grads[5], grads[6], grads[7], grads[8], grads[9], grads[10], grads[11], grads[12], grads[13], grads[14], grads[15], grads[16], grads[17], grads[18])
```

```python
import jax
import jax.numpy as jnp
from jax import lax
from jax.experimental import pallas as pl
from jax.experimental.pallas import tpu as pltpu
from jax.sharding import PartitionSpec as P

GROUP = 64
TAIL = 8
F32 = jnp.float32
BF16 = jnp.bfloat16
HIGHEST = lax.Precision.HIGHEST


def mm(a, b, dims=((1,), (0,))):
    return lax.dot_general(a.astype(BF16), b.astype(BF16), (dims, ((), ())), preferred_element_type=F32)


NN = ((1,), (0,))
NT = ((1,), (1,))
TN = ((0,), (0,))


def mm_exact(a, b, dims=NN):
    return lax.dot_general(a, b, (dims, ((), ())), precision=HIGHEST, preferred_element_type=F32)


def halves(a):
    high = a.astype(BF16)
    return high, (a - high.astype(F32)).astype(BF16)


def mm_split(a, b):
    a_high, a_low = halves(a)
    b_high, b_low = halves(b)
    return mm(a_high, b_high) + (mm(a_high, b_low) + mm(a_low, b_high))


def sigmoid(x):
    return 1.0 / (1.0 + jnp.exp(-x))


def softplus(x):
    return jnp.maximum(x, 0.0) + jnp.log1p(jnp.exp(-jnp.abs(x)))


def grid_iota(size):
    return (
        lax.broadcasted_iota(jnp.int32, (size, size), 0),
        lax.broadcasted_iota(jnp.int32, (size, size), 1),
    )


def unit_lower_inverses(lowers, row, col):
    size = lowers[0].shape[0]
    base = 16
    eye = jnp.where(row == col, 1.0, 0.0)
    powers = [jnp.where(row // base == col // base, -lower, 0.0) for lower in lowers]
    inverses = [eye + power for power in powers]
    reach = 2
    while reach < base:
        powers = [mm_split(power, power) for power in powers]
        inverses = [inverse + mm_split(inverse, power) for inverse, power in zip(inverses, powers)]
        reach *= 2
    while base < size:
        wide = 2 * base
        off = (row // wide == col // wide) & (row // base > col // base)
        right = [mm_split(jnp.where(off, lower, 0.0), inverse) for lower, inverse in zip(lowers, inverses)]
        inverses = [inverse - mm_split(inverse, r) for inverse, r in zip(inverses, right)]
        base = wide
    return inverses


def gates(p_ab, rate, bias, heads):
    pre = p_ab[:, :heads] + bias
    return sigmoid(p_ab[:, heads:]), -jnp.exp(rate) * softplus(pre), pre


def forward_kernel(
    pqkv, po, pab, taps, rate, bias, gain,
    mixed, conved, o_out, u_out, s_out, t_out,
    ext, state,
):
    heads = rate.shape[1]
    vals = po.shape[1]
    keys = (pqkv.shape[1] - vals) // 2
    dk, dv = keys // heads, vals // heads

    @pl.when(pl.program_id(0) == 0)
    def _():
        ext[...] = jnp.zeros_like(ext)
        state[...] = jnp.zeros_like(state)

    ext[TAIL:, :] = pqkv[...]
    n_taps = taps.shape[0]
    total = None
    for i in range(n_taps):
        start = TAIL - (n_taps - 1) + i
        term = ext[start : start + GROUP, :] * taps[i : i + 1, :]
        total = term if total is None else total + term
    conved[...] = total
    ext[:TAIL, :] = ext[GROUP:, :]

    row, col = grid_iota(GROUP)
    tri = jnp.where(row >= col, 1.0, 0.0)
    beta, log_decay, _ = gates(pab[...], rate[...], bias[...], heads)
    c_col = mm_exact(tri, log_decay)
    c_row = mm_exact(log_decay, jnp.where(row <= col, 1.0, 0.0), TN)
    start_decay = jnp.exp(c_col)
    end_decay = jnp.exp(c_col[GROUP - 1 :, :] - c_col)
    last_decay = jnp.exp(c_col[GROUP - 1 :, :])

    qs, ks, vs, bs, prods, relatives, lowers = [], [], [], [], [], [], []
    for h in range(heads):
        uq = conved[:, h * dk : (h + 1) * dk]
        uk = conved[:, keys + h * dk : keys + (h + 1) * dk]
        uv = conved[:, 2 * keys + h * dv : 2 * keys + (h + 1) * dv]
        q = uq * sigmoid(uq)
        qs.append(q * (lax.rsqrt(jnp.sum(q * q, -1, keepdims=True) + 1e-6) * dk**-0.5))
        k = uk * sigmoid(uk)
        ks.append(k * lax.rsqrt(jnp.sum(k * k, -1, keepdims=True) + 1e-6))
        vs.append(uv * sigmoid(uv))
        bs.append(beta[:, h : h + 1])
    for h in range(heads):
        prods.append(mm(jnp.concatenate([ks[h], qs[h]], 0), ks[h], NT))
    for h in range(heads):
        differ = jnp.minimum(c_col[:, h : h + 1] - c_row[h : h + 1, :], 0.0)
        relatives.append(jnp.where(row >= col, jnp.exp(differ), 0.0))
        lowers.append(jnp.where(row > col, bs[h] * relatives[h] * prods[h][:GROUP], 0.0))
    invs = [inverse.astype(BF16) for inverse in unit_lower_inverses(lowers, row, col)]
    states = [state[h] for h in range(heads)]
    lows = [s.astype(BF16) for s in states]
    reads = []
    for h in range(heads):
        e = start_decay[:, h : h + 1]
        reads.append(mm(jnp.concatenate([ks[h] * e, qs[h] * e], 0), lows[h]))
    us = [mm(invs[h], bs[h] * (vs[h] - reads[h][:GROUP])).astype(BF16) for h in range(heads)]
    outs = [reads[h][GROUP:] + mm(relatives[h] * prods[h][GROUP:], us[h]) for h in range(heads)]
    nexts = [
        last_decay[:, h : h + 1] * states[h] + mm(ks[h] * end_decay[:, h : h + 1], us[h], TN) for h in range(heads)
    ]
    for h in range(heads):
        cols = slice(h * dv, (h + 1) * dv)
        state[h] = nexts[h]
        t_out[0, h] = invs[h]
        s_out[0, h] = lows[h]
        u_out[:, cols] = us[h]
        o = outs[h]
        o_out[:, cols] = o.astype(o_out.dtype)
        n = o * lax.rsqrt(jnp.mean(o * o, -1, keepdims=True) + 1e-5)
        gate = po[:, cols]
        mixed[:, cols] = (n * gain[...] * (gate * sigmoid(gate))).astype(mixed.dtype)


def core_forward(pqkv, po, pab, taps, rate, bias, gain):
    rows, width = pqkv.shape
    vals = po.shape[1]
    keys = (width - vals) // 2
    heads = rate.shape[1]
    dk, dv = keys // heads, vals // heads
    blocks = rows // GROUP
    tokens = lambda width: pl.BlockSpec((GROUP, width), lambda n: (n, 0))
    fixed = lambda a: pl.BlockSpec(a.shape, lambda n: (0, 0))
    return pl.pallas_call(
        forward_kernel,
        grid=(blocks,),
        in_specs=[tokens(a.shape[1]) for a in (pqkv, po, pab)] + [fixed(a) for a in (taps, rate, bias, gain)],
        out_specs=[
            tokens(vals),
            tokens(2 * keys + vals),
            tokens(vals),
            tokens(vals),
            pl.BlockSpec((1, heads, dk, dv), lambda n: (n, 0, 0, 0)),
            pl.BlockSpec((1, heads, GROUP, GROUP), lambda n: (n, 0, 0, 0)),
        ],
        out_shape=[
            jax.ShapeDtypeStruct((rows, vals), BF16),
            jax.ShapeDtypeStruct((rows, 2 * keys + vals), F32),
            jax.ShapeDtypeStruct((rows, vals), BF16),
            jax.ShapeDtypeStruct((rows, vals), BF16),
            jax.ShapeDtypeStruct((blocks, heads, dk, dv), BF16),
            jax.ShapeDtypeStruct((blocks, heads, GROUP, GROUP), BF16),
        ],
        scratch_shapes=[
            pltpu.VMEM((GROUP + TAIL, 2 * keys + vals), F32),
            pltpu.VMEM((heads, dk, dv), F32),
        ],
        compiler_params=pltpu.CompilerParams(dimension_semantics=("arbitrary",), vmem_limit_bytes=40 * 2**20),
        cost_estimate=pl.CostEstimate(flops=8 * 10**9, bytes_accessed=32 * 2**20, transcendentals=10**7),
        name="core_forward",
    )(pqkv, po, pab, taps, rate, bias, gain)


def backward_kernel(
    gz, pqkv, po, pab, conved, o_in, u_in, s_in, t_in, taps, rate, bias, gain,
    dpqkv, dpo, dpab, dtaps, dsmall, dgain,
    ext, dstate,
):
    heads = rate.shape[1]
    vals = po.shape[1]
    keys = (pqkv.shape[1] - vals) // 2
    dk, dv = keys // heads, vals // heads

    @pl.when(pl.program_id(0) == 0)
    def _():
        ext[...] = jnp.zeros_like(ext)
        dstate[...] = jnp.zeros_like(dstate)
        for ref in (dtaps, dsmall, dgain):
            ref[...] = jnp.zeros_like(ref)

    row, col = grid_iota(GROUP)
    tri = jnp.where(row >= col, 1.0, 0.0)
    upper = jnp.where(row <= col, 1.0, 0.0)
    beta, log_decay, pre = gates(pab[...], rate[...], bias[...], heads)
    c_col = mm_exact(tri, log_decay)
    c_row = mm_exact(log_decay, upper, TN)
    start_decay = jnp.exp(c_col)
    end_decay = jnp.exp(c_col[GROUP - 1 :, :] - c_col)
    last_decay = jnp.exp(c_col[GROUP - 1 :, :])
    lane = lax.broadcasted_iota(jnp.int32, (1, heads), 1)
    d_beta = jnp.zeros((GROUP, heads), F32)
    after = jnp.zeros((GROUP, heads), F32)
    before = jnp.zeros((GROUP, heads), F32)
    d_log = jnp.zeros((GROUP, heads), F32)
    gain_sum = jnp.zeros((1, dv), F32)

    for h in range(heads):
        ks, vs = slice(h * dk, (h + 1) * dk), slice(h * dv, (h + 1) * dv)
        kx, vx = slice(keys + h * dk, keys + (h + 1) * dk), slice(2 * keys + h * dv, 2 * keys + (h + 1) * dv)
        here = lane == h
        uq, uk, uv = conved[:, ks], conved[:, kx], conved[:, vx]
        sq, sk, sv = sigmoid(uq), sigmoid(uk), sigmoid(uv)
        q = uq * sq
        q_norm = lax.rsqrt(jnp.sum(q * q, -1, keepdims=True) + 1e-6)
        q = q * q_norm
        k = uk * sk
        k_norm = lax.rsqrt(jnp.sum(k * k, -1, keepdims=True) + 1e-6)
        k = k * k_norm
        v = uv * sv
        qs = q * dk**-0.5
        b = beta[:, h : h + 1]
        e = start_decay[:, h : h + 1]
        f = end_decay[:, h : h + 1]
        kb = k.astype(BF16)
        qb = qs.astype(BF16)

        o = o_in[:, vs].astype(F32)
        o_norm = lax.rsqrt(jnp.mean(o * o, -1, keepdims=True) + 1e-5)
        n = o * o_norm
        gate = po[:, vs]
        sg = sigmoid(gate)
        g = gz[:, vs]
        gn = g * n
        act = gate * sg
        gain_sum = gain_sum + jnp.sum(gn * act, 0, keepdims=True)
        dpo[:, vs] = (gn * gain[...] * (sg * (1.0 + gate * (1.0 - sg)))).astype(dpo.dtype)
        dn = g * gain[...] * act
        do = o_norm * (dn - n * jnp.mean(dn * n, -1, keepdims=True))

        prod = mm(jnp.concatenate([kb, qb], 0), kb, NT)
        relative = jnp.where(row >= col, jnp.exp(jnp.minimum(c_col[:, h : h + 1] - c_row[h : h + 1, :], 0.0)), 0.0)
        kk, qk = prod[:GROUP], prod[GROUP:]
        strict = jnp.where(row > col, relative, 0.0)
        mix = relative * qk
        s_prev = s_in[0, h]
        u = u_in[:, vs]
        inv = t_in[0, h]
        ds = dstate[h]
        ds_low = ds.astype(BF16)
        dob = do.astype(BF16)
        ke, qe, kd = k * e, qs * e, k * f
        du = mm(mix, dob, TN) + mm(kd, ds_low)
        dr = mm(inv, du, TN)
        pair = jnp.concatenate([dob, dr.astype(BF16)], 0)
        dstate[h] = last_decay[:, h : h + 1] * ds + mm(jnp.concatenate([qe, -(b * ke)], 0), pair, TN)
        cross = mm(pair, u, NT)
        dmix = jnp.where(row >= col, cross[:GROUP], 0.0)
        dlow = jnp.where(row > col, -cross[GROUP:], 0.0)
        back = mm(pair, s_prev, NT)
        dqe, x = back[:GROUP], back[GROUP:]
        dkd = mm(u, ds_low, NT)
        dke = -(b * x)
        rk = strict * kk
        d_beta = d_beta + jnp.where(
            here,
            jnp.sum(dr * v, -1, keepdims=True) - jnp.sum(x * ke, -1, keepdims=True) + jnp.sum(dlow * rk, -1, keepdims=True),
            0.0,
        )
        dpair = dlow * (b * rk) + dmix * mix
        spread = mm(upper, dpair)
        last_part = last_decay[:, h : h + 1] * jnp.sum(ds * s_prev.astype(F32), keepdims=True)
        d_log = d_log + jnp.where(here, jnp.sum(jnp.where(row > col, spread, 0.0), -1, keepdims=True) + last_part, 0.0)
        after = after + jnp.where(here, jnp.sum(dqe * qe + dke * ke, -1, keepdims=True), 0.0)
        before = before + jnp.where(here, jnp.sum(dkd * kd, -1, keepdims=True), 0.0)
        dqk = dmix * relative
        dkk = dlow * (b * strict)
        first = mm(jnp.concatenate([dqk, dkk], 0), kb)
        dq = e * dqe + first[:GROUP]
        dk_ = e * dke + f * dkd + first[GROUP:] + mm(jnp.concatenate([dkk, dqk], 0), jnp.concatenate([kb, qb], 0), TN)
        dq = dq * dk**-0.5
        dq = q_norm * (dq - q * jnp.sum(dq * q, -1, keepdims=True))
        dk_ = k_norm * (dk_ - k * jnp.sum(dk_ * k, -1, keepdims=True))
        ext[:GROUP, ks] = dq * (sq * (1.0 + uq * (1.0 - sq)))
        ext[:GROUP, kx] = dk_ * (sk * (1.0 + uk * (1.0 - sk)))
        ext[:GROUP, vx] = (b * dr) * (sv * (1.0 + uv * (1.0 - sv)))

    d_log = d_log + mm_exact(upper, after) + mm_exact(jnp.where(row > col, 1.0, 0.0), before)
    d_pre = d_log * (-jnp.exp(rate[...])) * sigmoid(pre)
    dpab[:, :heads] = d_pre
    dpab[:, heads:] = d_beta * beta * (1.0 - beta)
    dsmall[0:1, :heads] += jnp.sum(d_log * log_decay, 0, keepdims=True)
    dsmall[0:1, heads:] += jnp.sum(d_pre, 0, keepdims=True)
    dgain[...] += gain_sum

    n_taps = taps.shape[0]
    rows_in = pqkv[...]
    total = None
    for i in range(n_taps):
        start = n_taps - 1 - i
        piece = ext[start : start + GROUP, :]
        term = piece * taps[i : i + 1, :]
        total = term if total is None else total + term
        dtaps[i : i + 1, :] += jnp.sum(piece * rows_in, 0, keepdims=True)
    dpqkv[...] = total.astype(dpqkv.dtype)
    ext[GROUP:, :] = ext[:TAIL, :]


def core_backward(gz, pqkv, po, pab, kept, taps, rate, bias, gain):
    conved, o_in, u_in, s_in, t_in = kept
    rows, width = pqkv.shape
    vals = po.shape[1]
    keys = (width - vals) // 2
    heads = rate.shape[1]
    dk, dv = keys // heads, vals // heads
    blocks = rows // GROUP
    tokens = lambda width: pl.BlockSpec((GROUP, width), lambda n: (blocks - 1 - n, 0))
    stacked = lambda a: pl.BlockSpec((1,) + a.shape[1:], lambda n: (blocks - 1 - n, 0, 0, 0))
    fixed = lambda shape: pl.BlockSpec(shape, lambda n: (0, 0))
    small = (1, 2 * heads)
    return pl.pallas_call(
        backward_kernel,
        grid=(blocks,),
        in_specs=[tokens(a.shape[1]) for a in (gz, pqkv, po, pab, conved, o_in, u_in)]
        + [stacked(s_in), stacked(t_in)]
        + [fixed(a.shape) for a in (taps, rate, bias, gain)],
        out_specs=[tokens(a.shape[1]) for a in (pqkv, po, pab)]
        + [fixed(taps.shape), fixed(small), fixed(gain.shape)],
        out_shape=[jax.ShapeDtypeStruct(a.shape, BF16) for a in (pqkv, po)]
        + [jax.ShapeDtypeStruct(pab.shape, F32)]
        + [jax.ShapeDtypeStruct(s, F32) for s in (taps.shape, small, gain.shape)],
        scratch_shapes=[
            pltpu.VMEM((GROUP + TAIL, 2 * keys + vals), F32),
            pltpu.VMEM((heads, dk, dv), F32),
        ],
        compiler_params=pltpu.CompilerParams(dimension_semantics=("arbitrary",), vmem_limit_bytes=40 * 2**20),
        cost_estimate=pl.CostEstimate(flops=20 * 10**9, bytes_accessed=48 * 2**20, transcendentals=10**7),
        name="core_backward",
    )(gz, pqkv, po, pab, conved, o_in, u_in, s_in, t_in, taps, rate, bias, gain)


def rms_norm(values, gain_vec):
    return values * lax.rsqrt(jnp.mean(values * values, -1, keepdims=True) + 1e-05) * gain_vec


def dot(a, b, dims=NN):
    return lax.dot_general(a, b, (dims, ((), ())), preferred_element_type=F32)


def swap(piece, mask):
    return lax.ppermute(piece, "tensor", [(i, i ^ mask) for i in range(4)])


def gather_rows(own):
    if lax.axis_size("tensor") != 4:
        return lax.all_gather(own, "tensor", axis=0, tiled=True)
    half = own.shape[0] // 2
    first, second = swap(own, 1), swap(own, 2)
    return jnp.concatenate([own, first, second, swap(second[:half], 1), swap(first[half:], 2)], 0)


def scatter_rows(part):
    if lax.axis_size("tensor") != 4:
        return lax.psum_scatter(part, "tensor", scatter_dimension=0, tiled=True).astype(F32)
    rows, half = part.shape[0] // 4, part.shape[1] // 2

    def chunk(k, columns):
        return part[k * rows : (k + 1) * rows, columns]

    sums = []
    for columns, one, two in ((slice(0, half), 1, 2), (slice(half, 2 * half), 2, 1)):
        got = swap(jnp.concatenate([chunk(one, columns), chunk(3, columns)], 0), one).astype(F32)
        own = chunk(0, columns).astype(F32) + got[:rows]
        passed = (chunk(two, columns).astype(F32) + got[rows:]).astype(BF16)
        sums.append(own + swap(passed, two).astype(F32))
    return jnp.concatenate(sums, 1)


def reorder(rows_in):
    if lax.axis_size("tensor") != 4:
        return rows_in
    rows = rows_in.shape[0] // 4
    me = lax.axis_index("tensor")
    return jnp.concatenate([lax.dynamic_slice_in_dim(rows_in, (me ^ k) * rows, rows, 0) for k in range(4)], 0)


def norm_back(values, gain_vec, grad):
    factor = lax.rsqrt(jnp.mean(values * values, -1, keepdims=True) + 1e-05)
    normal = values * factor
    scaled = grad * gain_vec
    return (
        factor * (scaled - normal * jnp.mean(scaled * normal, -1, keepdims=True)),
        jnp.sum(grad * normal, 0),
    )


def gather_dp(shard, axis):
    return lax.all_gather(shard.astype(BF16), "dp", axis=axis, tiled=True)


def scatter_dp(part, axis):
    return lax.psum_scatter(part.astype(BF16), "dp", scatter_dimension=axis, tiled=True).astype(F32)


def local(
    hidden_in,
    grad_out,
    mix_gain,
    w_query,
    w_key,
    w_value,
    conv_query,
    conv_key,
    conv_value,
    w_decay,
    w_beta,
    log_rate,
    decay_bias,
    w_outgate,
    head_gain,
    w_output,
    ffn_gain,
    w_gate,
    w_up,
    w_down,
):
    dp = lax.axis_size("dp")
    model = hidden_in.shape[1]
    keys, vals, hidden = w_query.shape[1], w_value.shape[1], w_gate.shape[1]
    heads = w_decay.shape[1]
    first_head = lax.axis_index("tensor") * heads
    rate = lax.dynamic_slice_in_dim(log_rate, first_head, heads)[None]
    bias = lax.dynamic_slice_in_dim(decay_bias, first_head, heads)[None]
    gain = head_gain[None]

    narrow = jnp.concatenate([w_decay, w_beta], 1).T
    kernels = jnp.concatenate([conv_query, conv_key, conv_value], 1)
    wide = max(narrow.shape[1], kernels.shape[1])
    pad = lambda a: jnp.pad(a, ((0, 0), (0, wide - a.shape[1])))
    few = lax.all_gather(jnp.concatenate([pad(narrow), pad(kernels)], 0).astype(BF16), "dp")
    unroll = lambda a: jnp.swapaxes(a, 0, 1).reshape(a.shape[1], -1)
    full_narrow = unroll(few[:, : 2 * heads, : narrow.shape[1]])
    pieces = few[:, 2 * heads :, : kernels.shape[1]]
    cut = (conv_query.shape[1], conv_query.shape[1] + conv_key.shape[1])
    taps = jnp.concatenate(
        [unroll(pieces[:, :, : cut[0]]), unroll(pieces[:, :, cut[0] : cut[1]]), unroll(pieces[:, :, cut[1] :])], 1
    ).astype(F32)

    full_qkv = gather_dp(jnp.concatenate([w_query, w_key, w_value], 1), 0)
    full_outgate = gather_dp(w_outgate, 0)
    full_output = gather_dp(w_output, 1)
    full_pair = gather_dp(jnp.concatenate([w_gate, w_up], 1), 0)
    full_down = gather_dp(w_down, 1)

    rows_in = hidden_in.astype(F32)
    normed = reorder(gather_rows(rms_norm(rows_in, mix_gain).astype(BF16)))
    pqkv = dot(normed, full_qkv)
    pab = dot(normed, full_narrow, NT)
    po = dot(normed, full_outgate)
    mixed, *kept = core_forward(pqkv, po, pab, taps, rate, bias, gain)
    middle = rows_in + scatter_rows(reorder(dot(mixed, full_output).astype(BF16)))

    ffn_rows = gather_rows(rms_norm(middle, ffn_gain).astype(BF16))
    pre = dot(ffn_rows, full_pair)
    gate_pre, up_pre = pre[:, :hidden], pre[:, hidden:]
    gate_sig = jax.nn.sigmoid(gate_pre)
    activ = (gate_pre * gate_sig * up_pre).astype(BF16)
    cot = gather_rows(grad_out)
    grad_w_down = scatter_dp(dot(activ, cot, TN), 1)
    hidden_out = (middle + scatter_rows(dot(activ, full_down).astype(BF16))).astype(BF16)
    grad_activ = dot(cot, full_down, NT)
    grad_gate_pre = (grad_activ * up_pre * gate_sig * (1.0 + gate_pre * (1.0 - gate_sig))).astype(BF16)
    grad_up_pre = (grad_activ * (gate_pre * gate_sig)).astype(BF16)
    grad_pre = jnp.concatenate([grad_gate_pre, grad_up_pre], 1)
    grad_pair = scatter_dp(dot(ffn_rows, grad_pre, TN), 0)
    grad_ffn_norm = scatter_rows(dot(grad_pre, full_pair, NT).astype(BF16))
    grad_middle_norm, ffn_gain_part = norm_back(middle, ffn_gain, grad_ffn_norm)
    grad_middle = grad_out.astype(F32) + grad_middle_norm

    mix_cot = reorder(gather_rows(grad_middle.astype(BF16)))
    grad_mixed = dot(mix_cot, full_output, NT)
    grad_w_output = scatter_dp(dot(mixed, mix_cot, TN), 1)
    grad_pqkv, grad_po, grad_pab, grad_taps, grad_small, grad_gain = core_backward(
        grad_mixed, pqkv, po, pab, kept, taps, rate, bias, gain
    )
    grad_w_outgate = scatter_dp(dot(normed, grad_po, TN), 0)
    grad_qkv = scatter_dp(dot(normed, grad_pqkv, TN), 0)
    low_pab = grad_pab.astype(BF16)
    grad_normed = dot(grad_pqkv, full_qkv, NT) + dot(grad_po, full_outgate, NT) + dot(low_pab, full_narrow)
    grad_mix_norm = scatter_rows(reorder(grad_normed.astype(BF16)))
    grad_rows, mix_gain_part = norm_back(rows_in, mix_gain, grad_mix_norm)
    grad_in = (grad_middle + grad_rows).astype(BF16)

    grad_narrow = dot(low_pab, normed, TN)
    roll = lambda a: jnp.swapaxes(a.reshape(a.shape[0], dp, -1), 0, 1)
    grad_kernels = jnp.concatenate(
        [roll(grad_taps[:, :keys]), roll(grad_taps[:, keys : 2 * keys]), roll(grad_taps[:, 2 * keys :])], 2
    )
    pad3 = lambda a: jnp.pad(a, ((0, 0), (0, 0), (0, wide - a.shape[2])))
    few_grads = lax.psum_scatter(
        jnp.concatenate([pad3(roll(grad_narrow)), pad3(grad_kernels)], 1), "dp", scatter_dimension=0, tiled=False
    )
    grad_narrow = few_grads[: 2 * heads, : narrow.shape[1]].T
    grad_kernels = few_grads[2 * heads :, : kernels.shape[1]]

    place = lambda a: lax.dynamic_update_slice_in_dim(jnp.zeros_like(log_rate), a, first_head, 0)
    sums = lax.psum(
        jnp.concatenate(
            [
                mix_gain_part,
                ffn_gain_part,
                grad_gain[0],
                place(grad_small[0, :heads]),
                place(grad_small[0, heads:]),
            ]
        ),
        ("dp", "tensor"),
    )
    ends = [model, 2 * model, 2 * model + head_gain.shape[0], 2 * model + head_gain.shape[0] + log_rate.shape[0]]
    grad_mix_gain, grad_ffn_gain, grad_head_gain, grad_log_rate, grad_decay_bias = jnp.split(sums, ends)
    return (
        hidden_out,
        grad_in,
        grad_mix_gain,
        grad_qkv[:, :keys],
        grad_qkv[:, keys : 2 * keys],
        grad_qkv[:, 2 * keys :],
        grad_kernels[:, : cut[0]],
        grad_kernels[:, cut[0] : cut[1]],
        grad_kernels[:, cut[1] :],
        grad_narrow[:, :heads],
        grad_narrow[:, heads:],
        grad_log_rate,
        grad_decay_bias,
        grad_w_outgate,
        grad_head_gain,
        grad_w_output,
        grad_ffn_gain,
        grad_pair[:, :hidden],
        grad_pair[:, hidden:],
        grad_w_down,
    )


def solution(mesh):
    rows, both, flat = P(("dp", "tensor"), None), P("dp", "tensor"), P(None, ("tensor", "dp"))
    turned = P("tensor", "dp")
    return jax.shard_map(
        local,
        mesh=mesh,
        in_specs=(
            *(rows, rows, P()),
            *(both, both, both, flat, flat, flat, both, both),
            *(P(), P(), both, P(), turned, P(), both, both, turned),
        ),
        out_specs=(
            *(rows, rows, P()),
            *(both, both, both, flat, flat, flat, both, both),
            *(P(), P(), both, P(), turned, P(), both, both, turned),
        ),
        check_vma=False,
    )
```

```python
import jax
import jax.numpy as jnp
from jax import lax
from jax.experimental import pallas as pl
from jax.experimental.pallas import tpu as pltpu
from jax.sharding import PartitionSpec as P

GROUP = 64
TAIL = 8
F32 = jnp.float32
BF16 = jnp.bfloat16
HIGHEST = lax.Precision.HIGHEST


def mm(a, b, dims=((1,), (0,))):
    return lax.dot_general(a.astype(BF16), b.astype(BF16), (dims, ((), ())), preferred_element_type=F32)


NN = ((1,), (0,))
NT = ((1,), (1,))
TN = ((0,), (0,))


def mm_exact(a, b, dims=NN):
    return lax.dot_general(a, b, (dims, ((), ())), precision=HIGHEST, preferred_element_type=F32)


def halves(a):
    high = a.astype(BF16)
    return high, (a - high.astype(F32)).astype(BF16)


def mm_split(a, b):
    a_high, a_low = halves(a)
    b_high, b_low = halves(b)
    return mm(a_high, b_high) + (mm(a_high, b_low) + mm(a_low, b_high))


def sigmoid(x):
    return 1.0 / (1.0 + jnp.exp(-x))


def softplus(x):
    return jnp.maximum(x, 0.0) + jnp.log1p(jnp.exp(-jnp.abs(x)))


def grid_iota(size):
    return (
        lax.broadcasted_iota(jnp.int32, (size, size), 0),
        lax.broadcasted_iota(jnp.int32, (size, size), 1),
    )


def unit_lower_inverses(lowers, row, col):
    size = lowers[0].shape[0]
    base = 16
    eye = jnp.where(row == col, 1.0, 0.0)
    powers = [jnp.where(row // base == col // base, -lower, 0.0) for lower in lowers]
    inverses = [eye + power for power in powers]
    reach = 2
    while reach < base:
        powers = [mm_split(power, power) for power in powers]
        inverses = [inverse + mm_split(inverse, power) for inverse, power in zip(inverses, powers)]
        reach *= 2
    while base < size:
        wide = 2 * base
        off = (row // wide == col // wide) & (row // base > col // base)
        right = [mm_split(jnp.where(off, lower, 0.0), inverse) for lower, inverse in zip(lowers, inverses)]
        inverses = [inverse - mm_split(inverse, r) for inverse, r in zip(inverses, right)]
        base = wide
    return inverses


def gates(p_ab, rate, bias, heads):
    pre = p_ab[:, :heads] + bias
    return sigmoid(p_ab[:, heads:]), -jnp.exp(rate) * softplus(pre), pre


def forward_kernel(
    pqkv, pab, taps, rate, bias,
    n_out, norm_out, conved, u_out, s_out, t_out,
    ext, state,
):
    heads = rate.shape[1]
    vals = n_out.shape[1]
    keys = (pqkv.shape[1] - vals) // 2
    dk, dv = keys // heads, vals // heads

    @pl.when(pl.program_id(0) == 0)
    def _():
        ext[...] = jnp.zeros_like(ext)
        state[...] = jnp.zeros_like(state)

    ext[TAIL:, :] = pqkv[...]
    n_taps = taps.shape[0]
    total = None
    for i in range(n_taps):
        start = TAIL - (n_taps - 1) + i
        term = ext[start : start + GROUP, :] * taps[i : i + 1, :]
        total = term if total is None else total + term
    conved[...] = total
    ext[:TAIL, :] = ext[GROUP:, :]

    row, col = grid_iota(GROUP)
    tri = jnp.where(row >= col, 1.0, 0.0)
    beta, log_decay, _ = gates(pab[...], rate[...], bias[...], heads)
    c_col = mm_exact(tri, log_decay)
    c_row = mm_exact(log_decay, jnp.where(row <= col, 1.0, 0.0), TN)
    start_decay = jnp.exp(c_col)
    end_decay = jnp.exp(c_col[GROUP - 1 :, :] - c_col)
    last_decay = jnp.exp(c_col[GROUP - 1 :, :])

    qs, ks, vs, bs, prods, relatives, lowers = [], [], [], [], [], [], []
    for h in range(heads):
        uq = conved[:, h * dk : (h + 1) * dk]
        uk = conved[:, keys + h * dk : keys + (h + 1) * dk]
        uv = conved[:, 2 * keys + h * dv : 2 * keys + (h + 1) * dv]
        q = uq * sigmoid(uq)
        qs.append(q * (lax.rsqrt(jnp.sum(q * q, -1, keepdims=True) + 1e-6) * dk**-0.5))
        k = uk * sigmoid(uk)
        ks.append(k * lax.rsqrt(jnp.sum(k * k, -1, keepdims=True) + 1e-6))
        vs.append(uv * sigmoid(uv))
        bs.append(beta[:, h : h + 1])
    for h in range(heads):
        prods.append(mm(jnp.concatenate([ks[h], qs[h]], 0), ks[h], NT))
    for h in range(heads):
        differ = jnp.minimum(c_col[:, h : h + 1] - c_row[h : h + 1, :], 0.0)
        relatives.append(jnp.where(row >= col, jnp.exp(differ), 0.0))
        lowers.append(jnp.where(row > col, bs[h] * relatives[h] * prods[h][:GROUP], 0.0))
    invs = [inverse.astype(BF16) for inverse in unit_lower_inverses(lowers, row, col)]
    states = [state[h] for h in range(heads)]
    lows = [s.astype(BF16) for s in states]
    reads = []
    for h in range(heads):
        e = start_decay[:, h : h + 1]
        reads.append(mm(jnp.concatenate([ks[h] * e, qs[h] * e], 0), lows[h]))
    us = [mm(invs[h], bs[h] * (vs[h] - reads[h][:GROUP])).astype(BF16) for h in range(heads)]
    outs = [reads[h][GROUP:] + mm(relatives[h] * prods[h][GROUP:], us[h]) for h in range(heads)]
    nexts = [
        last_decay[:, h : h + 1] * states[h] + mm(ks[h] * end_decay[:, h : h + 1], us[h], TN) for h in range(heads)
    ]
    for h in range(heads):
        cols = slice(h * dv, (h + 1) * dv)
        state[h] = nexts[h]
        t_out[0, h] = invs[h]
        s_out[0, h] = lows[h]
        u_out[:, cols] = us[h]
        o = outs[h]
        norm = lax.rsqrt(jnp.mean(o * o, -1, keepdims=True) + 1e-5)
        n_out[:, cols] = (o * norm).astype(n_out.dtype)
        norm_out[:, h : h + 1] = norm


def core_forward(pqkv, pab, taps, rate, bias, keys):
    rows, width = pqkv.shape
    vals = width - 2 * keys
    heads = rate.shape[1]
    dk, dv = keys // heads, vals // heads
    blocks = rows // GROUP
    tokens = lambda width: pl.BlockSpec((GROUP, width), lambda n: (n, 0))
    fixed = lambda a: pl.BlockSpec(a.shape, lambda n: (0, 0))
    return pl.pallas_call(
        forward_kernel,
        grid=(blocks,),
        in_specs=[tokens(a.shape[1]) for a in (pqkv, pab)] + [fixed(a) for a in (taps, rate, bias)],
        out_specs=[
            tokens(vals),
            tokens(heads),
            tokens(width),
            tokens(vals),
            pl.BlockSpec((1, heads, dk, dv), lambda n: (n, 0, 0, 0)),
            pl.BlockSpec((1, heads, GROUP, GROUP), lambda n: (n, 0, 0, 0)),
        ],
        out_shape=[
            jax.ShapeDtypeStruct((rows, vals), BF16),
            jax.ShapeDtypeStruct((rows, heads), F32),
            jax.ShapeDtypeStruct((rows, width), F32),
            jax.ShapeDtypeStruct((rows, vals), BF16),
            jax.ShapeDtypeStruct((blocks, heads, dk, dv), BF16),
            jax.ShapeDtypeStruct((blocks, heads, GROUP, GROUP), BF16),
        ],
        scratch_shapes=[
            pltpu.VMEM((GROUP + TAIL, 2 * keys + vals), F32),
            pltpu.VMEM((heads, dk, dv), F32),
        ],
        compiler_params=pltpu.CompilerParams(dimension_semantics=("arbitrary",), vmem_limit_bytes=40 * 2**20),
        cost_estimate=pl.CostEstimate(flops=8 * 10**9, bytes_accessed=32 * 2**20, transcendentals=10**7),
        name="core_forward",
    )(pqkv, pab, taps, rate, bias)


def backward_kernel(
    dn_in, pqkv, pab, n_in, norm_in, conved, u_in, s_in, t_in, taps, rate, bias,
    dpqkv, dpab, dtaps, dsmall, dgain,
    ext, dstate,
):
    heads = rate.shape[1]
    vals = dn_in.shape[1]
    keys = (pqkv.shape[1] - vals) // 2
    dk, dv = keys // heads, vals // heads

    @pl.when(pl.program_id(0) == 0)
    def _():
        ext[...] = jnp.zeros_like(ext)
        dstate[...] = jnp.zeros_like(dstate)
        for ref in (dtaps, dsmall, dgain):
            ref[...] = jnp.zeros_like(ref)

    row, col = grid_iota(GROUP)
    tri = jnp.where(row >= col, 1.0, 0.0)
    upper = jnp.where(row <= col, 1.0, 0.0)
    beta, log_decay, pre = gates(pab[...], rate[...], bias[...], heads)
    c_col = mm_exact(tri, log_decay)
    c_row = mm_exact(log_decay, upper, TN)
    start_decay = jnp.exp(c_col)
    end_decay = jnp.exp(c_col[GROUP - 1 :, :] - c_col)
    last_decay = jnp.exp(c_col[GROUP - 1 :, :])
    lane = lax.broadcasted_iota(jnp.int32, (1, heads), 1)
    d_beta = jnp.zeros((GROUP, heads), F32)
    after = jnp.zeros((GROUP, heads), F32)
    before = jnp.zeros((GROUP, heads), F32)
    d_log = jnp.zeros((GROUP, heads), F32)
    gain_sum = jnp.zeros((1, dv), F32)

    for h in range(heads):
        ks, vs = slice(h * dk, (h + 1) * dk), slice(h * dv, (h + 1) * dv)
        kx, vx = slice(keys + h * dk, keys + (h + 1) * dk), slice(2 * keys + h * dv, 2 * keys + (h + 1) * dv)
        here = lane == h
        uq, uk, uv = conved[:, ks], conved[:, kx], conved[:, vx]
        sq, sk, sv = sigmoid(uq), sigmoid(uk), sigmoid(uv)
        q = uq * sq
        q_norm = lax.rsqrt(jnp.sum(q * q, -1, keepdims=True) + 1e-6)
        q = q * q_norm
        k = uk * sk
        k_norm = lax.rsqrt(jnp.sum(k * k, -1, keepdims=True) + 1e-6)
        k = k * k_norm
        v = uv * sv
        qs = q * dk**-0.5
        b = beta[:, h : h + 1]
        e = start_decay[:, h : h + 1]
        f = end_decay[:, h : h + 1]
        kb = k.astype(BF16)
        qb = qs.astype(BF16)

        n = n_in[:, vs].astype(F32)
        dn = dn_in[:, vs]
        dnn = dn * n
        gain_sum = gain_sum + jnp.sum(dnn, 0, keepdims=True)
        do = norm_in[:, h : h + 1] * (dn - n * jnp.mean(dnn, -1, keepdims=True))

        prod = mm(jnp.concatenate([kb, qb], 0), kb, NT)
        relative = jnp.where(row >= col, jnp.exp(jnp.minimum(c_col[:, h : h + 1] - c_row[h : h + 1, :], 0.0)), 0.0)
        kk, qk = prod[:GROUP], prod[GROUP:]
        strict = jnp.where(row > col, relative, 0.0)
        mix = relative * qk
        s_prev = s_in[0, h]
        u = u_in[:, vs]
        inv = t_in[0, h]
        ds = dstate[h]
        ds_low = ds.astype(BF16)
        dob = do.astype(BF16)
        ke, qe, kd = k * e, qs * e, k * f
        du = mm(mix, dob, TN) + mm(kd, ds_low)
        dr = mm(inv, du, TN)
        pair = jnp.concatenate([dob, dr.astype(BF16)], 0)
        dstate[h] = last_decay[:, h : h + 1] * ds + mm(jnp.concatenate([qe, -(b * ke)], 0), pair, TN)
        cross = mm(pair, u, NT)
        dmix = jnp.where(row >= col, cross[:GROUP], 0.0)
        dlow = jnp.where(row > col, -cross[GROUP:], 0.0)
        back = mm(pair, s_prev, NT)
        dqe, x = back[:GROUP], back[GROUP:]
        dkd = mm(u, ds_low, NT)
        dke = -(b * x)
        rk = strict * kk
        d_beta = d_beta + jnp.where(
            here,
            jnp.sum(dr * v, -1, keepdims=True) - jnp.sum(x * ke, -1, keepdims=True) + jnp.sum(dlow * rk, -1, keepdims=True),
            0.0,
        )
        dpair = dlow * (b * rk) + dmix * mix
        spread = mm(upper, dpair)
        last_part = last_decay[:, h : h + 1] * jnp.sum(ds * s_prev.astype(F32), keepdims=True)
        d_log = d_log + jnp.where(here, jnp.sum(jnp.where(row > col, spread, 0.0), -1, keepdims=True) + last_part, 0.0)
        after = after + jnp.where(here, jnp.sum(dqe * qe + dke * ke, -1, keepdims=True), 0.0)
        before = before + jnp.where(here, jnp.sum(dkd * kd, -1, keepdims=True), 0.0)
        dqk = dmix * relative
        dkk = dlow * (b * strict)
        first = mm(jnp.concatenate([dqk, dkk], 0), kb)
        dq = e * dqe + first[:GROUP]
        dk_ = e * dke + f * dkd + first[GROUP:] + mm(jnp.concatenate([dkk, dqk], 0), jnp.concatenate([kb, qb], 0), TN)
        dq = dq * dk**-0.5
        dq = q_norm * (dq - q * jnp.sum(dq * q, -1, keepdims=True))
        dk_ = k_norm * (dk_ - k * jnp.sum(dk_ * k, -1, keepdims=True))
        ext[:GROUP, ks] = dq * (sq * (1.0 + uq * (1.0 - sq)))
        ext[:GROUP, kx] = dk_ * (sk * (1.0 + uk * (1.0 - sk)))
        ext[:GROUP, vx] = (b * dr) * (sv * (1.0 + uv * (1.0 - sv)))

    d_log = d_log + mm_exact(upper, after) + mm_exact(jnp.where(row > col, 1.0, 0.0), before)
    d_pre = d_log * (-jnp.exp(rate[...])) * sigmoid(pre)
    dpab[:, :heads] = d_pre
    dpab[:, heads:] = d_beta * beta * (1.0 - beta)
    dsmall[0:1, :heads] += jnp.sum(d_log * log_decay, 0, keepdims=True)
    dsmall[0:1, heads:] += jnp.sum(d_pre, 0, keepdims=True)
    dgain[...] += gain_sum

    n_taps = taps.shape[0]
    rows_in = pqkv[...]
    total = None
    for i in range(n_taps):
        start = n_taps - 1 - i
        piece = ext[start : start + GROUP, :]
        term = piece * taps[i : i + 1, :]
        total = term if total is None else total + term
        dtaps[i : i + 1, :] += jnp.sum(piece * rows_in, 0, keepdims=True)
    dpqkv[...] = total.astype(dpqkv.dtype)
    ext[GROUP:, :] = ext[:TAIL, :]


def core_backward(dn, pqkv, pab, kept, taps, rate, bias):
    n_in, norm_in, conved, u_in, s_in, t_in = kept
    rows, width = pqkv.shape
    vals = dn.shape[1]
    keys = (width - vals) // 2
    heads = rate.shape[1]
    dk, dv = keys // heads, vals // heads
    blocks = rows // GROUP
    tokens = lambda width: pl.BlockSpec((GROUP, width), lambda n: (blocks - 1 - n, 0))
    stacked = lambda a: pl.BlockSpec((1,) + a.shape[1:], lambda n: (blocks - 1 - n, 0, 0, 0))
    fixed = lambda shape: pl.BlockSpec(shape, lambda n: (0, 0))
    small = (1, 2 * heads)
    return pl.pallas_call(
        backward_kernel,
        grid=(blocks,),
        in_specs=[tokens(a.shape[1]) for a in (dn, pqkv, pab, n_in, norm_in, conved, u_in)]
        + [stacked(s_in), stacked(t_in)]
        + [fixed(a.shape) for a in (taps, rate, bias)],
        out_specs=[tokens(a.shape[1]) for a in (pqkv, pab)]
        + [fixed(taps.shape), fixed(small), fixed((1, dv))],
        out_shape=[jax.ShapeDtypeStruct(pqkv.shape, BF16), jax.ShapeDtypeStruct(pab.shape, F32)]
        + [jax.ShapeDtypeStruct(s, F32) for s in (taps.shape, small, (1, dv))],
        scratch_shapes=[
            pltpu.VMEM((GROUP + TAIL, 2 * keys + vals), F32),
            pltpu.VMEM((heads, dk, dv), F32),
        ],
        compiler_params=pltpu.CompilerParams(dimension_semantics=("arbitrary",), vmem_limit_bytes=40 * 2**20),
        cost_estimate=pl.CostEstimate(flops=20 * 10**9, bytes_accessed=48 * 2**20, transcendentals=10**7),
        name="core_backward",
    )(dn, pqkv, pab, n_in, norm_in, conved, u_in, s_in, t_in, taps, rate, bias)


def rms_norm(values, gain_vec):
    return values * lax.rsqrt(jnp.mean(values * values, -1, keepdims=True) + 1e-05) * gain_vec


def dot(a, b, dims=NN):
    return lax.dot_general(a, b, (dims, ((), ())), preferred_element_type=F32)


def swap(piece, mask):
    return lax.ppermute(piece, "tensor", [(i, i ^ mask) for i in range(4)])


def gather_rows(own):
    if lax.axis_size("tensor") != 4:
        return lax.all_gather(own, "tensor", axis=0, tiled=True)
    half = own.shape[0] // 2
    first, second = swap(own, 1), swap(own, 2)
    return jnp.concatenate([own, first, second, swap(second[:half], 1), swap(first[half:], 2)], 0)


def scatter_rows(part, beside=None):
    if lax.axis_size("tensor") != 4:
        total = lax.psum_scatter(part, "tensor", scatter_dimension=0, tiled=True).astype(F32)
        return total if beside is None else (total, beside)
    rows, half = part.shape[0] // 4, part.shape[1] // 2

    def chunk(k, columns):
        return part[k * rows : (k + 1) * rows, columns]

    plans = ((slice(0, half), 1, 2), (slice(half, 2 * half), 2, 1))
    arrived = [swap(jnp.concatenate([chunk(one, columns), chunk(3, columns)], 0), one) for columns, one, _ in plans]
    if beside is not None:
        arrived, beside = lax.optimization_barrier((arrived, beside))
    owns, passed = [], []
    for (columns, _, two), got in zip(plans, arrived):
        got = got.astype(F32)
        owns.append(chunk(0, columns).astype(F32) + got[:rows])
        passed.append((chunk(two, columns).astype(F32) + got[rows:]).astype(BF16))
    passed = lax.optimization_barrier(passed)
    sums = [own + swap(piece, two).astype(F32) for own, piece, (_, _, two) in zip(owns, passed, plans)]
    total = jnp.concatenate(sums, 1)
    return total if beside is None else (total, beside)


def sum_everywhere(values):
    for axis in ("dp", "tensor"):
        size = lax.axis_size(axis)
        if size & (size - 1):
            values = lax.psum(values, axis)
            continue
        mask = 1
        while mask < size:
            values = values + lax.ppermute(values, axis, [(i, i ^ mask) for i in range(size)])
            mask *= 2
    return values


def reorder(rows_in):
    if lax.axis_size("tensor") != 4:
        return rows_in
    rows = rows_in.shape[0] // 4
    me = lax.axis_index("tensor")
    return jnp.concatenate([lax.dynamic_slice_in_dim(rows_in, (me ^ k) * rows, rows, 0) for k in range(4)], 0)


def norm_back(values, gain_vec, grad):
    factor = lax.rsqrt(jnp.mean(values * values, -1, keepdims=True) + 1e-05)
    normal = values * factor
    scaled = grad * gain_vec
    return (
        factor * (scaled - normal * jnp.mean(scaled * normal, -1, keepdims=True)),
        jnp.sum(grad * normal, 0),
    )


def gather_dp(shard, axis):
    return lax.all_gather(shard.astype(BF16), "dp", axis=axis, tiled=True)


def scatter_dp(part, axis):
    return lax.psum_scatter(part, "dp", scatter_dimension=axis, tiled=True)


def local(
    hidden_in,
    grad_out,
    mix_gain,
    w_query,
    w_key,
    w_value,
    conv_query,
    conv_key,
    conv_value,
    w_decay,
    w_beta,
    log_rate,
    decay_bias,
    w_outgate,
    head_gain,
    w_output,
    ffn_gain,
    w_gate,
    w_up,
    w_down,
):
    dp = lax.axis_size("dp")
    model = hidden_in.shape[1]
    keys, vals, hidden = w_query.shape[1], w_value.shape[1], w_gate.shape[1]
    heads = w_decay.shape[1]
    first_head = lax.axis_index("tensor") * heads
    rate = lax.dynamic_slice_in_dim(log_rate, first_head, heads)[None]
    bias = lax.dynamic_slice_in_dim(decay_bias, first_head, heads)[None]
    gain = jnp.tile(head_gain, heads)

    narrow = jnp.concatenate([w_decay, w_beta], 1).T
    kernels = jnp.concatenate([conv_query, conv_key, conv_value], 1)
    wide = max(narrow.shape[1], kernels.shape[1])
    pad = lambda a: jnp.pad(a, ((0, 0), (0, wide - a.shape[1])))
    few = lax.all_gather(jnp.concatenate([pad(narrow), pad(kernels)], 0).astype(BF16), "dp")
    unroll = lambda a: jnp.swapaxes(a, 0, 1).reshape(a.shape[1], -1)
    full_narrow = unroll(few[:, : 2 * heads, : narrow.shape[1]])
    pieces = few[:, 2 * heads :, : kernels.shape[1]]
    cut = (conv_query.shape[1], conv_query.shape[1] + conv_key.shape[1])
    taps = jnp.concatenate(
        [unroll(pieces[:, :, : cut[0]]), unroll(pieces[:, :, cut[0] : cut[1]]), unroll(pieces[:, :, cut[1] :])], 1
    ).astype(F32)

    full_qkv = gather_dp(jnp.concatenate([w_query, w_key, w_value], 1), 0)
    full_gate_out = gather_dp(jnp.concatenate([w_outgate, w_output.T], 1), 0)
    full_outgate, full_output = full_gate_out[:, :vals], full_gate_out[:, vals:]
    full_pair = gather_dp(jnp.concatenate([w_gate, w_up], 1), 0)
    full_down = gather_dp(w_down, 1)

    hold = lax.optimization_barrier
    rows_in = hidden_in.astype(F32)
    normed = reorder(gather_rows(rms_norm(rows_in, mix_gain).astype(BF16)))
    cot_own, _ = hold((grad_out, normed))
    cot = gather_rows(cot_own)
    pqkv = dot(normed, full_qkv)
    pab = dot(normed, full_narrow, NT)
    pqkv, cot = hold((pqkv, cot))
    kept = core_forward(pqkv, pab, taps, rate, bias, keys)
    po = dot(normed, full_outgate)
    po_sig = jax.nn.sigmoid(po)
    mixed = (kept[0].astype(F32) * gain * (po * po_sig)).astype(BF16)
    middle = rows_in + scatter_rows(reorder(dot(mixed, full_output, NT).astype(BF16)))

    ffn_rows = gather_rows(rms_norm(middle, ffn_gain).astype(BF16))
    pre = dot(ffn_rows, full_pair)
    gate_pre, up_pre = pre[:, :hidden], pre[:, hidden:]
    gate_sig = jax.nn.sigmoid(gate_pre)
    activ = (gate_pre * gate_sig * up_pre).astype(BF16)
    cot, part_down = hold((cot, dot(activ, cot, TN).astype(BF16)))
    grad_w_down = scatter_dp(part_down, 1)
    grad_activ = dot(cot, full_down, NT)
    grad_gate_pre = (grad_activ * up_pre * gate_sig * (1.0 + gate_pre * (1.0 - gate_sig))).astype(BF16)
    grad_up_pre = (grad_activ * (gate_pre * gate_sig)).astype(BF16)
    grad_pre = jnp.concatenate([grad_gate_pre, grad_up_pre], 1)
    grad_ffn_norm, part_pair = scatter_rows(
        dot(grad_pre, full_pair, NT).astype(BF16), dot(ffn_rows, grad_pre, TN).astype(BF16)
    )
    grad_pair = scatter_dp(part_pair, 0)
    grad_middle_norm, ffn_gain_part = norm_back(middle, ffn_gain, grad_ffn_norm)
    grad_middle = grad_out.astype(F32) + grad_middle_norm

    mix_cot = reorder(gather_rows(grad_middle.astype(BF16)))
    grad_mixed = dot(mix_cot, full_output)
    grad_po = grad_mixed * kept[0].astype(F32) * gain * (po_sig * (1.0 + po * (1.0 - po_sig)))
    grad_po = grad_po.astype(BF16)
    grad_n = grad_mixed * gain * (po * po_sig)
    part_gate_out = jnp.concatenate([dot(normed, grad_po, TN), dot(mix_cot, mixed, TN)], 1).astype(BF16)
    grad_n, activ_late, grad_w_down, part_gate_out = hold((grad_n, activ, grad_w_down, part_gate_out))
    grad_gate_out = scatter_dp(part_gate_out, 0)
    out_part = dot(activ_late, full_down).astype(BF16)
    grad_n, out_part = hold((grad_n, out_part))
    hidden_out = (middle + scatter_rows(out_part)).astype(BF16)
    grad_pqkv, grad_pab, grad_taps, grad_small, grad_gain = core_backward(grad_n, pqkv, pab, kept, taps, rate, bias)
    grad_pqkv, grad_pair = hold((grad_pqkv, grad_pair))
    grad_pqkv, part_qkv = hold((grad_pqkv, dot(normed, grad_pqkv, TN).astype(BF16)))
    grad_qkv = scatter_dp(part_qkv, 0)
    low_pab = grad_pab.astype(BF16)
    grad_normed = dot(grad_pqkv, full_qkv, NT) + dot(grad_po, full_outgate, NT) + dot(low_pab, full_narrow)
    grad_mix_norm = scatter_rows(reorder(grad_normed.astype(BF16)))
    grad_rows, mix_gain_part = norm_back(rows_in, mix_gain, grad_mix_norm)
    grad_in = (grad_middle + grad_rows).astype(BF16)

    grad_narrow = dot(low_pab, normed, TN)
    roll = lambda a: jnp.swapaxes(a.reshape(a.shape[0], dp, -1), 0, 1)
    grad_kernels = jnp.concatenate(
        [roll(grad_taps[:, :keys]), roll(grad_taps[:, keys : 2 * keys]), roll(grad_taps[:, 2 * keys :])], 2
    )
    pad3 = lambda a: jnp.pad(a, ((0, 0), (0, 0), (0, wide - a.shape[2])))
    few_parts = jnp.concatenate([pad3(roll(grad_narrow)), pad3(grad_kernels)], 1)
    few_grads = jnp.sum(lax.all_to_all(few_parts, "dp", 0, 0, tiled=True), 0)
    grad_narrow = few_grads[: 2 * heads, : narrow.shape[1]].T
    grad_kernels = few_grads[2 * heads :, : kernels.shape[1]]

    place = lambda a: lax.dynamic_update_slice_in_dim(jnp.zeros_like(log_rate), a, first_head, 0)
    sums = sum_everywhere(
        jnp.concatenate(
            [
                mix_gain_part,
                ffn_gain_part,
                grad_gain[0] / head_gain,
                place(grad_small[0, :heads]),
                place(grad_small[0, heads:]),
            ]
        )
    )
    ends = [model, 2 * model, 2 * model + head_gain.shape[0], 2 * model + head_gain.shape[0] + log_rate.shape[0]]
    grad_mix_gain, grad_ffn_gain, grad_head_gain, grad_log_rate, grad_decay_bias = jnp.split(sums, ends)
    grad_qkv, grad_gate_out, grad_pair = grad_qkv.astype(F32), grad_gate_out.astype(F32), grad_pair.astype(F32)
    return (
        hidden_out,
        grad_in,
        grad_mix_gain,
        grad_qkv[:, :keys],
        grad_qkv[:, keys : 2 * keys],
        grad_qkv[:, 2 * keys :],
        grad_kernels[:, : cut[0]],
        grad_kernels[:, cut[0] : cut[1]],
        grad_kernels[:, cut[1] :],
        grad_narrow[:, :heads],
        grad_narrow[:, heads:],
        grad_log_rate,
        grad_decay_bias,
        grad_gate_out[:, :vals],
        grad_head_gain,
        grad_gate_out[:, vals:].T,
        grad_ffn_gain,
        grad_pair[:, :hidden],
        grad_pair[:, hidden:],
        grad_w_down.astype(F32),
    )


def solution(mesh):
    rows, both, flat = P(("dp", "tensor"), None), P("dp", "tensor"), P(None, ("tensor", "dp"))
    turned = P("tensor", "dp")
    return jax.shard_map(
        local,
        mesh=mesh,
        in_specs=(
            *(rows, rows, P()),
            *(both, both, both, flat, flat, flat, both, both),
            *(P(), P(), both, P(), turned, P(), both, both, turned),
        ),
        out_specs=(
            *(rows, rows, P()),
            *(both, both, both, flat, flat, flat, both, both),
            *(P(), P(), both, P(), turned, P(), both, both, turned),
        ),
        check_vma=False,
    )
```

```python
import jax
import jax.numpy as jnp
from jax import lax
from jax.experimental import pallas as pl
from jax.experimental.pallas import tpu as pltpu
from jax.sharding import PartitionSpec as P

GROUP = 64
TAIL = 8
F32 = jnp.float32
BF16 = jnp.bfloat16
HIGHEST = lax.Precision.HIGHEST


def mm(a, b, dims=((1,), (0,))):
    return lax.dot_general(a.astype(BF16), b.astype(BF16), (dims, ((), ())), preferred_element_type=F32)


NN = ((1,), (0,))
NT = ((1,), (1,))
TN = ((0,), (0,))


def mm_exact(a, b, dims=NN):
    return lax.dot_general(a, b, (dims, ((), ())), precision=HIGHEST, preferred_element_type=F32)


def halves(a):
    high = a.astype(BF16)
    return high, (a - high.astype(F32)).astype(BF16)


def mm_split(a, b):
    a_high, a_low = halves(a)
    b_high, b_low = halves(b)
    return mm(a_high, b_high) + (mm(a_high, b_low) + mm(a_low, b_high))


def sigmoid(x):
    return 1.0 / (1.0 + jnp.exp(-x))


def softplus(x):
    return jnp.maximum(x, 0.0) + jnp.log1p(jnp.exp(-jnp.abs(x)))


def grid_iota(size):
    return (
        lax.broadcasted_iota(jnp.int32, (size, size), 0),
        lax.broadcasted_iota(jnp.int32, (size, size), 1),
    )


def unit_lower_inverses(lowers, row, col):
    size = lowers[0].shape[0]
    base = 16
    eye = jnp.where(row == col, 1.0, 0.0)
    powers = [jnp.where(row // base == col // base, -lower, 0.0) for lower in lowers]
    inverses = [eye + power for power in powers]
    reach = 2
    while reach < base:
        powers = [mm_split(power, power) for power in powers]
        inverses = [inverse + mm_split(inverse, power) for inverse, power in zip(inverses, powers)]
        reach *= 2
    while base < size:
        wide = 2 * base
        off = (row // wide == col // wide) & (row // base > col // base)
        right = [mm_split(jnp.where(off, lower, 0.0), inverse) for lower, inverse in zip(lowers, inverses)]
        inverses = [inverse - mm_split(inverse, r) for inverse, r in zip(inverses, right)]
        base = wide
    return inverses


def gates(p_ab, rate, bias, heads):
    pre = p_ab[:, :heads] + bias
    return sigmoid(p_ab[:, heads:]), -jnp.exp(rate) * softplus(pre), pre


def forward_kernel(
    pqkv, pab, taps, rate, bias,
    n_out, norm_out, conved, u_out, s_out, t_out,
    ext, state,
):
    heads = rate.shape[1]
    vals = n_out.shape[1]
    keys = (pqkv.shape[1] - vals) // 2
    dk, dv = keys // heads, vals // heads

    @pl.when(pl.program_id(0) == 0)
    def _():
        ext[...] = jnp.zeros_like(ext)
        state[...] = jnp.zeros_like(state)

    ext[TAIL:, :] = pqkv[...]
    n_taps = taps.shape[0]
    total = None
    for i in range(n_taps):
        start = TAIL - (n_taps - 1) + i
        term = ext[start : start + GROUP, :] * taps[i : i + 1, :]
        total = term if total is None else total + term
    conved[...] = total
    ext[:TAIL, :] = ext[GROUP:, :]

    row, col = grid_iota(GROUP)
    tri = jnp.where(row >= col, 1.0, 0.0)
    beta, log_decay, _ = gates(pab[...], rate[...], bias[...], heads)
    c_col = mm_exact(tri, log_decay)
    c_row = mm_exact(log_decay, jnp.where(row <= col, 1.0, 0.0), TN)
    start_decay = jnp.exp(c_col)
    end_decay = jnp.exp(c_col[GROUP - 1 :, :] - c_col)
    last_decay = jnp.exp(c_col[GROUP - 1 :, :])

    qs, ks, vs, bs, prods, relatives, lowers = [], [], [], [], [], [], []
    for h in range(heads):
        uq = conved[:, h * dk : (h + 1) * dk]
        uk = conved[:, keys + h * dk : keys + (h + 1) * dk]
        uv = conved[:, 2 * keys + h * dv : 2 * keys + (h + 1) * dv]
        q = uq * sigmoid(uq)
        qs.append(q * (lax.rsqrt(jnp.sum(q * q, -1, keepdims=True) + 1e-6) * dk**-0.5))
        k = uk * sigmoid(uk)
        ks.append(k * lax.rsqrt(jnp.sum(k * k, -1, keepdims=True) + 1e-6))
        vs.append(uv * sigmoid(uv))
        bs.append(beta[:, h : h + 1])
    for h in range(heads):
        prods.append(mm(jnp.concatenate([ks[h], qs[h]], 0), ks[h], NT))
    for h in range(heads):
        differ = jnp.minimum(c_col[:, h : h + 1] - c_row[h : h + 1, :], 0.0)
        relatives.append(jnp.where(row >= col, jnp.exp(differ), 0.0))
        lowers.append(jnp.where(row > col, bs[h] * relatives[h] * prods[h][:GROUP], 0.0))
    invs = [inverse.astype(BF16) for inverse in unit_lower_inverses(lowers, row, col)]
    states = [state[h] for h in range(heads)]
    lows = [s.astype(BF16) for s in states]
    reads = []
    for h in range(heads):
        e = start_decay[:, h : h + 1]
        reads.append(mm(jnp.concatenate([ks[h] * e, qs[h] * e], 0), lows[h]))
    us = [mm(invs[h], bs[h] * (vs[h] - reads[h][:GROUP])).astype(BF16) for h in range(heads)]
    outs = [reads[h][GROUP:] + mm(relatives[h] * prods[h][GROUP:], us[h]) for h in range(heads)]
    nexts = [
        last_decay[:, h : h + 1] * states[h] + mm(ks[h] * end_decay[:, h : h + 1], us[h], TN) for h in range(heads)
    ]
    for h in range(heads):
        cols = slice(h * dv, (h + 1) * dv)
        state[h] = nexts[h]
        t_out[0, h] = invs[h]
        s_out[0, h] = lows[h]
        u_out[:, cols] = us[h]
        o = outs[h]
        norm = lax.rsqrt(jnp.mean(o * o, -1, keepdims=True) + 1e-5)
        n_out[:, cols] = (o * norm).astype(n_out.dtype)
        norm_out[:, h : h + 1] = norm


def core_forward(pqkv, pab, taps, rate, bias, keys):
    rows, width = pqkv.shape
    vals = width - 2 * keys
    heads = rate.shape[1]
    dk, dv = keys // heads, vals // heads
    blocks = rows // GROUP
    tokens = lambda width: pl.BlockSpec((GROUP, width), lambda n: (n, 0))
    fixed = lambda a: pl.BlockSpec(a.shape, lambda n: (0, 0))
    return pl.pallas_call(
        forward_kernel,
        grid=(blocks,),
        in_specs=[tokens(a.shape[1]) for a in (pqkv, pab)] + [fixed(a) for a in (taps, rate, bias)],
        out_specs=[
            tokens(vals),
            tokens(heads),
            tokens(width),
            tokens(vals),
            pl.BlockSpec((1, heads, dk, dv), lambda n: (n, 0, 0, 0)),
            pl.BlockSpec((1, heads, GROUP, GROUP), lambda n: (n, 0, 0, 0)),
        ],
        out_shape=[
            jax.ShapeDtypeStruct((rows, vals), BF16),
            jax.ShapeDtypeStruct((rows, heads), F32),
            jax.ShapeDtypeStruct((rows, width), F32),
            jax.ShapeDtypeStruct((rows, vals), BF16),
            jax.ShapeDtypeStruct((blocks, heads, dk, dv), BF16),
            jax.ShapeDtypeStruct((blocks, heads, GROUP, GROUP), BF16),
        ],
        scratch_shapes=[
            pltpu.VMEM((GROUP + TAIL, 2 * keys + vals), F32),
            pltpu.VMEM((heads, dk, dv), F32),
        ],
        compiler_params=pltpu.CompilerParams(dimension_semantics=("arbitrary",), vmem_limit_bytes=40 * 2**20),
        cost_estimate=pl.CostEstimate(flops=8 * 10**9, bytes_accessed=32 * 2**20, transcendentals=10**7),
        name="core_forward",
    )(pqkv, pab, taps, rate, bias)


def backward_kernel(
    dn_in, pqkv, pab, n_in, norm_in, conved, u_in, s_in, t_in, taps, rate, bias,
    dpqkv, dpab, dtaps, dsmall, dgain,
    ext, dstate,
):
    heads = rate.shape[1]
    vals = dn_in.shape[1]
    keys = (pqkv.shape[1] - vals) // 2
    dk, dv = keys // heads, vals // heads

    @pl.when(pl.program_id(0) == 0)
    def _():
        ext[...] = jnp.zeros_like(ext)
        dstate[...] = jnp.zeros_like(dstate)
        for ref in (dtaps, dsmall, dgain):
            ref[...] = jnp.zeros_like(ref)

    row, col = grid_iota(GROUP)
    tri = jnp.where(row >= col, 1.0, 0.0)
    upper = jnp.where(row <= col, 1.0, 0.0)
    beta, log_decay, pre = gates(pab[...], rate[...], bias[...], heads)
    c_col = mm_exact(tri, log_decay)
    c_row = mm_exact(log_decay, upper, TN)
    start_decay = jnp.exp(c_col)
    end_decay = jnp.exp(c_col[GROUP - 1 :, :] - c_col)
    last_decay = jnp.exp(c_col[GROUP - 1 :, :])
    lane = lax.broadcasted_iota(jnp.int32, (1, heads), 1)
    d_beta = jnp.zeros((GROUP, heads), F32)
    after = jnp.zeros((GROUP, heads), F32)
    before = jnp.zeros((GROUP, heads), F32)
    d_log = jnp.zeros((GROUP, heads), F32)
    gain_sum = jnp.zeros((1, dv), F32)

    for h in range(heads):
        ks, vs = slice(h * dk, (h + 1) * dk), slice(h * dv, (h + 1) * dv)
        kx, vx = slice(keys + h * dk, keys + (h + 1) * dk), slice(2 * keys + h * dv, 2 * keys + (h + 1) * dv)
        here = lane == h
        uq, uk, uv = conved[:, ks], conved[:, kx], conved[:, vx]
        sq, sk, sv = sigmoid(uq), sigmoid(uk), sigmoid(uv)
        q = uq * sq
        q_norm = lax.rsqrt(jnp.sum(q * q, -1, keepdims=True) + 1e-6)
        q = q * q_norm
        k = uk * sk
        k_norm = lax.rsqrt(jnp.sum(k * k, -1, keepdims=True) + 1e-6)
        k = k * k_norm
        v = uv * sv
        qs = q * dk**-0.5
        b = beta[:, h : h + 1]
        e = start_decay[:, h : h + 1]
        f = end_decay[:, h : h + 1]
        kb = k.astype(BF16)
        qb = qs.astype(BF16)

        n = n_in[:, vs].astype(F32)
        dn = dn_in[:, vs]
        dnn = dn * n
        gain_sum = gain_sum + jnp.sum(dnn, 0, keepdims=True)
        do = norm_in[:, h : h + 1] * (dn - n * jnp.mean(dnn, -1, keepdims=True))

        prod = mm(jnp.concatenate([kb, qb], 0), kb, NT)
        relative = jnp.where(row >= col, jnp.exp(jnp.minimum(c_col[:, h : h + 1] - c_row[h : h + 1, :], 0.0)), 0.0)
        kk, qk = prod[:GROUP], prod[GROUP:]
        strict = jnp.where(row > col, relative, 0.0)
        mix = relative * qk
        s_prev = s_in[0, h]
        u = u_in[:, vs]
        inv = t_in[0, h]
        ds = dstate[h]
        ds_low = ds.astype(BF16)
        dob = do.astype(BF16)
        ke, qe, kd = k * e, qs * e, k * f
        du = mm(mix, dob, TN) + mm(kd, ds_low)
        dr = mm(inv, du, TN)
        pair = jnp.concatenate([dob, dr.astype(BF16)], 0)
        dstate[h] = last_decay[:, h : h + 1] * ds + mm(jnp.concatenate([qe, -(b * ke)], 0), pair, TN)
        cross = mm(pair, u, NT)
        dmix = jnp.where(row >= col, cross[:GROUP], 0.0)
        dlow = jnp.where(row > col, -cross[GROUP:], 0.0)
        back = mm(pair, s_prev, NT)
        dqe, x = back[:GROUP], back[GROUP:]
        dkd = mm(u, ds_low, NT)
        dke = -(b * x)
        rk = strict * kk
        d_beta = d_beta + jnp.where(
            here,
            jnp.sum(dr * v, -1, keepdims=True) - jnp.sum(x * ke, -1, keepdims=True) + jnp.sum(dlow * rk, -1, keepdims=True),
            0.0,
        )
        dpair = dlow * (b * rk) + dmix * mix
        spread = mm(upper, dpair)
        last_part = last_decay[:, h : h + 1] * jnp.sum(ds * s_prev.astype(F32), keepdims=True)
        d_log = d_log + jnp.where(here, jnp.sum(jnp.where(row > col, spread, 0.0), -1, keepdims=True) + last_part, 0.0)
        after = after + jnp.where(here, jnp.sum(dqe * qe + dke * ke, -1, keepdims=True), 0.0)
        before = before + jnp.where(here, jnp.sum(dkd * kd, -1, keepdims=True), 0.0)
        dqk = dmix * relative
        dkk = dlow * (b * strict)
        first = mm(jnp.concatenate([dqk, dkk], 0), kb)
        dq = e * dqe + first[:GROUP]
        dk_ = e * dke + f * dkd + first[GROUP:] + mm(jnp.concatenate([dkk, dqk], 0), jnp.concatenate([kb, qb], 0), TN)
        dq = dq * dk**-0.5
        dq = q_norm * (dq - q * jnp.sum(dq * q, -1, keepdims=True))
        dk_ = k_norm * (dk_ - k * jnp.sum(dk_ * k, -1, keepdims=True))
        ext[:GROUP, ks] = dq * (sq * (1.0 + uq * (1.0 - sq)))
        ext[:GROUP, kx] = dk_ * (sk * (1.0 + uk * (1.0 - sk)))
        ext[:GROUP, vx] = (b * dr) * (sv * (1.0 + uv * (1.0 - sv)))

    d_log = d_log + mm_exact(upper, after) + mm_exact(jnp.where(row > col, 1.0, 0.0), before)
    d_pre = d_log * (-jnp.exp(rate[...])) * sigmoid(pre)
    dpab[:, :heads] = d_pre
    dpab[:, heads:] = d_beta * beta * (1.0 - beta)
    dsmall[0:1, :heads] += jnp.sum(d_log * log_decay, 0, keepdims=True)
    dsmall[0:1, heads:] += jnp.sum(d_pre, 0, keepdims=True)
    dgain[...] += gain_sum

    n_taps = taps.shape[0]
    rows_in = pqkv[...]
    total = None
    for i in range(n_taps):
        start = n_taps - 1 - i
        piece = ext[start : start + GROUP, :]
        term = piece * taps[i : i + 1, :]
        total = term if total is None else total + term
        dtaps[i : i + 1, :] += jnp.sum(piece * rows_in, 0, keepdims=True)
    dpqkv[...] = total.astype(dpqkv.dtype)
    ext[GROUP:, :] = ext[:TAIL, :]


def core_backward(dn, pqkv, pab, kept, taps, rate, bias):
    n_in, norm_in, conved, u_in, s_in, t_in = kept
    rows, width = pqkv.shape
    vals = dn.shape[1]
    keys = (width - vals) // 2
    heads = rate.shape[1]
    dk, dv = keys // heads, vals // heads
    blocks = rows // GROUP
    tokens = lambda width: pl.BlockSpec((GROUP, width), lambda n: (blocks - 1 - n, 0))
    stacked = lambda a: pl.BlockSpec((1,) + a.shape[1:], lambda n: (blocks - 1 - n, 0, 0, 0))
    fixed = lambda shape: pl.BlockSpec(shape, lambda n: (0, 0))
    small = (1, 2 * heads)
    return pl.pallas_call(
        backward_kernel,
        grid=(blocks,),
        in_specs=[tokens(a.shape[1]) for a in (dn, pqkv, pab, n_in, norm_in, conved, u_in)]
        + [stacked(s_in), stacked(t_in)]
        + [fixed(a.shape) for a in (taps, rate, bias)],
        out_specs=[tokens(a.shape[1]) for a in (pqkv, pab)]
        + [fixed(taps.shape), fixed(small), fixed((1, dv))],
        out_shape=[jax.ShapeDtypeStruct(pqkv.shape, BF16), jax.ShapeDtypeStruct(pab.shape, F32)]
        + [jax.ShapeDtypeStruct(s, F32) for s in (taps.shape, small, (1, dv))],
        scratch_shapes=[
            pltpu.VMEM((GROUP + TAIL, 2 * keys + vals), F32),
            pltpu.VMEM((heads, dk, dv), F32),
        ],
        compiler_params=pltpu.CompilerParams(dimension_semantics=("arbitrary",), vmem_limit_bytes=40 * 2**20),
        cost_estimate=pl.CostEstimate(flops=20 * 10**9, bytes_accessed=48 * 2**20, transcendentals=10**7),
        name="core_backward",
    )(dn, pqkv, pab, n_in, norm_in, conved, u_in, s_in, t_in, taps, rate, bias)


def rms_norm(values, gain_vec):
    return values * lax.rsqrt(jnp.mean(values * values, -1, keepdims=True) + 1e-05) * gain_vec


def dot(a, b, dims=NN):
    return lax.dot_general(a, b, (dims, ((), ())), preferred_element_type=F32)


def swap(piece, mask):
    return lax.ppermute(piece, "tensor", [(i, i ^ mask) for i in range(4)])


def gather_rows(own, beside=None):
    if lax.axis_size("tensor") != 4:
        full = lax.all_gather(own, "tensor", axis=0, tiled=True)
        return full if beside is None else (full, beside)
    half = own.shape[0] // 2
    first, second = swap(own, 1), swap(own, 2)
    if beside is not None:
        first, second, beside = lax.optimization_barrier((first, second, beside))
    full = jnp.concatenate([own, first, second, swap(second[:half], 1), swap(first[half:], 2)], 0)
    return full if beside is None else (full, beside)


def scatter_rows(part, beside=None):
    if lax.axis_size("tensor") != 4:
        total = lax.psum_scatter(part, "tensor", scatter_dimension=0, tiled=True).astype(F32)
        return total if beside is None else (total, beside)
    rows, half = part.shape[0] // 4, part.shape[1] // 2

    def chunk(k, columns):
        return part[k * rows : (k + 1) * rows, columns]

    plans = ((slice(0, half), 1, 2), (slice(half, 2 * half), 2, 1))
    arrived = [swap(jnp.concatenate([chunk(one, columns), chunk(3, columns)], 0), one) for columns, one, _ in plans]
    if beside is not None:
        arrived, beside = lax.optimization_barrier((arrived, beside))
    owns, passed = [], []
    for (columns, _, two), got in zip(plans, arrived):
        got = got.astype(F32)
        owns.append(chunk(0, columns).astype(F32) + got[:rows])
        passed.append((chunk(two, columns).astype(F32) + got[rows:]).astype(BF16))
    passed = lax.optimization_barrier(passed)
    sums = [own + swap(piece, two).astype(F32) for own, piece, (_, _, two) in zip(owns, passed, plans)]
    total = jnp.concatenate(sums, 1)
    return total if beside is None else (total, beside)


def sum_everywhere(values):
    for axis in ("dp", "tensor"):
        size = lax.axis_size(axis)
        if size & (size - 1):
            values = lax.psum(values, axis)
            continue
        mask = 1
        while mask < size:
            values = values + lax.ppermute(values, axis, [(i, i ^ mask) for i in range(size)])
            mask *= 2
    return values


def reorder(rows_in):
    if lax.axis_size("tensor") != 4:
        return rows_in
    rows = rows_in.shape[0] // 4
    me = lax.axis_index("tensor")
    return jnp.concatenate([lax.dynamic_slice_in_dim(rows_in, (me ^ k) * rows, rows, 0) for k in range(4)], 0)


def norm_back(values, gain_vec, grad):
    factor = lax.rsqrt(jnp.mean(values * values, -1, keepdims=True) + 1e-05)
    normal = values * factor
    scaled = grad * gain_vec
    return (
        factor * (scaled - normal * jnp.mean(scaled * normal, -1, keepdims=True)),
        jnp.sum(grad * normal, 0),
    )


def gather_dp(shard, axis):
    return lax.all_gather(shard.astype(BF16), "dp", axis=axis, tiled=True)


def sibling(piece):
    return lax.ppermute(piece, "dp", [(i, i ^ 1) for i in range(lax.axis_size("dp"))])


def split_blocks(full):
    size = lax.axis_size("dp")
    width = full.shape[1] // size
    core = lax.axis_index("dp") % 2

    def pick(c):
        return jnp.concatenate(
            [lax.dynamic_slice_in_dim(full, (2 * i + c) * width, width, 1) for i in range(size // 2)], 1
        )

    return pick(core), pick(1 - core)


def scatter_dp(part, axis):
    return lax.psum_scatter(part, "dp", scatter_dimension=axis, tiled=True)


def scatter_chips(part, axis):
    size = lax.axis_size("dp")
    groups = [list(range(core, size, 2)) for core in range(2)]
    return lax.psum_scatter(part, "dp", scatter_dimension=axis, tiled=True, axis_index_groups=groups)


def local(
    hidden_in,
    grad_out,
    mix_gain,
    w_query,
    w_key,
    w_value,
    conv_query,
    conv_key,
    conv_value,
    w_decay,
    w_beta,
    log_rate,
    decay_bias,
    w_outgate,
    head_gain,
    w_output,
    ffn_gain,
    w_gate,
    w_up,
    w_down,
):
    dp = lax.axis_size("dp")
    model = hidden_in.shape[1]
    keys, vals, hidden = w_query.shape[1], w_value.shape[1], w_gate.shape[1]
    heads = w_decay.shape[1]
    first_head = lax.axis_index("tensor") * heads
    rate = lax.dynamic_slice_in_dim(log_rate, first_head, heads)[None]
    bias = lax.dynamic_slice_in_dim(decay_bias, first_head, heads)[None]
    gain = jnp.tile(head_gain, heads)

    narrow = jnp.concatenate([w_decay, w_beta], 1).T
    kernels = jnp.concatenate([conv_query, conv_key, conv_value], 1)
    wide = max(narrow.shape[1], kernels.shape[1])
    pad = lambda a: jnp.pad(a, ((0, 0), (0, wide - a.shape[1])))
    few = lax.all_gather(jnp.concatenate([pad(narrow), pad(kernels)], 0).astype(BF16), "dp")
    unroll = lambda a: jnp.swapaxes(a, 0, 1).reshape(a.shape[1], -1)
    full_narrow = unroll(few[:, : 2 * heads, : narrow.shape[1]])
    pieces = few[:, 2 * heads :, : kernels.shape[1]]
    cut = (conv_query.shape[1], conv_query.shape[1] + conv_key.shape[1])
    taps = jnp.concatenate(
        [unroll(pieces[:, :, : cut[0]]), unroll(pieces[:, :, cut[0] : cut[1]]), unroll(pieces[:, :, cut[1] :])], 1
    ).astype(F32)

    full_qkv = gather_dp(jnp.concatenate([w_query, w_key, w_value], 1), 0)
    full_gate_out = gather_dp(jnp.concatenate([w_outgate, w_output.T], 1), 0)
    full_outgate, full_output = full_gate_out[:, :vals], full_gate_out[:, vals:]
    full_pair = gather_dp(jnp.concatenate([w_gate, w_up], 1), 0)
    full_down = gather_dp(w_down, 1)

    hold = lax.optimization_barrier
    rows_in = hidden_in.astype(F32)
    normed = reorder(gather_rows(rms_norm(rows_in, mix_gain).astype(BF16)))
    cot_own, _ = hold((grad_out, normed))
    cot = gather_rows(cot_own)
    pqkv = dot(normed, full_qkv)
    pab = dot(normed, full_narrow, NT)
    pqkv, cot, normed_here, normed_there = hold((pqkv, cot, *split_blocks(normed)))
    kept = core_forward(pqkv, pab, taps, rate, bias, keys)
    po = dot(normed, full_outgate)
    po_sig = jax.nn.sigmoid(po)
    mixed = (kept[0].astype(F32) * gain * (po * po_sig)).astype(BF16)
    middle = rows_in + scatter_rows(reorder(dot(mixed, full_output, NT).astype(BF16)))

    ffn_rows = gather_rows(rms_norm(middle, ffn_gain).astype(BF16))
    pre = dot(ffn_rows, full_pair)
    gate_pre, up_pre = pre[:, :hidden], pre[:, hidden:]
    gate_sig = jax.nn.sigmoid(gate_pre)
    activ = (gate_pre * gate_sig * up_pre).astype(BF16)
    cot, part_down = hold((cot, dot(activ, cot, TN).astype(BF16)))
    grad_w_down = scatter_dp(part_down, 1)
    grad_activ = dot(cot, full_down, NT)
    grad_gate_pre = (grad_activ * up_pre * gate_sig * (1.0 + gate_pre * (1.0 - gate_sig))).astype(BF16)
    grad_up_pre = (grad_activ * (gate_pre * gate_sig)).astype(BF16)
    grad_pre = jnp.concatenate([grad_gate_pre, grad_up_pre], 1)
    ffn_here, ffn_there = split_blocks(ffn_rows)
    grad_pre, sent = hold((grad_pre, dot(ffn_there, grad_pre, TN).astype(BF16)))
    got = sibling(sent)
    grad_ffn_rows, got = hold((dot(grad_pre, full_pair, NT).astype(BF16), got))
    part_pair = (dot(ffn_here, grad_pre, TN) + got.astype(F32)).astype(BF16)
    grad_ffn_norm, part_pair = scatter_rows(grad_ffn_rows, part_pair)
    grad_pair = scatter_chips(part_pair, 0)
    grad_middle_norm, ffn_gain_part = norm_back(middle, ffn_gain, grad_ffn_norm)
    grad_middle = grad_out.astype(F32) + grad_middle_norm

    activ_late, mix_low = hold((activ, grad_middle.astype(BF16)))
    mix_cot, out_part = gather_rows(mix_low, dot(activ_late, full_down).astype(BF16))
    mix_cot = reorder(mix_cot)
    mix_here, mix_there = split_blocks(mix_cot)
    mix_cot, sent_output = hold((mix_cot, dot(mix_there, mixed, TN).astype(BF16)))
    grad_mixed = dot(mix_cot, full_output)
    grad_po = grad_mixed * kept[0].astype(F32) * gain * (po_sig * (1.0 + po * (1.0 - po_sig)))
    grad_po = grad_po.astype(BF16)
    grad_n = grad_mixed * gain * (po * po_sig)
    sent_outgate = dot(normed_there, grad_po, TN).astype(BF16)
    got_output, got_outgate = sibling(sent_output), sibling(sent_outgate)
    part_output = (dot(mix_here, mixed, TN) + got_output.astype(F32)).astype(BF16)
    part_outgate = (dot(normed_here, grad_po, TN) + got_outgate.astype(F32)).astype(BF16)
    part_gate_out = jnp.concatenate([part_outgate, part_output], 1)
    grad_n, grad_w_down, part_gate_out = hold((grad_n, grad_w_down, part_gate_out))
    grad_gate_out = scatter_chips(part_gate_out, 0)
    grad_pqkv, grad_pab, grad_taps, grad_small, grad_gain = core_backward(grad_n, pqkv, pab, kept, taps, rate, bias)
    grad_pqkv, grad_pair = hold((grad_pqkv, grad_pair))
    out_rows, grad_pqkv = scatter_rows(out_part, grad_pqkv)
    hidden_out = (middle + out_rows).astype(BF16)
    part_qkv = dot(normed, grad_pqkv, TN).astype(BF16)
    grad_pqkv, grad_pab, grad_taps, part_qkv = hold((grad_pqkv, grad_pab, grad_taps, part_qkv))
    grad_qkv = scatter_dp(part_qkv, 0)
    low_pab = grad_pab.astype(BF16)
    grad_normed = dot(grad_pqkv, full_qkv, NT) + dot(grad_po, full_outgate, NT) + dot(low_pab, full_narrow)
    mix_gain_part = jnp.sum(grad_normed * normed.astype(F32), 0) / mix_gain
    grad_mix_norm = scatter_rows(reorder(grad_normed.astype(BF16)))
    grad_rows, _ = norm_back(rows_in, mix_gain, grad_mix_norm)
    grad_in = (grad_middle + grad_rows).astype(BF16)

    grad_narrow = dot(low_pab, normed, TN)
    roll = lambda a: jnp.swapaxes(a.reshape(a.shape[0], dp, -1), 0, 1)
    grad_kernels = jnp.concatenate(
        [roll(grad_taps[:, :keys]), roll(grad_taps[:, keys : 2 * keys]), roll(grad_taps[:, 2 * keys :])], 2
    )
    pad3 = lambda a: jnp.pad(a, ((0, 0), (0, 0), (0, wide - a.shape[2])))
    few_parts = jnp.concatenate([pad3(roll(grad_narrow)), pad3(grad_kernels)], 1)
    few_grads = jnp.sum(lax.all_to_all(few_parts, "dp", 0, 0, tiled=True), 0)
    grad_narrow = few_grads[: 2 * heads, : narrow.shape[1]].T
    grad_kernels = few_grads[2 * heads :, : kernels.shape[1]]

    place = lambda a: lax.dynamic_update_slice_in_dim(jnp.zeros_like(log_rate), a, first_head, 0)
    sums = sum_everywhere(
        jnp.concatenate(
            [
                mix_gain_part,
                ffn_gain_part,
                grad_gain[0] / head_gain,
                place(grad_small[0, :heads]),
                place(grad_small[0, heads:]),
            ]
        )
    )
    ends = [model, 2 * model, 2 * model + head_gain.shape[0], 2 * model + head_gain.shape[0] + log_rate.shape[0]]
    grad_mix_gain, grad_ffn_gain, grad_head_gain, grad_log_rate, grad_decay_bias = jnp.split(sums, ends)
    grad_qkv, grad_gate_out, grad_pair = grad_qkv.astype(F32), grad_gate_out.astype(F32), grad_pair.astype(F32)
    return (
        hidden_out,
        grad_in,
        grad_mix_gain,
        grad_qkv[:, :keys],
        grad_qkv[:, keys : 2 * keys],
        grad_qkv[:, 2 * keys :],
        grad_kernels[:, : cut[0]],
        grad_kernels[:, cut[0] : cut[1]],
        grad_kernels[:, cut[1] :],
        grad_narrow[:, :heads],
        grad_narrow[:, heads:],
        grad_log_rate,
        grad_decay_bias,
        grad_gate_out[:, :vals],
        grad_head_gain,
        grad_gate_out[:, vals:].T,
        grad_ffn_gain,
        grad_pair[:, :hidden],
        grad_pair[:, hidden:],
        grad_w_down.astype(F32),
    )


def solution(mesh):
    rows, both, flat = P(("dp", "tensor"), None), P("dp", "tensor"), P(None, ("tensor", "dp"))
    turned = P("tensor", "dp")
    return jax.shard_map(
        local,
        mesh=mesh,
        in_specs=(
            *(rows, rows, P()),
            *(both, both, both, flat, flat, flat, both, both),
            *(P(), P(), both, P(), turned, P(), both, both, turned),
        ),
        out_specs=(
            *(rows, rows, P()),
            *(both, both, both, flat, flat, flat, both, both),
            *(P(), P(), both, P(), turned, P(), both, both, turned),
        ),
        check_vma=False,
    )
```

```python
import jax
import jax.numpy as jnp
from jax import lax
from jax.experimental import pallas as pl
from jax.experimental.pallas import tpu as pltpu
from jax.sharding import PartitionSpec as P

GROUP = 64
TAIL = 8
F32 = jnp.float32
BF16 = jnp.bfloat16
HIGHEST = lax.Precision.HIGHEST


def mm(a, b, dims=((1,), (0,))):
    return lax.dot_general(a.astype(BF16), b.astype(BF16), (dims, ((), ())), preferred_element_type=F32)


NN = ((1,), (0,))
NT = ((1,), (1,))
TN = ((0,), (0,))


def mm_exact(a, b, dims=NN):
    return lax.dot_general(a, b, (dims, ((), ())), precision=HIGHEST, preferred_element_type=F32)


def halves(a):
    high = a.astype(BF16)
    return high, (a - high.astype(F32)).astype(BF16)


def mm_split(a, b):
    a_high, a_low = halves(a)
    b_high, b_low = halves(b)
    return mm(a_high, b_high) + (mm(a_high, b_low) + mm(a_low, b_high))


def sigmoid(x):
    return 1.0 / (1.0 + jnp.exp(-x))


def softplus(x):
    return jnp.maximum(x, 0.0) + jnp.log1p(jnp.exp(-jnp.abs(x)))


def grid_iota(size):
    return (
        lax.broadcasted_iota(jnp.int32, (size, size), 0),
        lax.broadcasted_iota(jnp.int32, (size, size), 1),
    )


def unit_lower_inverses(lowers, row, col):
    size = lowers[0].shape[0]
    base = 16
    eye = jnp.where(row == col, 1.0, 0.0)
    powers = [jnp.where(row // base == col // base, -lower, 0.0) for lower in lowers]
    inverses = [eye + power for power in powers]
    reach = 2
    while reach < base:
        powers = [mm_split(power, power) for power in powers]
        inverses = [inverse + mm_split(inverse, power) for inverse, power in zip(inverses, powers)]
        reach *= 2
    while base < size:
        wide = 2 * base
        off = (row // wide == col // wide) & (row // base > col // base)
        right = [mm_split(jnp.where(off, lower, 0.0), inverse) for lower, inverse in zip(lowers, inverses)]
        inverses = [inverse - mm_split(inverse, r) for inverse, r in zip(inverses, right)]
        base = wide
    return inverses


def gates(p_ab, rate, bias, heads):
    pre = p_ab[:, :heads] + bias
    return sigmoid(p_ab[:, heads:]), -jnp.exp(rate) * softplus(pre), pre


def forward_kernel(
    pqkv, pab, taps, rate, bias,
    n_out, norm_out, conved, u_out, s_out, t_out,
    ext, state,
):
    heads = rate.shape[1]
    vals = n_out.shape[1]
    keys = (pqkv.shape[1] - vals) // 2
    dk, dv = keys // heads, vals // heads

    @pl.when(pl.program_id(0) == 0)
    def _():
        ext[...] = jnp.zeros_like(ext)
        state[...] = jnp.zeros_like(state)

    ext[TAIL:, :] = pqkv[...]
    n_taps = taps.shape[0]
    total = None
    for i in range(n_taps):
        start = TAIL - (n_taps - 1) + i
        term = ext[start : start + GROUP, :] * taps[i : i + 1, :]
        total = term if total is None else total + term
    conved[...] = total
    ext[:TAIL, :] = ext[GROUP:, :]

    row, col = grid_iota(GROUP)
    tri = jnp.where(row >= col, 1.0, 0.0)
    beta, log_decay, _ = gates(pab[...], rate[...], bias[...], heads)
    c_col = mm_exact(tri, log_decay)
    c_row = mm_exact(log_decay, jnp.where(row <= col, 1.0, 0.0), TN)
    start_decay = jnp.exp(c_col)
    end_decay = jnp.exp(c_col[GROUP - 1 :, :] - c_col)
    last_decay = jnp.exp(c_col[GROUP - 1 :, :])

    qs, ks, vs, bs, prods, relatives, lowers = [], [], [], [], [], [], []
    for h in range(heads):
        uq = conved[:, h * dk : (h + 1) * dk]
        uk = conved[:, keys + h * dk : keys + (h + 1) * dk]
        uv = conved[:, 2 * keys + h * dv : 2 * keys + (h + 1) * dv]
        q = uq * sigmoid(uq)
        qs.append(q * (lax.rsqrt(jnp.sum(q * q, -1, keepdims=True) + 1e-6) * dk**-0.5))
        k = uk * sigmoid(uk)
        ks.append(k * lax.rsqrt(jnp.sum(k * k, -1, keepdims=True) + 1e-6))
        vs.append(uv * sigmoid(uv))
        bs.append(beta[:, h : h + 1])
    for h in range(heads):
        prods.append(mm(jnp.concatenate([ks[h], qs[h]], 0), ks[h], NT))
    for h in range(heads):
        differ = jnp.minimum(c_col[:, h : h + 1] - c_row[h : h + 1, :], 0.0)
        relatives.append(jnp.where(row >= col, jnp.exp(differ), 0.0))
        lowers.append(jnp.where(row > col, bs[h] * relatives[h] * prods[h][:GROUP], 0.0))
    invs = [inverse.astype(BF16) for inverse in unit_lower_inverses(lowers, row, col)]
    states = [state[h] for h in range(heads)]
    lows = [s.astype(BF16) for s in states]
    reads = []
    for h in range(heads):
        e = start_decay[:, h : h + 1]
        reads.append(mm(jnp.concatenate([ks[h] * e, qs[h] * e], 0), lows[h]))
    us = [mm(invs[h], bs[h] * (vs[h] - reads[h][:GROUP])).astype(BF16) for h in range(heads)]
    outs = [reads[h][GROUP:] + mm(relatives[h] * prods[h][GROUP:], us[h]) for h in range(heads)]
    nexts = [
        last_decay[:, h : h + 1] * states[h] + mm(ks[h] * end_decay[:, h : h + 1], us[h], TN) for h in range(heads)
    ]
    for h in range(heads):
        cols = slice(h * dv, (h + 1) * dv)
        state[h] = nexts[h]
        t_out[0, h] = invs[h]
        s_out[0, h] = lows[h]
        u_out[:, cols] = us[h]
        o = outs[h]
        norm = lax.rsqrt(jnp.mean(o * o, -1, keepdims=True) + 1e-5)
        n_out[:, cols] = (o * norm).astype(n_out.dtype)
        norm_out[:, h : h + 1] = norm


def core_forward(pqkv, pab, taps, rate, bias, keys):
    rows, width = pqkv.shape
    vals = width - 2 * keys
    heads = rate.shape[1]
    dk, dv = keys // heads, vals // heads
    blocks = rows // GROUP
    tokens = lambda width: pl.BlockSpec((GROUP, width), lambda n: (n, 0))
    fixed = lambda a: pl.BlockSpec(a.shape, lambda n: (0, 0))
    return pl.pallas_call(
        forward_kernel,
        grid=(blocks,),
        in_specs=[tokens(a.shape[1]) for a in (pqkv, pab)] + [fixed(a) for a in (taps, rate, bias)],
        out_specs=[
            tokens(vals),
            tokens(heads),
            tokens(width),
            tokens(vals),
            pl.BlockSpec((1, heads, dk, dv), lambda n: (n, 0, 0, 0)),
            pl.BlockSpec((1, heads, GROUP, GROUP), lambda n: (n, 0, 0, 0)),
        ],
        out_shape=[
            jax.ShapeDtypeStruct((rows, vals), BF16),
            jax.ShapeDtypeStruct((rows, heads), F32),
            jax.ShapeDtypeStruct((rows, width), F32),
            jax.ShapeDtypeStruct((rows, vals), BF16),
            jax.ShapeDtypeStruct((blocks, heads, dk, dv), BF16),
            jax.ShapeDtypeStruct((blocks, heads, GROUP, GROUP), BF16),
        ],
        scratch_shapes=[
            pltpu.VMEM((GROUP + TAIL, 2 * keys + vals), F32),
            pltpu.VMEM((heads, dk, dv), F32),
        ],
        compiler_params=pltpu.CompilerParams(dimension_semantics=("arbitrary",), vmem_limit_bytes=40 * 2**20),
        cost_estimate=pl.CostEstimate(flops=8 * 10**9, bytes_accessed=32 * 2**20, transcendentals=10**7),
        name="core_forward",
    )(pqkv, pab, taps, rate, bias)


def backward_kernel(
    dn_in, pqkv, pab, n_in, norm_in, conved, u_in, s_in, t_in, taps, rate, bias,
    dpqkv, dpab, dtaps, dsmall, dgain,
    ext, dstate,
):
    heads = rate.shape[1]
    vals = dn_in.shape[1]
    keys = (pqkv.shape[1] - vals) // 2
    dk, dv = keys // heads, vals // heads

    @pl.when(pl.program_id(0) == 0)
    def _():
        ext[...] = jnp.zeros_like(ext)
        dstate[...] = jnp.zeros_like(dstate)
        for ref in (dtaps, dsmall, dgain):
            ref[...] = jnp.zeros_like(ref)

    row, col = grid_iota(GROUP)
    tri = jnp.where(row >= col, 1.0, 0.0)
    upper = jnp.where(row <= col, 1.0, 0.0)
    beta, log_decay, pre = gates(pab[...], rate[...], bias[...], heads)
    c_col = mm_exact(tri, log_decay)
    c_row = mm_exact(log_decay, upper, TN)
    start_decay = jnp.exp(c_col)
    end_decay = jnp.exp(c_col[GROUP - 1 :, :] - c_col)
    last_decay = jnp.exp(c_col[GROUP - 1 :, :])
    lane = lax.broadcasted_iota(jnp.int32, (1, heads), 1)
    d_beta = jnp.zeros((GROUP, heads), F32)
    after = jnp.zeros((GROUP, heads), F32)
    before = jnp.zeros((GROUP, heads), F32)
    d_log = jnp.zeros((GROUP, heads), F32)
    gain_sum = jnp.zeros((1, dv), F32)

    for h in range(heads):
        ks, vs = slice(h * dk, (h + 1) * dk), slice(h * dv, (h + 1) * dv)
        kx, vx = slice(keys + h * dk, keys + (h + 1) * dk), slice(2 * keys + h * dv, 2 * keys + (h + 1) * dv)
        here = lane == h
        uq, uk, uv = conved[:, ks], conved[:, kx], conved[:, vx]
        sq, sk, sv = sigmoid(uq), sigmoid(uk), sigmoid(uv)
        q = uq * sq
        q_norm = lax.rsqrt(jnp.sum(q * q, -1, keepdims=True) + 1e-6)
        q = q * q_norm
        k = uk * sk
        k_norm = lax.rsqrt(jnp.sum(k * k, -1, keepdims=True) + 1e-6)
        k = k * k_norm
        v = uv * sv
        qs = q * dk**-0.5
        b = beta[:, h : h + 1]
        e = start_decay[:, h : h + 1]
        f = end_decay[:, h : h + 1]
        kb = k.astype(BF16)
        qb = qs.astype(BF16)

        n = n_in[:, vs].astype(F32)
        dn = dn_in[:, vs]
        dnn = dn * n
        gain_sum = gain_sum + jnp.sum(dnn, 0, keepdims=True)
        do = norm_in[:, h : h + 1] * (dn - n * jnp.mean(dnn, -1, keepdims=True))

        prod = mm(jnp.concatenate([kb, qb], 0), kb, NT)
        relative = jnp.where(row >= col, jnp.exp(jnp.minimum(c_col[:, h : h + 1] - c_row[h : h + 1, :], 0.0)), 0.0)
        kk, qk = prod[:GROUP], prod[GROUP:]
        strict = jnp.where(row > col, relative, 0.0)
        mix = relative * qk
        s_prev = s_in[0, h]
        u = u_in[:, vs]
        inv = t_in[0, h]
        ds = dstate[h]
        ds_low = ds.astype(BF16)
        dob = do.astype(BF16)
        ke, qe, kd = k * e, qs * e, k * f
        du = mm(mix, dob, TN) + mm(kd, ds_low)
        dr = mm(inv, du, TN)
        pair = jnp.concatenate([dob, dr.astype(BF16)], 0)
        dstate[h] = last_decay[:, h : h + 1] * ds + mm(jnp.concatenate([qe, -(b * ke)], 0), pair, TN)
        cross = mm(pair, u, NT)
        dmix = jnp.where(row >= col, cross[:GROUP], 0.0)
        dlow = jnp.where(row > col, -cross[GROUP:], 0.0)
        back = mm(pair, s_prev, NT)
        dqe, x = back[:GROUP], back[GROUP:]
        dkd = mm(u, ds_low, NT)
        dke = -(b * x)
        rk = strict * kk
        d_beta = d_beta + jnp.where(
            here,
            jnp.sum(dr * v, -1, keepdims=True) - jnp.sum(x * ke, -1, keepdims=True) + jnp.sum(dlow * rk, -1, keepdims=True),
            0.0,
        )
        dpair = dlow * (b * rk) + dmix * mix
        spread = mm(upper, dpair)
        last_part = last_decay[:, h : h + 1] * jnp.sum(ds * s_prev.astype(F32), keepdims=True)
        d_log = d_log + jnp.where(here, jnp.sum(jnp.where(row > col, spread, 0.0), -1, keepdims=True) + last_part, 0.0)
        after = after + jnp.where(here, jnp.sum(dqe * qe + dke * ke, -1, keepdims=True), 0.0)
        before = before + jnp.where(here, jnp.sum(dkd * kd, -1, keepdims=True), 0.0)
        dqk = dmix * relative
        dkk = dlow * (b * strict)
        first = mm(jnp.concatenate([dqk, dkk], 0), kb)
        dq = e * dqe + first[:GROUP]
        dk_ = e * dke + f * dkd + first[GROUP:] + mm(jnp.concatenate([dkk, dqk], 0), jnp.concatenate([kb, qb], 0), TN)
        dq = dq * dk**-0.5
        dq = q_norm * (dq - q * jnp.sum(dq * q, -1, keepdims=True))
        dk_ = k_norm * (dk_ - k * jnp.sum(dk_ * k, -1, keepdims=True))
        ext[:GROUP, ks] = dq * (sq * (1.0 + uq * (1.0 - sq)))
        ext[:GROUP, kx] = dk_ * (sk * (1.0 + uk * (1.0 - sk)))
        ext[:GROUP, vx] = (b * dr) * (sv * (1.0 + uv * (1.0 - sv)))

    d_log = d_log + mm_exact(upper, after) + mm_exact(jnp.where(row > col, 1.0, 0.0), before)
    d_pre = d_log * (-jnp.exp(rate[...])) * sigmoid(pre)
    dpab[:, :heads] = d_pre
    dpab[:, heads:] = d_beta * beta * (1.0 - beta)
    dsmall[0:1, :heads] += jnp.sum(d_log * log_decay, 0, keepdims=True)
    dsmall[0:1, heads:] += jnp.sum(d_pre, 0, keepdims=True)
    dgain[...] += gain_sum

    n_taps = taps.shape[0]
    rows_in = pqkv[...]
    total = None
    for i in range(n_taps):
        start = n_taps - 1 - i
        piece = ext[start : start + GROUP, :]
        term = piece * taps[i : i + 1, :]
        total = term if total is None else total + term
        dtaps[i : i + 1, :] += jnp.sum(piece * rows_in, 0, keepdims=True)
    dpqkv[...] = total.astype(dpqkv.dtype)
    ext[GROUP:, :] = ext[:TAIL, :]


def core_backward(dn, pqkv, pab, kept, taps, rate, bias):
    n_in, norm_in, conved, u_in, s_in, t_in = kept
    rows, width = pqkv.shape
    vals = dn.shape[1]
    keys = (width - vals) // 2
    heads = rate.shape[1]
    dk, dv = keys // heads, vals // heads
    blocks = rows // GROUP
    tokens = lambda width: pl.BlockSpec((GROUP, width), lambda n: (blocks - 1 - n, 0))
    stacked = lambda a: pl.BlockSpec((1,) + a.shape[1:], lambda n: (blocks - 1 - n, 0, 0, 0))
    fixed = lambda shape: pl.BlockSpec(shape, lambda n: (0, 0))
    small = (1, 2 * heads)
    return pl.pallas_call(
        backward_kernel,
        grid=(blocks,),
        in_specs=[tokens(a.shape[1]) for a in (dn, pqkv, pab, n_in, norm_in, conved, u_in)]
        + [stacked(s_in), stacked(t_in)]
        + [fixed(a.shape) for a in (taps, rate, bias)],
        out_specs=[tokens(a.shape[1]) for a in (pqkv, pab)]
        + [fixed(taps.shape), fixed(small), fixed((1, dv))],
        out_shape=[jax.ShapeDtypeStruct(pqkv.shape, BF16), jax.ShapeDtypeStruct(pab.shape, F32)]
        + [jax.ShapeDtypeStruct(s, F32) for s in (taps.shape, small, (1, dv))],
        scratch_shapes=[
            pltpu.VMEM((GROUP + TAIL, 2 * keys + vals), F32),
            pltpu.VMEM((heads, dk, dv), F32),
        ],
        compiler_params=pltpu.CompilerParams(dimension_semantics=("arbitrary",), vmem_limit_bytes=40 * 2**20),
        cost_estimate=pl.CostEstimate(flops=20 * 10**9, bytes_accessed=48 * 2**20, transcendentals=10**7),
        name="core_backward",
    )(dn, pqkv, pab, n_in, norm_in, conved, u_in, s_in, t_in, taps, rate, bias)


def projections_kernel(dqkv, dpo, dab, w_qkv, w_out, w_ab, normed, out, sums):
    grad = (
        mm(dqkv[...], w_qkv[...], NT)
        + mm(dpo[...], w_out[...], NT)
        + mm(dab[...], w_ab[...])
    )
    out[...] = grad.astype(out.dtype)
    sums[...] = jnp.sum(grad * normed[...].astype(F32), 0, keepdims=True)


def projections_back(dqkv, dpo, dab, w_qkv, w_out, w_ab, normed):
    rows, model = normed.shape
    tile = 256
    whole = lambda a: pl.BlockSpec(a.shape, lambda n: (0, 0), pipeline_mode=pl.Buffered(1))
    return pl.pallas_call(
        projections_kernel,
        grid=(model // tile,),
        in_specs=[
            whole(dqkv),
            whole(dpo),
            whole(dab),
            pl.BlockSpec((tile, dqkv.shape[1]), lambda n: (n, 0)),
            pl.BlockSpec((tile, dpo.shape[1]), lambda n: (n, 0)),
            pl.BlockSpec((dab.shape[1], tile), lambda n: (0, n)),
            pl.BlockSpec((rows, tile), lambda n: (0, n)),
        ],
        out_specs=[pl.BlockSpec((rows, tile), lambda n: (0, n)), pl.BlockSpec((1, tile), lambda n: (0, n))],
        out_shape=[jax.ShapeDtypeStruct((rows, model), BF16), jax.ShapeDtypeStruct((1, model), F32)],
        compiler_params=pltpu.CompilerParams(dimension_semantics=("arbitrary",), vmem_limit_bytes=40 * 2**20),
        cost_estimate=pl.CostEstimate(
            flops=2 * rows * model * (dqkv.shape[1] + dpo.shape[1]), bytes_accessed=32 * 2**20, transcendentals=0
        ),
        name="projections_back",
    )(dqkv, dpo, dab, w_qkv, w_out, w_ab, normed)


def rms_norm(values, gain_vec):
    return values * lax.rsqrt(jnp.mean(values * values, -1, keepdims=True) + 1e-05) * gain_vec


def dot(a, b, dims=NN):
    return lax.dot_general(a, b, (dims, ((), ())), preferred_element_type=F32)


def swap(piece, mask):
    return lax.ppermute(piece, "tensor", [(i, i ^ mask) for i in range(4)])


def gather_rows(own, beside=None):
    if lax.axis_size("tensor") != 4:
        full = lax.all_gather(own, "tensor", axis=0, tiled=True)
        return full if beside is None else (full, beside)
    half = own.shape[0] // 2
    first, second = swap(own, 1), swap(own, 2)
    if beside is not None:
        first, second, beside = lax.optimization_barrier((first, second, beside))
    full = jnp.concatenate([own, first, second, swap(second[:half], 1), swap(first[half:], 2)], 0)
    return full if beside is None else (full, beside)


def scatter_rows(part, beside=None):
    if lax.axis_size("tensor") != 4:
        total = lax.psum_scatter(part, "tensor", scatter_dimension=0, tiled=True).astype(F32)
        return total if beside is None else (total, beside)
    rows, half = part.shape[0] // 4, part.shape[1] // 2

    def chunk(k, columns):
        return part[k * rows : (k + 1) * rows, columns]

    plans = ((slice(0, half), 1, 2), (slice(half, 2 * half), 2, 1))
    arrived = [swap(jnp.concatenate([chunk(one, columns), chunk(3, columns)], 0), one) for columns, one, _ in plans]
    if beside is not None:
        arrived, beside = lax.optimization_barrier((arrived, beside))
    owns, passed = [], []
    for (columns, _, two), got in zip(plans, arrived):
        got = got.astype(F32)
        owns.append(chunk(0, columns).astype(F32) + got[:rows])
        passed.append((chunk(two, columns).astype(F32) + got[rows:]).astype(BF16))
    passed = lax.optimization_barrier(passed)
    sums = [own + swap(piece, two).astype(F32) for own, piece, (_, _, two) in zip(owns, passed, plans)]
    total = jnp.concatenate(sums, 1)
    return total if beside is None else (total, beside)


def scatter_direct(part, beside):
    if lax.axis_size("tensor") != 4:
        return lax.psum_scatter(part, "tensor", scatter_dimension=0, tiled=True).astype(F32), beside
    chunks = jnp.split(part, 4)
    arrived, beside = lax.optimization_barrier(([swap(chunks[k], k) for k in range(1, 4)], beside))
    return sum((piece.astype(F32) for piece in arrived), chunks[0].astype(F32)), beside


def sum_along(values, axis):
    size = lax.axis_size(axis)
    if size & (size - 1):
        return lax.psum(values, axis)
    mask = 1
    while mask < size:
        values = values + lax.ppermute(values, axis, [(i, i ^ mask) for i in range(size)])
        mask *= 2
    return values


def reorder(rows_in):
    if lax.axis_size("tensor") != 4:
        return rows_in
    rows = rows_in.shape[0] // 4
    me = lax.axis_index("tensor")
    return jnp.concatenate([lax.dynamic_slice_in_dim(rows_in, (me ^ k) * rows, rows, 0) for k in range(4)], 0)


def norm_back(values, gain_vec, grad):
    factor = lax.rsqrt(jnp.mean(values * values, -1, keepdims=True) + 1e-05)
    normal = values * factor
    scaled = grad * gain_vec
    return (
        factor * (scaled - normal * jnp.mean(scaled * normal, -1, keepdims=True)),
        jnp.sum(grad * normal, 0),
    )


def gather_dp(shard, axis):
    return lax.all_gather(shard.astype(BF16), "dp", axis=axis, tiled=True)


def sibling(piece):
    return lax.ppermute(piece, "dp", [(i, i ^ 1) for i in range(lax.axis_size("dp"))])


def split_blocks(full):
    size = lax.axis_size("dp")
    width = full.shape[1] // size
    core = lax.axis_index("dp") % 2

    def pick(c):
        return jnp.concatenate(
            [lax.dynamic_slice_in_dim(full, (2 * i + c) * width, width, 1) for i in range(size // 2)], 1
        )

    return pick(core), pick(1 - core)


def scatter_dp(part, axis):
    return lax.psum_scatter(part, "dp", scatter_dimension=axis, tiled=True)


def scatter_chips(part, axis):
    size = lax.axis_size("dp")
    groups = [list(range(core, size, 2)) for core in range(2)]
    return lax.psum_scatter(part, "dp", scatter_dimension=axis, tiled=True, axis_index_groups=groups)


def local(
    hidden_in,
    grad_out,
    mix_gain,
    w_query,
    w_key,
    w_value,
    conv_query,
    conv_key,
    conv_value,
    w_decay,
    w_beta,
    log_rate,
    decay_bias,
    w_outgate,
    head_gain,
    w_output,
    ffn_gain,
    w_gate,
    w_up,
    w_down,
):
    dp = lax.axis_size("dp")
    model = hidden_in.shape[1]
    keys, vals, hidden = w_query.shape[1], w_value.shape[1], w_gate.shape[1]
    heads = w_decay.shape[1]
    first_head = lax.axis_index("tensor") * heads
    rate = lax.dynamic_slice_in_dim(log_rate, first_head, heads)[None]
    bias = lax.dynamic_slice_in_dim(decay_bias, first_head, heads)[None]
    gain = jnp.tile(head_gain, heads)

    narrow = jnp.concatenate([w_decay, w_beta], 1).T
    kernels = jnp.concatenate([conv_query, conv_key, conv_value], 1)
    wide = max(narrow.shape[1], kernels.shape[1])
    pad = lambda a: jnp.pad(a, ((0, 0), (0, wide - a.shape[1])))
    few = lax.all_gather(jnp.concatenate([pad(narrow), pad(kernels)], 0).astype(BF16), "dp")
    unroll = lambda a: jnp.swapaxes(a, 0, 1).reshape(a.shape[1], -1)
    full_narrow = unroll(few[:, : 2 * heads, : narrow.shape[1]])
    pieces = few[:, 2 * heads :, : kernels.shape[1]]
    cut = (conv_query.shape[1], conv_query.shape[1] + conv_key.shape[1])
    taps = jnp.concatenate(
        [unroll(pieces[:, :, : cut[0]]), unroll(pieces[:, :, cut[0] : cut[1]]), unroll(pieces[:, :, cut[1] :])], 1
    ).astype(F32)

    full_qkv = gather_dp(jnp.concatenate([w_query, w_key, w_value], 1), 0)
    full_gate_out = gather_dp(jnp.concatenate([w_outgate, w_output.T], 1), 0)
    full_outgate, full_output = full_gate_out[:, :vals], full_gate_out[:, vals:]
    full_pair = gather_dp(jnp.concatenate([w_gate, w_up], 1), 0)
    full_down = gather_dp(w_down, 1)

    hold = lax.optimization_barrier
    rows_in = hidden_in.astype(F32)
    normed = reorder(gather_rows(rms_norm(rows_in, mix_gain).astype(BF16)))
    cot_own, _ = hold((grad_out, normed))
    cot = gather_rows(cot_own)
    pqkv = dot(normed, full_qkv)
    pab = dot(normed, full_narrow, NT)
    pqkv, cot, normed_here, normed_there = hold((pqkv, cot, *split_blocks(normed)))
    kept = core_forward(pqkv, pab, taps, rate, bias, keys)
    po = dot(normed, full_outgate)
    po_sig = jax.nn.sigmoid(po)
    mixed = (kept[0].astype(F32) * gain * (po * po_sig)).astype(BF16)
    middle = rows_in + scatter_rows(reorder(dot(mixed, full_output, NT).astype(BF16)))

    ffn_rows = gather_rows(rms_norm(middle, ffn_gain).astype(BF16))
    pre = dot(ffn_rows, full_pair)
    gate_pre, up_pre = pre[:, :hidden], pre[:, hidden:]
    gate_sig = jax.nn.sigmoid(gate_pre)
    activ = (gate_pre * gate_sig * up_pre).astype(BF16)
    cot, part_down = hold((cot, dot(activ, cot, TN).astype(BF16)))
    grad_w_down = scatter_dp(part_down, 1)
    grad_activ = dot(cot, full_down, NT)
    grad_gate_pre = (grad_activ * up_pre * gate_sig * (1.0 + gate_pre * (1.0 - gate_sig))).astype(BF16)
    grad_up_pre = (grad_activ * (gate_pre * gate_sig)).astype(BF16)
    grad_pre = jnp.concatenate([grad_gate_pre, grad_up_pre], 1)
    ffn_here, ffn_there = split_blocks(ffn_rows)
    grad_pre, sent = hold((grad_pre, dot(ffn_there, grad_pre, TN).astype(BF16)))
    got = sibling(sent)
    grad_ffn_rows, got = hold((dot(grad_pre, full_pair, NT).astype(BF16), got))
    part_pair = (dot(ffn_here, grad_pre, TN) + got.astype(F32)).astype(BF16)
    grad_ffn_norm, part_pair = scatter_rows(grad_ffn_rows, part_pair)
    grad_pair = scatter_chips(part_pair, 0)
    grad_middle_norm, ffn_gain_part = norm_back(middle, ffn_gain, grad_ffn_norm)
    grad_middle = grad_out.astype(F32) + grad_middle_norm

    activ_late, mix_low = hold((activ, grad_middle.astype(BF16)))
    mix_cot, out_part = gather_rows(mix_low, dot(activ_late, full_down).astype(BF16))
    mix_cot = reorder(mix_cot)
    mix_here, mix_there = split_blocks(mix_cot)
    mix_cot, sent_output = hold((mix_cot, dot(mix_there, mixed, TN).astype(BF16)))
    grad_mixed = dot(mix_cot, full_output)
    grad_po = grad_mixed * kept[0].astype(F32) * gain * (po_sig * (1.0 + po * (1.0 - po_sig)))
    grad_po = grad_po.astype(BF16)
    grad_n = grad_mixed * gain * (po * po_sig)
    sent_outgate = dot(normed_there, grad_po, TN).astype(BF16)
    got_output, got_outgate = sibling(sent_output), sibling(sent_outgate)
    part_output = (dot(mix_here, mixed, TN) + got_output.astype(F32)).astype(BF16)
    part_outgate = (dot(normed_here, grad_po, TN) + got_outgate.astype(F32)).astype(BF16)
    part_gate_out = jnp.concatenate([part_outgate, part_output], 1)
    grad_n, grad_w_down, part_gate_out = hold((grad_n, grad_w_down, part_gate_out))
    grad_gate_out = scatter_chips(part_gate_out, 0)
    grad_pqkv, grad_pab, grad_taps, grad_small, grad_gain = core_backward(grad_n, pqkv, pab, kept, taps, rate, bias)
    grad_pqkv, grad_pair = hold((grad_pqkv, grad_pair))
    out_rows, grad_pqkv = scatter_direct(out_part, grad_pqkv)
    grad_pqkv, sent = hold((grad_pqkv, dot(normed_there, grad_pqkv, TN).astype(BF16)))
    got = sibling(sent)
    part_qkv = (dot(normed_here, grad_pqkv, TN) + got.astype(F32)).astype(BF16)
    grad_pqkv, grad_pab, grad_taps, part_qkv = hold((grad_pqkv, grad_pab, grad_taps, part_qkv))
    grad_qkv = scatter_chips(part_qkv, 0)
    low_pab = grad_pab.astype(BF16)
    grad_normed, gain_sum = projections_back(grad_pqkv, grad_po, low_pab, full_qkv, full_gate_out, full_narrow, normed)
    mix_gain_part = gain_sum[0] / mix_gain
    grad_narrow = dot(low_pab, normed, TN)
    roll = lambda a: jnp.swapaxes(a.reshape(a.shape[0], dp, -1), 0, 1)
    grad_kernels = jnp.concatenate(
        [roll(grad_taps[:, :keys]), roll(grad_taps[:, keys : 2 * keys]), roll(grad_taps[:, 2 * keys :])], 2
    )
    pad3 = lambda a: jnp.pad(a, ((0, 0), (0, 0), (0, wide - a.shape[2])))
    few_parts = jnp.concatenate([pad3(roll(grad_narrow)), pad3(grad_kernels)], 1)
    few_grads = jnp.sum(lax.all_to_all(few_parts, "dp", 0, 0, tiled=True), 0)
    grad_narrow = few_grads[: 2 * heads, : narrow.shape[1]].T
    grad_kernels = few_grads[2 * heads :, : kernels.shape[1]]

    place = lambda a: lax.dynamic_update_slice_in_dim(jnp.zeros_like(log_rate), a, first_head, 0)
    gains = jnp.concatenate(
        [
            mix_gain_part,
            ffn_gain_part,
            grad_gain[0] / head_gain,
            place(grad_small[0, :heads]),
            place(grad_small[0, heads:]),
        ]
    )
    grad_normed, grad_pair, grad_w_down, grad_gate_out, out_rows, gains = hold(
        (grad_normed, grad_pair, grad_w_down, grad_gate_out, out_rows, gains)
    )
    hidden_out = (middle + out_rows).astype(BF16)
    grad_mix_norm, gains = scatter_rows(reorder(grad_normed), sum_along(gains, "dp"))
    sums = sum_along(gains, "tensor")
    grad_rows, _ = norm_back(rows_in, mix_gain, grad_mix_norm)
    grad_in = (grad_middle + grad_rows).astype(BF16)
    ends = [model, 2 * model, 2 * model + head_gain.shape[0], 2 * model + head_gain.shape[0] + log_rate.shape[0]]
    grad_mix_gain, grad_ffn_gain, grad_head_gain, grad_log_rate, grad_decay_bias = jnp.split(sums, ends)
    grad_qkv, grad_gate_out, grad_pair = grad_qkv.astype(F32), grad_gate_out.astype(F32), grad_pair.astype(F32)
    return (
        hidden_out,
        grad_in,
        grad_mix_gain,
        grad_qkv[:, :keys],
        grad_qkv[:, keys : 2 * keys],
        grad_qkv[:, 2 * keys :],
        grad_kernels[:, : cut[0]],
        grad_kernels[:, cut[0] : cut[1]],
        grad_kernels[:, cut[1] :],
        grad_narrow[:, :heads],
        grad_narrow[:, heads:],
        grad_log_rate,
        grad_decay_bias,
        grad_gate_out[:, :vals],
        grad_head_gain,
        grad_gate_out[:, vals:].T,
        grad_ffn_gain,
        grad_pair[:, :hidden],
        grad_pair[:, hidden:],
        grad_w_down.astype(F32),
    )


def solution(mesh):
    rows, both, flat = P(("dp", "tensor"), None), P("dp", "tensor"), P(None, ("tensor", "dp"))
    turned = P("tensor", "dp")
    return jax.shard_map(
        local,
        mesh=mesh,
        in_specs=(
            *(rows, rows, P()),
            *(both, both, both, flat, flat, flat, both, both),
            *(P(), P(), both, P(), turned, P(), both, both, turned),
        ),
        out_specs=(
            *(rows, rows, P()),
            *(both, both, both, flat, flat, flat, both, both),
            *(P(), P(), both, P(), turned, P(), both, both, turned),
        ),
        check_vma=False,
    )
```

```python
import jax
import jax.numpy as jnp
from jax import lax
from jax.experimental import pallas as pl
from jax.experimental.pallas import tpu as pltpu
from jax.sharding import PartitionSpec as P

GROUP = 64
TAIL = 8
F32 = jnp.float32
BF16 = jnp.bfloat16
HIGHEST = lax.Precision.HIGHEST


def mm(a, b, dims=((1,), (0,))):
    return lax.dot_general(a.astype(BF16), b.astype(BF16), (dims, ((), ())), preferred_element_type=F32)


NN = ((1,), (0,))
NT = ((1,), (1,))
TN = ((0,), (0,))


def mm_exact(a, b, dims=NN):
    return lax.dot_general(a, b, (dims, ((), ())), precision=HIGHEST, preferred_element_type=F32)


def halves(a):
    high = a.astype(BF16)
    return high, (a - high.astype(F32)).astype(BF16)


def mm_split(a, b, dims=NN):
    a_high, a_low = halves(a)
    b_high, b_low = halves(b)
    return mm(a_high, b_high, dims) + (mm(a_high, b_low, dims) + mm(a_low, b_high, dims))


def sigmoid(x):
    return 1.0 / (1.0 + jnp.exp(-x))


def softplus(x):
    return jnp.maximum(x, 0.0) + jnp.log1p(jnp.exp(-jnp.abs(x)))


def grid_iota(size):
    return (
        lax.broadcasted_iota(jnp.int32, (size, size), 0),
        lax.broadcasted_iota(jnp.int32, (size, size), 1),
    )


def unit_lower_inverses(lowers, row, col):
    size = lowers[0].shape[0]
    base = 16
    eye = jnp.where(row == col, 1.0, 0.0)
    powers = [jnp.where(row // base == col // base, -lower, 0.0) for lower in lowers]
    inverses = [eye + power for power in powers]
    reach = 2
    while reach < base:
        powers = [mm_split(power, power) for power in powers]
        inverses = [inverse + mm_split(inverse, power) for inverse, power in zip(inverses, powers)]
        reach *= 2
    while base < size:
        wide = 2 * base
        off = (row // wide == col // wide) & (row // base > col // base)
        right = [mm_split(jnp.where(off, lower, 0.0), inverse) for lower, inverse in zip(lowers, inverses)]
        inverses = [inverse - mm_split(inverse, r) for inverse, r in zip(inverses, right)]
        base = wide
    return inverses


def gates(p_ab, rate, bias, heads):
    pre = p_ab[:, :heads] + bias
    return sigmoid(p_ab[:, heads:]), -jnp.exp(rate) * softplus(pre), pre


def forward_kernel(
    pqkv, pab, taps, rate, bias,
    n_out, norm_out, conved, u_out, s_out, t_out,
    ext, state,
):
    heads = rate.shape[1]
    vals = n_out.shape[1]
    keys = (pqkv.shape[1] - vals) // 2
    dk, dv = keys // heads, vals // heads

    @pl.when(pl.program_id(0) == 0)
    def _():
        ext[...] = jnp.zeros_like(ext)
        state[...] = jnp.zeros_like(state)

    ext[TAIL:, :] = pqkv[...]
    n_taps = taps.shape[0]
    total = None
    for i in range(n_taps):
        start = TAIL - (n_taps - 1) + i
        term = ext[start : start + GROUP, :] * taps[i : i + 1, :]
        total = term if total is None else total + term
    conved[...] = total
    ext[:TAIL, :] = ext[GROUP:, :]

    row, col = grid_iota(GROUP)
    tri = jnp.where(row >= col, 1.0, 0.0)
    beta, log_decay, _ = gates(pab[...], rate[...], bias[...], heads)
    c_col = mm_exact(tri, log_decay)
    c_row = mm_exact(log_decay, jnp.where(row <= col, 1.0, 0.0), TN)
    start_decay = jnp.exp(c_col)
    end_decay = jnp.exp(c_col[GROUP - 1 :, :] - c_col)
    last_decay = jnp.exp(c_col[GROUP - 1 :, :])

    qs, ks, vs, bs, prods, relatives, lowers = [], [], [], [], [], [], []
    for h in range(heads):
        uq = conved[:, h * dk : (h + 1) * dk]
        uk = conved[:, keys + h * dk : keys + (h + 1) * dk]
        uv = conved[:, 2 * keys + h * dv : 2 * keys + (h + 1) * dv]
        q = uq * sigmoid(uq)
        qs.append(q * (lax.rsqrt(jnp.sum(q * q, -1, keepdims=True) + 1e-6) * dk**-0.5))
        k = uk * sigmoid(uk)
        ks.append(k * lax.rsqrt(jnp.sum(k * k, -1, keepdims=True) + 1e-6))
        vs.append(uv * sigmoid(uv))
        bs.append(beta[:, h : h + 1])
    for h in range(heads):
        prods.append(mm_split(jnp.concatenate([ks[h], qs[h]], 0), ks[h], NT))
    for h in range(heads):
        differ = jnp.minimum(c_col[:, h : h + 1] - c_row[h : h + 1, :], 0.0)
        relatives.append(jnp.where(row >= col, jnp.exp(differ), 0.0))
        lowers.append(jnp.where(row > col, bs[h] * relatives[h] * prods[h][:GROUP], 0.0))
    invs = [inverse for inverse in unit_lower_inverses(lowers, row, col)]
    states = [state[h] for h in range(heads)]
    lows = states
    reads = []
    for h in range(heads):
        e = start_decay[:, h : h + 1]
        reads.append(mm_split(jnp.concatenate([ks[h] * e, qs[h] * e], 0), lows[h]))
    us = [mm_split(invs[h], bs[h] * (vs[h] - reads[h][:GROUP])) for h in range(heads)]
    outs = [reads[h][GROUP:] + mm_split(relatives[h] * prods[h][GROUP:], us[h]) for h in range(heads)]
    nexts = [
        last_decay[:, h : h + 1] * states[h] + mm_split(ks[h] * end_decay[:, h : h + 1], us[h], TN) for h in range(heads)
    ]
    for h in range(heads):
        cols = slice(h * dv, (h + 1) * dv)
        state[h] = nexts[h]
        t_out[0, h] = invs[h].astype(t_out.dtype)
        s_out[0, h] = lows[h].astype(s_out.dtype)
        u_out[:, cols] = us[h].astype(u_out.dtype)
        o = outs[h]
        norm = lax.rsqrt(jnp.mean(o * o, -1, keepdims=True) + 1e-5)
        n_out[:, cols] = (o * norm).astype(n_out.dtype)
        norm_out[:, h : h + 1] = norm


def core_forward(pqkv, pab, taps, rate, bias, keys):
    rows, width = pqkv.shape
    vals = width - 2 * keys
    heads = rate.shape[1]
    dk, dv = keys // heads, vals // heads
    blocks = rows // GROUP
    tokens = lambda width: pl.BlockSpec((GROUP, width), lambda n: (n, 0))
    fixed = lambda a: pl.BlockSpec(a.shape, lambda n: (0, 0))
    return pl.pallas_call(
        forward_kernel,
        grid=(blocks,),
        in_specs=[tokens(a.shape[1]) for a in (pqkv, pab)] + [fixed(a) for a in (taps, rate, bias)],
        out_specs=[
            tokens(vals),
            tokens(heads),
            tokens(width),
            tokens(vals),
            pl.BlockSpec((1, heads, dk, dv), lambda n: (n, 0, 0, 0)),
            pl.BlockSpec((1, heads, GROUP, GROUP), lambda n: (n, 0, 0, 0)),
        ],
        out_shape=[
            jax.ShapeDtypeStruct((rows, vals), BF16),
            jax.ShapeDtypeStruct((rows, heads), F32),
            jax.ShapeDtypeStruct((rows, width), F32),
            jax.ShapeDtypeStruct((rows, vals), BF16),
            jax.ShapeDtypeStruct((blocks, heads, dk, dv), BF16),
            jax.ShapeDtypeStruct((blocks, heads, GROUP, GROUP), BF16),
        ],
        scratch_shapes=[
            pltpu.VMEM((GROUP + TAIL, 2 * keys + vals), F32),
            pltpu.VMEM((heads, dk, dv), F32),
        ],
        compiler_params=pltpu.CompilerParams(dimension_semantics=("arbitrary",), vmem_limit_bytes=40 * 2**20),
        cost_estimate=pl.CostEstimate(flops=8 * 10**9, bytes_accessed=32 * 2**20, transcendentals=10**7),
        name="core_forward",
    )(pqkv, pab, taps, rate, bias)


def backward_kernel(
    dn_in, pqkv, pab, n_in, norm_in, conved, u_in, s_in, t_in, taps, rate, bias,
    dpqkv, dpab, dtaps, dsmall, dgain,
    ext, dstate,
):
    heads = rate.shape[1]
    vals = dn_in.shape[1]
    keys = (pqkv.shape[1] - vals) // 2
    dk, dv = keys // heads, vals // heads

    @pl.when(pl.program_id(0) == 0)
    def _():
        ext[...] = jnp.zeros_like(ext)
        dstate[...] = jnp.zeros_like(dstate)
        for ref in (dtaps, dsmall, dgain):
            ref[...] = jnp.zeros_like(ref)

    row, col = grid_iota(GROUP)
    tri = jnp.where(row >= col, 1.0, 0.0)
    upper = jnp.where(row <= col, 1.0, 0.0)
    beta, log_decay, pre = gates(pab[...], rate[...], bias[...], heads)
    c_col = mm_exact(tri, log_decay)
    c_row = mm_exact(log_decay, upper, TN)
    start_decay = jnp.exp(c_col)
    end_decay = jnp.exp(c_col[GROUP - 1 :, :] - c_col)
    last_decay = jnp.exp(c_col[GROUP - 1 :, :])
    lane = lax.broadcasted_iota(jnp.int32, (1, heads), 1)
    d_beta = jnp.zeros((GROUP, heads), F32)
    after = jnp.zeros((GROUP, heads), F32)
    before = jnp.zeros((GROUP, heads), F32)
    d_log = jnp.zeros((GROUP, heads), F32)
    gain_sum = jnp.zeros((1, dv), F32)

    for h in range(heads):
        ks, vs = slice(h * dk, (h + 1) * dk), slice(h * dv, (h + 1) * dv)
        kx, vx = slice(keys + h * dk, keys + (h + 1) * dk), slice(2 * keys + h * dv, 2 * keys + (h + 1) * dv)
        here = lane == h
        uq, uk, uv = conved[:, ks], conved[:, kx], conved[:, vx]
        sq, sk, sv = sigmoid(uq), sigmoid(uk), sigmoid(uv)
        q = uq * sq
        q_norm = lax.rsqrt(jnp.sum(q * q, -1, keepdims=True) + 1e-6)
        q = q * q_norm
        k = uk * sk
        k_norm = lax.rsqrt(jnp.sum(k * k, -1, keepdims=True) + 1e-6)
        k = k * k_norm
        v = uv * sv
        qs = q * dk**-0.5
        b = beta[:, h : h + 1]
        e = start_decay[:, h : h + 1]
        f = end_decay[:, h : h + 1]
        kb = k.astype(BF16)
        qb = qs.astype(BF16)

        n = n_in[:, vs].astype(F32)
        dn = dn_in[:, vs]
        dnn = dn * n
        gain_sum = gain_sum + jnp.sum(dnn, 0, keepdims=True)
        do = norm_in[:, h : h + 1] * (dn - n * jnp.mean(dnn, -1, keepdims=True))

        prod = mm(jnp.concatenate([kb, qb], 0), kb, NT)
        relative = jnp.where(row >= col, jnp.exp(jnp.minimum(c_col[:, h : h + 1] - c_row[h : h + 1, :], 0.0)), 0.0)
        kk, qk = prod[:GROUP], prod[GROUP:]
        strict = jnp.where(row > col, relative, 0.0)
        mix = relative * qk
        s_prev = s_in[0, h]
        u = u_in[:, vs]
        inv = t_in[0, h]
        ds = dstate[h]
        ds_low = ds.astype(BF16)
        dob = do.astype(BF16)
        ke, qe, kd = k * e, qs * e, k * f
        du = mm_split(mix, do, TN) + mm_split(kd, ds)
        du_hi, du_lo = halves(du)
        dr = mm(inv, du_hi, TN) + mm(inv, du_lo, TN)
        pair = jnp.concatenate([dob, dr.astype(BF16)], 0)
        dstate[h] = last_decay[:, h : h + 1] * ds + mm(jnp.concatenate([qe, -(b * ke)], 0), pair, TN)
        rest = jnp.concatenate([halves(do)[1], halves(dr)[1]], 0)
        cross = mm(pair, u, NT) + mm(rest, u, NT)
        dmix = jnp.where(row >= col, cross[:GROUP], 0.0)
        dlow = jnp.where(row > col, -cross[GROUP:], 0.0)
        back = mm(pair, s_prev, NT) + mm(rest, s_prev, NT)
        dqe, x = back[:GROUP], back[GROUP:]
        dkd = mm(u, ds_low, NT)
        dke = -(b * x)
        rk = strict * kk
        d_beta = d_beta + jnp.where(
            here,
            jnp.sum(dr * v, -1, keepdims=True) - jnp.sum(x * ke, -1, keepdims=True) + jnp.sum(dlow * rk, -1, keepdims=True),
            0.0,
        )
        dpair = dlow * (b * rk) + dmix * mix
        spread = mm(upper, dpair)
        last_part = last_decay[:, h : h + 1] * jnp.sum(ds * s_prev.astype(F32), keepdims=True)
        d_log = d_log + jnp.where(here, jnp.sum(jnp.where(row > col, spread, 0.0), -1, keepdims=True) + last_part, 0.0)
        after = after + jnp.where(here, jnp.sum(dqe * qe + dke * ke, -1, keepdims=True), 0.0)
        before = before + jnp.where(here, jnp.sum(dkd * kd, -1, keepdims=True), 0.0)
        dqk = dmix * relative
        dkk = dlow * (b * strict)
        first = mm(jnp.concatenate([dqk, dkk], 0), kb)
        dq = e * dqe + first[:GROUP]
        dk_ = e * dke + f * dkd + first[GROUP:] + mm(jnp.concatenate([dkk, dqk], 0), jnp.concatenate([kb, qb], 0), TN)
        dq = dq * dk**-0.5
        dq = q_norm * (dq - q * jnp.sum(dq * q, -1, keepdims=True))
        dk_ = k_norm * (dk_ - k * jnp.sum(dk_ * k, -1, keepdims=True))
        ext[:GROUP, ks] = dq * (sq * (1.0 + uq * (1.0 - sq)))
        ext[:GROUP, kx] = dk_ * (sk * (1.0 + uk * (1.0 - sk)))
        ext[:GROUP, vx] = (b * dr) * (sv * (1.0 + uv * (1.0 - sv)))

    d_log = d_log + mm_exact(upper, after) + mm_exact(jnp.where(row > col, 1.0, 0.0), before)
    d_pre = d_log * (-jnp.exp(rate[...])) * sigmoid(pre)
    dpab[:, :heads] = d_pre
    dpab[:, heads:] = d_beta * beta * (1.0 - beta)
    dsmall[0:1, :heads] += jnp.sum(d_log * log_decay, 0, keepdims=True)
    dsmall[0:1, heads:] += jnp.sum(d_pre, 0, keepdims=True)
    dgain[...] += gain_sum

    n_taps = taps.shape[0]
    rows_in = pqkv[...]
    total = None
    for i in range(n_taps):
        start = n_taps - 1 - i
        piece = ext[start : start + GROUP, :]
        term = piece * taps[i : i + 1, :]
        total = term if total is None else total + term
        dtaps[i : i + 1, :] += jnp.sum(piece * rows_in, 0, keepdims=True)
    dpqkv[...] = total.astype(dpqkv.dtype)
    ext[GROUP:, :] = ext[:TAIL, :]


def core_backward(dn, pqkv, pab, kept, taps, rate, bias):
    n_in, norm_in, conved, u_in, s_in, t_in = kept
    rows, width = pqkv.shape
    vals = dn.shape[1]
    keys = (width - vals) // 2
    heads = rate.shape[1]
    dk, dv = keys // heads, vals // heads
    blocks = rows // GROUP
    tokens = lambda width: pl.BlockSpec((GROUP, width), lambda n: (blocks - 1 - n, 0))
    stacked = lambda a: pl.BlockSpec((1,) + a.shape[1:], lambda n: (blocks - 1 - n, 0, 0, 0))
    fixed = lambda shape: pl.BlockSpec(shape, lambda n: (0, 0))
    small = (1, 2 * heads)
    return pl.pallas_call(
        backward_kernel,
        grid=(blocks,),
        in_specs=[tokens(a.shape[1]) for a in (dn, pqkv, pab, n_in, norm_in, conved, u_in)]
        + [stacked(s_in), stacked(t_in)]
        + [fixed(a.shape) for a in (taps, rate, bias)],
        out_specs=[tokens(a.shape[1]) for a in (pqkv, pab)]
        + [fixed(taps.shape), fixed(small), fixed((1, dv))],
        out_shape=[jax.ShapeDtypeStruct(pqkv.shape, BF16), jax.ShapeDtypeStruct(pab.shape, F32)]
        + [jax.ShapeDtypeStruct(s, F32) for s in (taps.shape, small, (1, dv))],
        scratch_shapes=[
            pltpu.VMEM((GROUP + TAIL, 2 * keys + vals), F32),
            pltpu.VMEM((heads, dk, dv), F32),
        ],
        compiler_params=pltpu.CompilerParams(dimension_semantics=("arbitrary",), vmem_limit_bytes=40 * 2**20),
        cost_estimate=pl.CostEstimate(flops=20 * 10**9, bytes_accessed=48 * 2**20, transcendentals=10**7),
        name="core_backward",
    )(dn, pqkv, pab, n_in, norm_in, conved, u_in, s_in, t_in, taps, rate, bias)


def projections_kernel(dqkv, dpo, dab, w_qkv, w_out, w_ab, normed, out, sums):
    grad = (
        mm(dqkv[...], w_qkv[...], NT)
        + mm(dpo[...], w_out[...], NT)
        + mm(dab[...], w_ab[...])
    )
    out[...] = grad.astype(out.dtype)
    sums[...] = jnp.sum(grad * normed[...].astype(F32), 0, keepdims=True)


def projections_back(dqkv, dpo, dab, w_qkv, w_out, w_ab, normed):
    rows, model = normed.shape
    tile = 256
    whole = lambda a: pl.BlockSpec(a.shape, lambda n: (0, 0), pipeline_mode=pl.Buffered(1))
    return pl.pallas_call(
        projections_kernel,
        grid=(model // tile,),
        in_specs=[
            whole(dqkv),
            whole(dpo),
            whole(dab),
            pl.BlockSpec((tile, dqkv.shape[1]), lambda n: (n, 0)),
            pl.BlockSpec((tile, dpo.shape[1]), lambda n: (n, 0)),
            pl.BlockSpec((dab.shape[1], tile), lambda n: (0, n)),
            pl.BlockSpec((rows, tile), lambda n: (0, n)),
        ],
        out_specs=[pl.BlockSpec((rows, tile), lambda n: (0, n)), pl.BlockSpec((1, tile), lambda n: (0, n))],
        out_shape=[jax.ShapeDtypeStruct((rows, model), BF16), jax.ShapeDtypeStruct((1, model), F32)],
        compiler_params=pltpu.CompilerParams(dimension_semantics=("arbitrary",), vmem_limit_bytes=40 * 2**20),
        cost_estimate=pl.CostEstimate(
            flops=2 * rows * model * (dqkv.shape[1] + dpo.shape[1]), bytes_accessed=32 * 2**20, transcendentals=0
        ),
        name="projections_back",
    )(dqkv, dpo, dab, w_qkv, w_out, w_ab, normed)


def side_by_side_kernel(*refs):
    *parts, out = refs
    at = 0
    for part in parts:
        out[:, at : at + part.shape[1]] = part[...].astype(out.dtype)
        at += part.shape[1]


def side_by_side(*parts):
    rows = parts[0].shape[0]
    step = rows // 4
    width = sum(a.shape[1] for a in parts)
    band = lambda columns: pl.BlockSpec((step, columns), lambda n: (n, 0))
    return pl.pallas_call(
        side_by_side_kernel,
        grid=(4,),
        in_specs=[band(a.shape[1]) for a in parts],
        out_specs=band(width),
        out_shape=jax.ShapeDtypeStruct((rows, width), BF16),
        name="side_by_side",
    )(*parts)


def apart_kernel(whole, *outs):
    at = 0
    for out in outs:
        out[...] = whole[:, at : at + out.shape[1]].astype(out.dtype)
        at += out.shape[1]


def apart(whole, *widths):
    rows = whole.shape[0]
    step = rows // 4
    band = lambda columns: pl.BlockSpec((step, columns), lambda n: (n, 0))
    return pl.pallas_call(
        apart_kernel,
        grid=(4,),
        in_specs=[band(whole.shape[1])],
        out_specs=[band(width) for width in widths],
        out_shape=[jax.ShapeDtypeStruct((rows, width), F32) for width in widths],
        name="apart",
    )(whole)


def rms_norm(values, gain_vec):
    return values * lax.rsqrt(jnp.mean(values * values, -1, keepdims=True) + 1e-05) * gain_vec


def dot(a, b, dims=NN):
    return lax.dot_general(a, b, (dims, ((), ())), preferred_element_type=F32)


def swap(piece, mask):
    return lax.ppermute(piece, "tensor", [(i, i ^ mask) for i in range(4)])


def gather_rows(own, beside=None):
    if lax.axis_size("tensor") != 4:
        full = lax.all_gather(own, "tensor", axis=0, tiled=True)
        return full if beside is None else (full, beside)
    half = own.shape[0] // 2
    first, second = swap(own, 1), swap(own, 2)
    if beside is not None:
        first, second, beside = lax.optimization_barrier((first, second, beside))
    full = jnp.concatenate([own, first, second, swap(second[:half], 1), swap(first[half:], 2)], 0)
    return full if beside is None else (full, beside)


def scatter_rows(part, beside=None):
    if lax.axis_size("tensor") != 4:
        total = lax.psum_scatter(part, "tensor", scatter_dimension=0, tiled=True).astype(F32)
        return total if beside is None else (total, beside)
    rows, half = part.shape[0] // 4, part.shape[1] // 2

    def chunk(k, columns):
        return part[k * rows : (k + 1) * rows, columns]

    plans = ((slice(0, half), 1, 2), (slice(half, 2 * half), 2, 1))
    arrived = [swap(jnp.concatenate([chunk(one, columns), chunk(3, columns)], 0), one) for columns, one, _ in plans]
    if beside is not None:
        arrived, beside = lax.optimization_barrier((arrived, beside))
    owns, passed = [], []
    for (columns, _, two), got in zip(plans, arrived):
        got = got.astype(F32)
        owns.append(chunk(0, columns).astype(F32) + got[:rows])
        passed.append((chunk(two, columns).astype(F32) + got[rows:]).astype(BF16))
    passed = lax.optimization_barrier(passed)
    sums = [own + swap(piece, two).astype(F32) for own, piece, (_, _, two) in zip(owns, passed, plans)]
    total = jnp.concatenate(sums, 1)
    return total if beside is None else (total, beside)


def scatter_direct(part, beside):
    if lax.axis_size("tensor") != 4:
        return lax.psum_scatter(part, "tensor", scatter_dimension=0, tiled=True).astype(F32), beside
    chunks = jnp.split(part, 4)
    arrived, beside = lax.optimization_barrier(([swap(chunks[k], k) for k in range(1, 4)], beside))
    return sum((piece.astype(F32) for piece in arrived), chunks[0].astype(F32)), beside


def sum_along(values, axis):
    size = lax.axis_size(axis)
    if size & (size - 1):
        return lax.psum(values, axis)
    mask = 1
    while mask < size:
        values = values + lax.ppermute(values, axis, [(i, i ^ mask) for i in range(size)])
        mask *= 2
    return values


def reorder(rows_in):
    if lax.axis_size("tensor") != 4:
        return rows_in
    rows = rows_in.shape[0] // 4
    me = lax.axis_index("tensor")
    return jnp.concatenate([lax.dynamic_slice_in_dim(rows_in, (me ^ k) * rows, rows, 0) for k in range(4)], 0)


def norm_back(values, gain_vec, grad):
    factor = lax.rsqrt(jnp.mean(values * values, -1, keepdims=True) + 1e-05)
    normal = values * factor
    scaled = grad * gain_vec
    return (
        factor * (scaled - normal * jnp.mean(scaled * normal, -1, keepdims=True)),
        jnp.sum(grad * normal, 0),
    )


def gather_dp(shard, axis):
    return lax.all_gather(shard.astype(BF16), "dp", axis=axis, tiled=True)


def sibling(piece):
    return lax.ppermute(piece, "dp", [(i, i ^ 1) for i in range(lax.axis_size("dp"))])


def split_blocks(full):
    size = lax.axis_size("dp")
    width = full.shape[1] // size
    core = lax.axis_index("dp") % 2

    def pick(c):
        return jnp.concatenate(
            [lax.dynamic_slice_in_dim(full, (2 * i + c) * width, width, 1) for i in range(size // 2)], 1
        )

    return pick(core), pick(1 - core)


def scatter_chips(part, axis):
    size = lax.axis_size("dp")
    groups = [list(range(core, size, 2)) for core in range(2)]
    return lax.psum_scatter(part, "dp", scatter_dimension=axis, tiled=True, axis_index_groups=groups)


def local(
    hidden_in,
    grad_out,
    mix_gain,
    w_query,
    w_key,
    w_value,
    conv_query,
    conv_key,
    conv_value,
    w_decay,
    w_beta,
    log_rate,
    decay_bias,
    w_outgate,
    head_gain,
    w_output,
    ffn_gain,
    w_gate,
    w_up,
    w_down,
):
    dp = lax.axis_size("dp")
    model = hidden_in.shape[1]
    keys, vals, hidden = w_query.shape[1], w_value.shape[1], w_gate.shape[1]
    heads = w_decay.shape[1]
    first_head = lax.axis_index("tensor") * heads
    rate = lax.dynamic_slice_in_dim(log_rate, first_head, heads)[None]
    bias = lax.dynamic_slice_in_dim(decay_bias, first_head, heads)[None]
    gain = jnp.tile(head_gain, heads)

    narrow = jnp.concatenate([w_decay, w_beta], 1).T
    kernels = jnp.concatenate([conv_query, conv_key, conv_value], 1)
    wide = max(narrow.shape[1], kernels.shape[1])
    pad = lambda a: jnp.pad(a, ((0, 0), (0, wide - a.shape[1])))
    few = lax.all_gather(jnp.concatenate([pad(narrow), pad(kernels)], 0).astype(BF16), "dp")
    unroll = lambda a: jnp.swapaxes(a, 0, 1).reshape(a.shape[1], -1)
    full_narrow = unroll(few[:, : 2 * heads, : narrow.shape[1]])
    pieces = few[:, 2 * heads :, : kernels.shape[1]]
    cut = (conv_query.shape[1], conv_query.shape[1] + conv_key.shape[1])
    taps = jnp.concatenate(
        [unroll(pieces[:, :, : cut[0]]), unroll(pieces[:, :, cut[0] : cut[1]]), unroll(pieces[:, :, cut[1] :])], 1
    ).astype(F32)

    full_qkv = gather_dp(side_by_side(w_query, w_key, w_value), 0)
    full_gate_out = gather_dp(jnp.concatenate([w_outgate, w_output.T], 1), 0)
    full_outgate, full_output = full_gate_out[:, :vals], full_gate_out[:, vals:]
    full_pair = gather_dp(jnp.concatenate([w_gate, w_up], 1), 0)
    full_down = gather_dp(w_down, 1)

    hold = lax.optimization_barrier
    rows_in = hidden_in.astype(F32)
    normed = reorder(gather_rows(rms_norm(rows_in, mix_gain).astype(BF16)))
    cot_own, _ = hold((grad_out, normed))
    cot = gather_rows(cot_own)
    pqkv = dot(normed, full_qkv)
    pab = dot(normed, full_narrow, NT)
    pqkv, cot, normed_here, normed_there = hold((pqkv, cot, *split_blocks(normed)))
    kept = core_forward(pqkv, pab, taps, rate, bias, keys)
    po = dot(normed, full_outgate)
    po_sig = jax.nn.sigmoid(po)
    mixed = (kept[0].astype(F32) * gain * (po * po_sig)).astype(BF16)
    middle = rows_in + scatter_rows(reorder(dot(mixed, full_output, NT).astype(BF16)))

    ffn_rows = gather_rows(rms_norm(middle, ffn_gain).astype(BF16))
    pre = dot(ffn_rows, full_pair)
    gate_pre, up_pre = pre[:, :hidden], pre[:, hidden:]
    gate_sig = jax.nn.sigmoid(gate_pre)
    activ = (gate_pre * gate_sig * up_pre).astype(BF16)
    cot, part_down = hold((cot, dot(activ, cot, TN).astype(BF16)))
    grad_w_down = lax.psum_scatter(part_down, "dp", scatter_dimension=1, tiled=True)
    grad_activ = dot(cot, full_down, NT)
    grad_gate_pre = (grad_activ * up_pre * gate_sig * (1.0 + gate_pre * (1.0 - gate_sig))).astype(BF16)
    grad_up_pre = (grad_activ * (gate_pre * gate_sig)).astype(BF16)
    grad_pre = jnp.concatenate([grad_gate_pre, grad_up_pre], 1)
    ffn_here, ffn_there = split_blocks(ffn_rows)
    grad_pre, sent = hold((grad_pre, dot(ffn_there, grad_pre, TN).astype(BF16)))
    got = sibling(sent)
    grad_ffn_rows, got = hold((dot(grad_pre, full_pair, NT).astype(BF16), got))
    part_pair = (dot(ffn_here, grad_pre, TN) + got.astype(F32)).astype(BF16)
    grad_ffn_norm, part_pair = scatter_rows(grad_ffn_rows, part_pair)
    grad_pair = scatter_chips(part_pair, 0)
    grad_middle_norm, ffn_gain_part = norm_back(middle, ffn_gain, grad_ffn_norm)
    grad_middle = grad_out.astype(F32) + grad_middle_norm

    activ_late, mix_low = hold((activ, grad_middle.astype(BF16)))
    mix_cot, out_part = gather_rows(mix_low, dot(activ_late, full_down).astype(BF16))
    mix_cot = reorder(mix_cot)
    mix_here, mix_there = split_blocks(mix_cot)
    mix_cot, sent_output = hold((mix_cot, dot(mix_there, mixed, TN).astype(BF16)))
    grad_mixed = dot(mix_cot, full_output)
    grad_po = grad_mixed * kept[0].astype(F32) * gain * (po_sig * (1.0 + po * (1.0 - po_sig)))
    grad_po = grad_po.astype(BF16)
    grad_n = grad_mixed * gain * (po * po_sig)
    sent_outgate = dot(normed_there, grad_po, TN).astype(BF16)
    got_output, got_outgate = sibling(sent_output), sibling(sent_outgate)
    part_output = (dot(mix_here, mixed, TN) + got_output.astype(F32)).astype(BF16)
    part_outgate = (dot(normed_here, grad_po, TN) + got_outgate.astype(F32)).astype(BF16)
    part_gate_out = jnp.concatenate([part_outgate, part_output], 1)
    grad_n, grad_w_down, part_gate_out = hold((grad_n, grad_w_down, part_gate_out))
    grad_gate_out = scatter_chips(part_gate_out, 0)
    grad_pqkv, grad_pab, grad_taps, grad_small, grad_gain = core_backward(grad_n, pqkv, pab, kept, taps, rate, bias)
    grad_pqkv, grad_pair = hold((grad_pqkv, grad_pair))
    out_rows, grad_pqkv = scatter_direct(out_part, grad_pqkv)
    grad_pqkv, sent = hold((grad_pqkv, dot(normed_there, grad_pqkv, TN).astype(BF16)))
    got = sibling(sent)
    part_qkv = (dot(normed_here, grad_pqkv, TN) + got.astype(F32)).astype(BF16)
    grad_pqkv, grad_pab, grad_taps, part_qkv = hold((grad_pqkv, grad_pab, grad_taps, part_qkv))
    grad_qkv = scatter_chips(part_qkv, 0)
    low_pab = grad_pab.astype(BF16)
    grad_normed, gain_sum = projections_back(grad_pqkv, grad_po, low_pab, full_qkv, full_gate_out, full_narrow, normed)
    mix_gain_part = gain_sum[0] / mix_gain
    grad_narrow = dot(low_pab, normed, TN)
    roll = lambda a: jnp.swapaxes(a.reshape(a.shape[0], dp, -1), 0, 1)
    grad_kernels = jnp.concatenate(
        [roll(grad_taps[:, :keys]), roll(grad_taps[:, keys : 2 * keys]), roll(grad_taps[:, 2 * keys :])], 2
    )
    pad3 = lambda a: jnp.pad(a, ((0, 0), (0, 0), (0, wide - a.shape[2])))
    few_parts = jnp.concatenate([pad3(roll(grad_narrow)), pad3(grad_kernels)], 1)
    few_grads = jnp.sum(lax.all_to_all(few_parts, "dp", 0, 0, tiled=True), 0)
    grad_narrow = few_grads[: 2 * heads, : narrow.shape[1]].T
    grad_kernels = few_grads[2 * heads :, : kernels.shape[1]]

    place = lambda a: lax.dynamic_update_slice_in_dim(jnp.zeros_like(log_rate), a, first_head, 0)
    gains = jnp.concatenate(
        [
            mix_gain_part,
            ffn_gain_part,
            grad_gain[0] / head_gain,
            place(grad_small[0, :heads]),
            place(grad_small[0, heads:]),
        ]
    )
    grad_normed, grad_pair, grad_w_down, grad_gate_out, out_rows, gains = hold(
        (grad_normed, grad_pair, grad_w_down, grad_gate_out, out_rows, gains)
    )
    hidden_out = (middle + out_rows).astype(BF16)
    grad_mix_norm, gains = scatter_rows(reorder(grad_normed), sum_along(gains, "dp"))
    sums = sum_along(gains, "tensor")
    grad_rows, _ = norm_back(rows_in, mix_gain, grad_mix_norm)
    grad_in = (grad_middle + grad_rows).astype(BF16)
    ends = [model, 2 * model, 2 * model + head_gain.shape[0], 2 * model + head_gain.shape[0] + log_rate.shape[0]]
    grad_mix_gain, grad_ffn_gain, grad_head_gain, grad_log_rate, grad_decay_bias = jnp.split(sums, ends)
    grad_w_query, grad_w_key, grad_w_value = apart(grad_qkv, keys, keys, vals)
    grad_gate_out, grad_pair = grad_gate_out.astype(F32), grad_pair.astype(F32)
    return (
        hidden_out,
        grad_in,
        grad_mix_gain,
        grad_w_query,
        grad_w_key,
        grad_w_value,
        grad_kernels[:, : cut[0]],
        grad_kernels[:, cut[0] : cut[1]],
        grad_kernels[:, cut[1] :],
        grad_narrow[:, :heads],
        grad_narrow[:, heads:],
        grad_log_rate,
        grad_decay_bias,
        grad_gate_out[:, :vals],
        grad_head_gain,
        grad_gate_out[:, vals:].T,
        grad_ffn_gain,
        grad_pair[:, :hidden],
        grad_pair[:, hidden:],
        grad_w_down.astype(F32),
    )


def solution(mesh):
    rows, both, flat = P(("dp", "tensor"), None), P("dp", "tensor"), P(None, ("tensor", "dp"))
    turned = P("tensor", "dp")
    return jax.shard_map(
        local,
        mesh=mesh,
        in_specs=(
            *(rows, rows, P()),
            *(both, both, both, flat, flat, flat, both, both),
            *(P(), P(), both, P(), turned, P(), both, both, turned),
        ),
        out_specs=(
            *(rows, rows, P()),
            *(both, both, both, flat, flat, flat, both, both),
            *(P(), P(), both, P(), turned, P(), both, both, turned),
        ),
        check_vma=False,
    )
```

```python
import jax
import jax.numpy as jnp
from jax import lax
from jax.experimental import pallas as pl
from jax.experimental.pallas import tpu as pltpu
from jax.sharding import PartitionSpec as P

GROUP = 64
TAIL = 8
F32 = jnp.float32
BF16 = jnp.bfloat16
HIGHEST = lax.Precision.HIGHEST


def mm(a, b, dims=((1,), (0,))):
    return lax.dot_general(a.astype(BF16), b.astype(BF16), (dims, ((), ())), preferred_element_type=F32)


NN = ((1,), (0,))
NT = ((1,), (1,))
TN = ((0,), (0,))


def mm_exact(a, b, dims=NN):
    return lax.dot_general(a, b, (dims, ((), ())), precision=HIGHEST, preferred_element_type=F32)


def halves(a):
    high = a.astype(BF16)
    return high, (a - high.astype(F32)).astype(BF16)


def mm_split(a, b, dims=NN):
    a_high, a_low = halves(a)
    b_high, b_low = halves(b)
    return mm(a_high, b_high, dims) + (mm(a_high, b_low, dims) + mm(a_low, b_high, dims))


def sigmoid(x):
    return 1.0 / (1.0 + jnp.exp(-x))


def softplus(x):
    return jnp.maximum(x, 0.0) + jnp.log1p(jnp.exp(-jnp.abs(x)))


def grid_iota(size):
    return (
        lax.broadcasted_iota(jnp.int32, (size, size), 0),
        lax.broadcasted_iota(jnp.int32, (size, size), 1),
    )


def unit_lower_inverses(lowers, row, col):
    size = lowers[0].shape[0]
    base = 16
    eye = jnp.where(row == col, 1.0, 0.0)
    powers = [jnp.where(row // base == col // base, -lower, 0.0) for lower in lowers]
    inverses = [eye + power for power in powers]
    reach = 2
    while reach < base:
        powers = [mm_split(power, power) for power in powers]
        inverses = [inverse + mm_split(inverse, power) for inverse, power in zip(inverses, powers)]
        reach *= 2
    while base < size:
        wide = 2 * base
        off = (row // wide == col // wide) & (row // base > col // base)
        right = [mm_split(jnp.where(off, lower, 0.0), inverse) for lower, inverse in zip(lowers, inverses)]
        inverses = [inverse - mm_split(inverse, r) for inverse, r in zip(inverses, right)]
        base = wide
    return inverses


def gates(p_ab, rate, bias, heads):
    pre = p_ab[:, :heads] + bias
    return sigmoid(p_ab[:, heads:]), -jnp.exp(rate) * softplus(pre), pre


def forward_kernel(
    pqkv, pab, taps, rate, bias,
    n_out, norm_out, conved, u_out, s_out, t_out,
    ext, state,
):
    heads = rate.shape[1]
    vals = n_out.shape[1]
    keys = (pqkv.shape[1] - vals) // 2
    dk, dv = keys // heads, vals // heads

    @pl.when(pl.program_id(0) == 0)
    def _():
        ext[...] = jnp.zeros_like(ext)
        state[...] = jnp.zeros_like(state)

    ext[TAIL:, :] = pqkv[...]
    n_taps = taps.shape[0]
    total = None
    for i in range(n_taps):
        start = TAIL - (n_taps - 1) + i
        term = ext[start : start + GROUP, :] * taps[i : i + 1, :]
        total = term if total is None else total + term
    conved[...] = total
    ext[:TAIL, :] = ext[GROUP:, :]

    row, col = grid_iota(GROUP)
    tri = jnp.where(row >= col, 1.0, 0.0)
    beta, log_decay, _ = gates(pab[...], rate[...], bias[...], heads)
    c_col = mm_exact(tri, log_decay)
    c_row = mm_exact(log_decay, jnp.where(row <= col, 1.0, 0.0), TN)
    start_decay = jnp.exp(c_col)
    end_decay = jnp.exp(c_col[GROUP - 1 :, :] - c_col)
    last_decay = jnp.exp(c_col[GROUP - 1 :, :])

    qs, ks, vs, bs, prods, relatives, lowers = [], [], [], [], [], [], []
    for h in range(heads):
        uq = conved[:, h * dk : (h + 1) * dk]
        uk = conved[:, keys + h * dk : keys + (h + 1) * dk]
        uv = conved[:, 2 * keys + h * dv : 2 * keys + (h + 1) * dv]
        q = uq * sigmoid(uq)
        qs.append(q * (lax.rsqrt(jnp.sum(q * q, -1, keepdims=True) + 1e-6) * dk**-0.5))
        k = uk * sigmoid(uk)
        ks.append(k * lax.rsqrt(jnp.sum(k * k, -1, keepdims=True) + 1e-6))
        vs.append(uv * sigmoid(uv))
        bs.append(beta[:, h : h + 1])
    for h in range(heads):
        prods.append(mm_split(jnp.concatenate([ks[h], qs[h]], 0), ks[h], NT))
    for h in range(heads):
        differ = jnp.minimum(c_col[:, h : h + 1] - c_row[h : h + 1, :], 0.0)
        relatives.append(jnp.where(row >= col, jnp.exp(differ), 0.0))
        lowers.append(jnp.where(row > col, bs[h] * relatives[h] * prods[h][:GROUP], 0.0))
    invs = [inverse for inverse in unit_lower_inverses(lowers, row, col)]
    states = [state[h] for h in range(heads)]
    lows = states
    reads = []
    for h in range(heads):
        e = start_decay[:, h : h + 1]
        reads.append(mm_split(jnp.concatenate([ks[h] * e, qs[h] * e], 0), lows[h]))
    us = [mm_split(invs[h], bs[h] * (vs[h] - reads[h][:GROUP])) for h in range(heads)]
    outs = [reads[h][GROUP:] + mm_split(relatives[h] * prods[h][GROUP:], us[h]) for h in range(heads)]
    nexts = [
        last_decay[:, h : h + 1] * states[h] + mm_split(ks[h] * end_decay[:, h : h + 1], us[h], TN) for h in range(heads)
    ]
    for h in range(heads):
        cols = slice(h * dv, (h + 1) * dv)
        state[h] = nexts[h]
        t_out[0, h] = invs[h].astype(t_out.dtype)
        s_out[0, h] = lows[h].astype(s_out.dtype)
        u_out[:, cols] = us[h].astype(u_out.dtype)
        o = outs[h]
        norm = lax.rsqrt(jnp.mean(o * o, -1, keepdims=True) + 1e-5)
        n_out[:, cols] = (o * norm).astype(n_out.dtype)
        norm_out[:, h : h + 1] = norm


def core_forward(pqkv, pab, taps, rate, bias, keys):
    rows, width = pqkv.shape
    vals = width - 2 * keys
    heads = rate.shape[1]
    dk, dv = keys // heads, vals // heads
    blocks = rows // GROUP
    tokens = lambda width: pl.BlockSpec((GROUP, width), lambda n: (n, 0))
    fixed = lambda a: pl.BlockSpec(a.shape, lambda n: (0, 0))
    return pl.pallas_call(
        forward_kernel,
        grid=(blocks,),
        in_specs=[tokens(a.shape[1]) for a in (pqkv, pab)] + [fixed(a) for a in (taps, rate, bias)],
        out_specs=[
            tokens(vals),
            tokens(heads),
            tokens(width),
            tokens(vals),
            pl.BlockSpec((1, heads, dk, dv), lambda n: (n, 0, 0, 0)),
            pl.BlockSpec((1, heads, GROUP, GROUP), lambda n: (n, 0, 0, 0)),
        ],
        out_shape=[
            jax.ShapeDtypeStruct((rows, vals), BF16),
            jax.ShapeDtypeStruct((rows, heads), F32),
            jax.ShapeDtypeStruct((rows, width), F32),
            jax.ShapeDtypeStruct((rows, vals), BF16),
            jax.ShapeDtypeStruct((blocks, heads, dk, dv), BF16),
            jax.ShapeDtypeStruct((blocks, heads, GROUP, GROUP), BF16),
        ],
        scratch_shapes=[
            pltpu.VMEM((GROUP + TAIL, 2 * keys + vals), F32),
            pltpu.VMEM((heads, dk, dv), F32),
        ],
        compiler_params=pltpu.CompilerParams(dimension_semantics=("arbitrary",), vmem_limit_bytes=40 * 2**20),
        cost_estimate=pl.CostEstimate(flops=8 * 10**9, bytes_accessed=32 * 2**20, transcendentals=10**7),
        name="core_forward",
    )(pqkv, pab, taps, rate, bias)


def backward_kernel(
    dn_in, pqkv, pab, n_in, norm_in, conved, u_in, s_in, t_in, taps, rate, bias,
    dpqkv, dpab, dtaps, dsmall, dgain,
    ext, dstate,
):
    heads = rate.shape[1]
    vals = dn_in.shape[1]
    keys = (pqkv.shape[1] - vals) // 2
    dk, dv = keys // heads, vals // heads

    @pl.when(pl.program_id(0) == 0)
    def _():
        ext[...] = jnp.zeros_like(ext)
        dstate[...] = jnp.zeros_like(dstate)
        for ref in (dtaps, dsmall, dgain):
            ref[...] = jnp.zeros_like(ref)

    row, col = grid_iota(GROUP)
    tri = jnp.where(row >= col, 1.0, 0.0)
    upper = jnp.where(row <= col, 1.0, 0.0)
    beta, log_decay, pre = gates(pab[...], rate[...], bias[...], heads)
    c_col = mm_exact(tri, log_decay)
    c_row = mm_exact(log_decay, upper, TN)
    start_decay = jnp.exp(c_col)
    end_decay = jnp.exp(c_col[GROUP - 1 :, :] - c_col)
    last_decay = jnp.exp(c_col[GROUP - 1 :, :])
    lane = lax.broadcasted_iota(jnp.int32, (1, heads), 1)
    d_beta = jnp.zeros((GROUP, heads), F32)
    after = jnp.zeros((GROUP, heads), F32)
    before = jnp.zeros((GROUP, heads), F32)
    d_log = jnp.zeros((GROUP, heads), F32)
    gain_sum = jnp.zeros((1, dv), F32)

    for h in range(heads):
        ks, vs = slice(h * dk, (h + 1) * dk), slice(h * dv, (h + 1) * dv)
        kx, vx = slice(keys + h * dk, keys + (h + 1) * dk), slice(2 * keys + h * dv, 2 * keys + (h + 1) * dv)
        here = lane == h
        uq, uk, uv = conved[:, ks], conved[:, kx], conved[:, vx]
        sq, sk, sv = sigmoid(uq), sigmoid(uk), sigmoid(uv)
        q = uq * sq
        q_norm = lax.rsqrt(jnp.sum(q * q, -1, keepdims=True) + 1e-6)
        q = q * q_norm
        k = uk * sk
        k_norm = lax.rsqrt(jnp.sum(k * k, -1, keepdims=True) + 1e-6)
        k = k * k_norm
        v = uv * sv
        qs = q * dk**-0.5
        b = beta[:, h : h + 1]
        e = start_decay[:, h : h + 1]
        f = end_decay[:, h : h + 1]
        kb = k.astype(BF16)
        qb = qs.astype(BF16)

        n = n_in[:, vs].astype(F32)
        dn = dn_in[:, vs]
        dnn = dn * n
        gain_sum = gain_sum + jnp.sum(dnn, 0, keepdims=True)
        do = norm_in[:, h : h + 1] * (dn - n * jnp.mean(dnn, -1, keepdims=True))

        prod = mm(jnp.concatenate([kb, qb], 0), kb, NT)
        relative = jnp.where(row >= col, jnp.exp(jnp.minimum(c_col[:, h : h + 1] - c_row[h : h + 1, :], 0.0)), 0.0)
        kk, qk = prod[:GROUP], prod[GROUP:]
        strict = jnp.where(row > col, relative, 0.0)
        mix = relative * qk
        s_prev = s_in[0, h]
        u = u_in[:, vs]
        inv = t_in[0, h]
        ds = dstate[h]
        ds_low = ds.astype(BF16)
        dob = do.astype(BF16)
        ke, qe, kd = k * e, qs * e, k * f
        du = mm_split(mix, do, TN) + mm_split(kd, ds)
        du_hi, du_lo = halves(du)
        dr = mm(inv, du_hi, TN) + mm(inv, du_lo, TN)
        pair = jnp.concatenate([dob, dr.astype(BF16)], 0)
        dstate[h] = last_decay[:, h : h + 1] * ds + mm(jnp.concatenate([qe, -(b * ke)], 0), pair, TN)
        rest = jnp.concatenate([halves(do)[1], halves(dr)[1]], 0)
        cross = mm(pair, u, NT) + mm(rest, u, NT)
        dmix = jnp.where(row >= col, cross[:GROUP], 0.0)
        dlow = jnp.where(row > col, -cross[GROUP:], 0.0)
        back = mm(pair, s_prev, NT) + mm(rest, s_prev, NT)
        dqe, x = back[:GROUP], back[GROUP:]
        dkd = mm(u, ds_low, NT)
        dke = -(b * x)
        rk = strict * kk
        d_beta = d_beta + jnp.where(
            here,
            jnp.sum(dr * v, -1, keepdims=True) - jnp.sum(x * ke, -1, keepdims=True) + jnp.sum(dlow * rk, -1, keepdims=True),
            0.0,
        )
        dpair = dlow * (b * rk) + dmix * mix
        spread = mm(upper, dpair)
        last_part = last_decay[:, h : h + 1] * jnp.sum(ds * s_prev.astype(F32), keepdims=True)
        d_log = d_log + jnp.where(here, jnp.sum(jnp.where(row > col, spread, 0.0), -1, keepdims=True) + last_part, 0.0)
        after = after + jnp.where(here, jnp.sum(dqe * qe + dke * ke, -1, keepdims=True), 0.0)
        before = before + jnp.where(here, jnp.sum(dkd * kd, -1, keepdims=True), 0.0)
        dqk = dmix * relative
        dkk = dlow * (b * strict)
        first = mm(jnp.concatenate([dqk, dkk], 0), kb)
        dq = e * dqe + first[:GROUP]
        dk_ = e * dke + f * dkd + first[GROUP:] + mm(jnp.concatenate([dkk, dqk], 0), jnp.concatenate([kb, qb], 0), TN)
        dq = dq * dk**-0.5
        dq = q_norm * (dq - q * jnp.sum(dq * q, -1, keepdims=True))
        dk_ = k_norm * (dk_ - k * jnp.sum(dk_ * k, -1, keepdims=True))
        ext[:GROUP, ks] = dq * (sq * (1.0 + uq * (1.0 - sq)))
        ext[:GROUP, kx] = dk_ * (sk * (1.0 + uk * (1.0 - sk)))
        ext[:GROUP, vx] = (b * dr) * (sv * (1.0 + uv * (1.0 - sv)))

    d_log = d_log + mm_exact(upper, after) + mm_exact(jnp.where(row > col, 1.0, 0.0), before)
    d_pre = d_log * (-jnp.exp(rate[...])) * sigmoid(pre)
    dpab[:, :heads] = d_pre
    dpab[:, heads:] = d_beta * beta * (1.0 - beta)
    dsmall[0:1, :heads] += jnp.sum(d_log * log_decay, 0, keepdims=True)
    dsmall[0:1, heads:] += jnp.sum(d_pre, 0, keepdims=True)
    dgain[...] += gain_sum

    n_taps = taps.shape[0]
    rows_in = pqkv[...]
    total = None
    for i in range(n_taps):
        start = n_taps - 1 - i
        piece = ext[start : start + GROUP, :]
        term = piece * taps[i : i + 1, :]
        total = term if total is None else total + term
        dtaps[i : i + 1, :] += jnp.sum(piece * rows_in, 0, keepdims=True)
    dpqkv[...] = total.astype(dpqkv.dtype)
    ext[GROUP:, :] = ext[:TAIL, :]


def core_backward(dn, pqkv, pab, kept, taps, rate, bias):
    n_in, norm_in, conved, u_in, s_in, t_in = kept
    rows, width = pqkv.shape
    vals = dn.shape[1]
    keys = (width - vals) // 2
    heads = rate.shape[1]
    dk, dv = keys // heads, vals // heads
    blocks = rows // GROUP
    tokens = lambda width: pl.BlockSpec((GROUP, width), lambda n: (blocks - 1 - n, 0))
    stacked = lambda a: pl.BlockSpec((1,) + a.shape[1:], lambda n: (blocks - 1 - n, 0, 0, 0))
    fixed = lambda shape: pl.BlockSpec(shape, lambda n: (0, 0))
    small = (1, 2 * heads)
    return pl.pallas_call(
        backward_kernel,
        grid=(blocks,),
        in_specs=[tokens(a.shape[1]) for a in (dn, pqkv, pab, n_in, norm_in, conved, u_in)]
        + [stacked(s_in), stacked(t_in)]
        + [fixed(a.shape) for a in (taps, rate, bias)],
        out_specs=[tokens(a.shape[1]) for a in (pqkv, pab)]
        + [fixed(taps.shape), fixed(small), fixed((1, dv))],
        out_shape=[jax.ShapeDtypeStruct(pqkv.shape, BF16), jax.ShapeDtypeStruct(pab.shape, F32)]
        + [jax.ShapeDtypeStruct(s, F32) for s in (taps.shape, small, (1, dv))],
        scratch_shapes=[
            pltpu.VMEM((GROUP + TAIL, 2 * keys + vals), F32),
            pltpu.VMEM((heads, dk, dv), F32),
        ],
        compiler_params=pltpu.CompilerParams(dimension_semantics=("arbitrary",), vmem_limit_bytes=40 * 2**20),
        cost_estimate=pl.CostEstimate(flops=20 * 10**9, bytes_accessed=48 * 2**20, transcendentals=10**7),
        name="core_backward",
    )(dn, pqkv, pab, n_in, norm_in, conved, u_in, s_in, t_in, taps, rate, bias)


def projections_kernel(dqkv, dpo, dab, w_qkv, w_out, w_ab, normed, out, sums):
    grad = (
        mm(dqkv[...], w_qkv[...], NT)
        + mm(dpo[...], w_out[...], NT)
        + mm(dab[...], w_ab[...])
    )
    out[...] = grad.astype(out.dtype)
    sums[...] = jnp.sum(grad * normed[...].astype(F32), 0, keepdims=True)


def projections_back(dqkv, dpo, dab, w_qkv, w_out, w_ab, normed):
    rows, model = normed.shape
    tile = 256
    whole = lambda a: pl.BlockSpec(a.shape, lambda n: (0, 0), pipeline_mode=pl.Buffered(1))
    return pl.pallas_call(
        projections_kernel,
        grid=(model // tile,),
        in_specs=[
            whole(dqkv),
            whole(dpo),
            whole(dab),
            pl.BlockSpec((tile, dqkv.shape[1]), lambda n: (n, 0)),
            pl.BlockSpec((tile, dpo.shape[1]), lambda n: (n, 0)),
            pl.BlockSpec((dab.shape[1], tile), lambda n: (0, n)),
            pl.BlockSpec((rows, tile), lambda n: (0, n)),
        ],
        out_specs=[pl.BlockSpec((rows, tile), lambda n: (0, n)), pl.BlockSpec((1, tile), lambda n: (0, n))],
        out_shape=[jax.ShapeDtypeStruct((rows, model), BF16), jax.ShapeDtypeStruct((1, model), F32)],
        compiler_params=pltpu.CompilerParams(dimension_semantics=("arbitrary",), vmem_limit_bytes=40 * 2**20),
        cost_estimate=pl.CostEstimate(
            flops=2 * rows * model * (dqkv.shape[1] + dpo.shape[1]), bytes_accessed=32 * 2**20, transcendentals=0
        ),
        name="projections_back",
    )(dqkv, dpo, dab, w_qkv, w_out, w_ab, normed)


def side_by_side_kernel(*refs):
    *parts, out = refs
    at = 0
    for part in parts:
        out[:, at : at + part.shape[1]] = part[...].astype(out.dtype)
        at += part.shape[1]


def side_by_side(*parts):
    rows = parts[0].shape[0]
    step = rows // 2
    width = sum(a.shape[1] for a in parts)
    band = lambda columns: pl.BlockSpec((step, columns), lambda n: (n, 0))
    return pl.pallas_call(
        side_by_side_kernel,
        grid=(2,),
        in_specs=[band(a.shape[1]) for a in parts],
        out_specs=band(width),
        out_shape=jax.ShapeDtypeStruct((rows, width), BF16),
        name="side_by_side",
    )(*parts)


def apart_kernel(whole, *outs):
    at = 0
    for out in outs:
        out[...] = whole[:, at : at + out.shape[1]].astype(out.dtype)
        at += out.shape[1]


def apart(whole, *widths):
    rows = whole.shape[0]
    step = rows // 2
    band = lambda columns: pl.BlockSpec((step, columns), lambda n: (n, 0))
    return pl.pallas_call(
        apart_kernel,
        grid=(2,),
        in_specs=[band(whole.shape[1])],
        out_specs=[band(width) for width in widths],
        out_shape=[jax.ShapeDtypeStruct((rows, width), F32) for width in widths],
        name="apart",
    )(whole)


def rms_norm(values, gain_vec):
    return values * lax.rsqrt(jnp.mean(values * values, -1, keepdims=True) + 1e-05) * gain_vec


def dot(a, b, dims=NN):
    return lax.dot_general(a, b, (dims, ((), ())), preferred_element_type=F32)


def swap(piece, mask):
    return lax.ppermute(piece, "tensor", [(i, i ^ mask) for i in range(4)])


def gather_rows(own, beside=None):
    if lax.axis_size("tensor") != 4:
        full = lax.all_gather(own, "tensor", axis=0, tiled=True)
        return full if beside is None else (full, beside)
    half = own.shape[0] // 2
    first, second = swap(own, 1), swap(own, 2)
    if beside is not None:
        first, second, beside = lax.optimization_barrier((first, second, beside))
    full = jnp.concatenate([own, first, second, swap(second[:half], 1), swap(first[half:], 2)], 0)
    return full if beside is None else (full, beside)


def scatter_rows(part, beside=None):
    if lax.axis_size("tensor") != 4:
        total = lax.psum_scatter(part, "tensor", scatter_dimension=0, tiled=True).astype(F32)
        return total if beside is None else (total, beside)
    rows, half = part.shape[0] // 4, part.shape[1] // 2

    def chunk(k, columns):
        return part[k * rows : (k + 1) * rows, columns]

    plans = ((slice(0, half), 1, 2), (slice(half, 2 * half), 2, 1))
    arrived = [swap(jnp.concatenate([chunk(one, columns), chunk(3, columns)], 0), one) for columns, one, _ in plans]
    if beside is not None:
        arrived, beside = lax.optimization_barrier((arrived, beside))
    owns, passed = [], []
    for (columns, _, two), got in zip(plans, arrived):
        got = got.astype(F32)
        owns.append(chunk(0, columns).astype(F32) + got[:rows])
        passed.append((chunk(two, columns).astype(F32) + got[rows:]).astype(BF16))
    passed = lax.optimization_barrier(passed)
    sums = [own + swap(piece, two).astype(F32) for own, piece, (_, _, two) in zip(owns, passed, plans)]
    total = jnp.concatenate(sums, 1)
    return total if beside is None else (total, beside)


def scatter_direct(part, beside):
    if lax.axis_size("tensor") != 4:
        return lax.psum_scatter(part, "tensor", scatter_dimension=0, tiled=True).astype(F32), beside
    chunks = jnp.split(part, 4)
    arrived, beside = lax.optimization_barrier(([swap(chunks[k], k) for k in range(1, 4)], beside))
    return sum((piece.astype(F32) for piece in arrived), chunks[0].astype(F32)), beside


def sum_along(values, axis):
    size = lax.axis_size(axis)
    if size & (size - 1):
        return lax.psum(values, axis)
    mask = 1
    while mask < size:
        values = values + lax.ppermute(values, axis, [(i, i ^ mask) for i in range(size)])
        mask *= 2
    return values


def reorder(rows_in):
    if lax.axis_size("tensor") != 4:
        return rows_in
    rows = rows_in.shape[0] // 4
    me = lax.axis_index("tensor")
    return jnp.concatenate([lax.dynamic_slice_in_dim(rows_in, (me ^ k) * rows, rows, 0) for k in range(4)], 0)


def norm_back(values, gain_vec, grad):
    factor = lax.rsqrt(jnp.mean(values * values, -1, keepdims=True) + 1e-05)
    normal = values * factor
    scaled = grad * gain_vec
    return (
        factor * (scaled - normal * jnp.mean(scaled * normal, -1, keepdims=True)),
        jnp.sum(grad * normal, 0),
    )


def gather_dp(shard, axis):
    return lax.all_gather(shard.astype(BF16), "dp", axis=axis, tiled=True)


def sibling(piece):
    return lax.ppermute(piece, "dp", [(i, i ^ 1) for i in range(lax.axis_size("dp"))])


def split_blocks(full):
    size = lax.axis_size("dp")
    width = full.shape[1] // size
    core = lax.axis_index("dp") % 2

    def pick(c):
        return jnp.concatenate(
            [lax.dynamic_slice_in_dim(full, (2 * i + c) * width, width, 1) for i in range(size // 2)], 1
        )

    return pick(core), pick(1 - core)


def scatter_chips(part, axis):
    size = lax.axis_size("dp")
    groups = [list(range(core, size, 2)) for core in range(2)]
    return lax.psum_scatter(part, "dp", scatter_dimension=axis, tiled=True, axis_index_groups=groups)


def local(
    hidden_in,
    grad_out,
    mix_gain,
    w_query,
    w_key,
    w_value,
    conv_query,
    conv_key,
    conv_value,
    w_decay,
    w_beta,
    log_rate,
    decay_bias,
    w_outgate,
    head_gain,
    w_output,
    ffn_gain,
    w_gate,
    w_up,
    w_down,
):
    dp = lax.axis_size("dp")
    model = hidden_in.shape[1]
    keys, vals, hidden = w_query.shape[1], w_value.shape[1], w_gate.shape[1]
    heads = w_decay.shape[1]
    first_head = lax.axis_index("tensor") * heads
    rate = lax.dynamic_slice_in_dim(log_rate, first_head, heads)[None]
    bias = lax.dynamic_slice_in_dim(decay_bias, first_head, heads)[None]
    gain = jnp.tile(head_gain, heads)

    narrow = jnp.concatenate([w_decay, w_beta], 1).T
    kernels = jnp.concatenate([conv_query, conv_key, conv_value], 1)
    wide = max(narrow.shape[1], kernels.shape[1])
    pad = lambda a: jnp.pad(a, ((0, 0), (0, wide - a.shape[1])))
    few = lax.all_gather(jnp.concatenate([pad(narrow), pad(kernels)], 0).astype(BF16), "dp")
    unroll = lambda a: jnp.swapaxes(a, 0, 1).reshape(a.shape[1], -1)
    full_narrow = unroll(few[:, : 2 * heads, : narrow.shape[1]])
    pieces = few[:, 2 * heads :, : kernels.shape[1]]
    cut = (conv_query.shape[1], conv_query.shape[1] + conv_key.shape[1])
    taps = jnp.concatenate(
        [unroll(pieces[:, :, : cut[0]]), unroll(pieces[:, :, cut[0] : cut[1]]), unroll(pieces[:, :, cut[1] :])], 1
    ).astype(F32)

    full_qkv = gather_dp(side_by_side(w_query, w_key, w_value), 0)
    full_gate_out = gather_dp(jnp.concatenate([w_outgate, w_output.T], 1), 0)
    full_outgate, full_output = full_gate_out[:, :vals], full_gate_out[:, vals:]
    full_pair = gather_dp(jnp.concatenate([w_gate, w_up], 1), 0)
    full_down = gather_dp(w_down, 1)

    hold = lax.optimization_barrier
    rows_in = hidden_in.astype(F32)
    normed = reorder(gather_rows(rms_norm(rows_in, mix_gain).astype(BF16)))
    cot_own, _ = hold((grad_out, normed))
    cot = gather_rows(cot_own)
    pqkv = dot(normed, full_qkv)
    pab = dot(normed, full_narrow, NT)
    pqkv, cot, normed_here, normed_there = hold((pqkv, cot, *split_blocks(normed)))
    kept = core_forward(pqkv, pab, taps, rate, bias, keys)
    po = dot(normed, full_outgate)
    po_sig = jax.nn.sigmoid(po)
    mixed = (kept[0].astype(F32) * gain * (po * po_sig)).astype(BF16)
    middle = rows_in + scatter_rows(reorder(dot(mixed, full_output, NT).astype(BF16)))

    ffn_rows = gather_rows(rms_norm(middle, ffn_gain).astype(BF16))
    pre = dot(ffn_rows, full_pair)
    gate_pre, up_pre = pre[:, :hidden], pre[:, hidden:]
    gate_sig = jax.nn.sigmoid(gate_pre)
    activ = (gate_pre * gate_sig * up_pre).astype(BF16)
    cot, part_down = hold((cot, dot(activ, cot, TN).astype(BF16)))
    grad_w_down = lax.psum_scatter(part_down, "dp", scatter_dimension=1, tiled=True)
    grad_activ = dot(cot, full_down, NT)
    grad_gate_pre = (grad_activ * up_pre * gate_sig * (1.0 + gate_pre * (1.0 - gate_sig))).astype(BF16)
    grad_up_pre = (grad_activ * (gate_pre * gate_sig)).astype(BF16)
    grad_pre = jnp.concatenate([grad_gate_pre, grad_up_pre], 1)
    ffn_here, ffn_there = split_blocks(ffn_rows)
    grad_pre, sent = hold((grad_pre, dot(ffn_there, grad_pre, TN).astype(BF16)))
    got = sibling(sent)
    grad_ffn_rows, got = hold((dot(grad_pre, full_pair, NT).astype(BF16), got))
    part_pair = (dot(ffn_here, grad_pre, TN) + got.astype(F32)).astype(BF16)
    grad_ffn_norm, part_pair = scatter_rows(grad_ffn_rows, part_pair)
    grad_pair = scatter_chips(part_pair, 0)
    grad_middle_norm, ffn_gain_part = norm_back(middle, ffn_gain, grad_ffn_norm)
    grad_middle = grad_out.astype(F32) + grad_middle_norm

    activ_late, mix_low = hold((activ, grad_middle.astype(BF16)))
    mix_cot, out_part = gather_rows(mix_low, dot(activ_late, full_down).astype(BF16))
    mix_cot = reorder(mix_cot)
    mix_here, mix_there = split_blocks(mix_cot)
    mix_cot, sent_output = hold((mix_cot, dot(mix_there, mixed, TN).astype(BF16)))
    grad_mixed = dot(mix_cot, full_output)
    grad_po = grad_mixed * kept[0].astype(F32) * gain * (po_sig * (1.0 + po * (1.0 - po_sig)))
    grad_po = grad_po.astype(BF16)
    grad_n = grad_mixed * gain * (po * po_sig)
    sent_outgate = dot(normed_there, grad_po, TN).astype(BF16)
    got_output, got_outgate = sibling(sent_output), sibling(sent_outgate)
    part_output = (dot(mix_here, mixed, TN) + got_output.astype(F32)).astype(BF16)
    part_outgate = (dot(normed_here, grad_po, TN) + got_outgate.astype(F32)).astype(BF16)
    part_gate_out = jnp.concatenate([part_outgate, part_output], 1)
    grad_n, grad_w_down, part_gate_out = hold((grad_n, grad_w_down, part_gate_out))
    grad_gate_out = scatter_chips(part_gate_out, 0)
    grad_pqkv, grad_pab, grad_taps, grad_small, grad_gain = core_backward(grad_n, pqkv, pab, kept, taps, rate, bias)
    grad_pqkv, grad_pair = hold((grad_pqkv, grad_pair))
    out_rows, grad_pqkv = scatter_direct(out_part, grad_pqkv)
    grad_pqkv, sent = hold((grad_pqkv, dot(normed_there, grad_pqkv, TN).astype(BF16)))
    got = sibling(sent)
    part_qkv = (dot(normed_here, grad_pqkv, TN) + got.astype(F32)).astype(BF16)
    grad_pqkv, grad_pab, grad_taps, part_qkv = hold((grad_pqkv, grad_pab, grad_taps, part_qkv))
    grad_qkv = scatter_chips(part_qkv, 0)
    low_pab = grad_pab.astype(BF16)
    grad_normed, gain_sum = projections_back(grad_pqkv, grad_po, low_pab, full_qkv, full_gate_out, full_narrow, normed)
    mix_gain_part = gain_sum[0] / mix_gain
    grad_narrow = dot(low_pab, normed, TN)
    roll = lambda a: jnp.swapaxes(a.reshape(a.shape[0], dp, -1), 0, 1)
    grad_kernels = jnp.concatenate(
        [roll(grad_taps[:, :keys]), roll(grad_taps[:, keys : 2 * keys]), roll(grad_taps[:, 2 * keys :])], 2
    )
    pad3 = lambda a: jnp.pad(a, ((0, 0), (0, 0), (0, wide - a.shape[2])))
    few_parts = jnp.concatenate([pad3(roll(grad_narrow)), pad3(grad_kernels)], 1)
    few_grads = jnp.sum(lax.all_to_all(few_parts, "dp", 0, 0, tiled=True), 0)
    grad_narrow = few_grads[: 2 * heads, : narrow.shape[1]].T
    grad_kernels = few_grads[2 * heads :, : kernels.shape[1]]

    place = lambda a: lax.dynamic_update_slice_in_dim(jnp.zeros_like(log_rate), a, first_head, 0)
    gains = jnp.concatenate(
        [
            mix_gain_part,
            ffn_gain_part,
            grad_gain[0] / head_gain,
            place(grad_small[0, :heads]),
            place(grad_small[0, heads:]),
        ]
    )
    grad_normed, grad_pair, grad_w_down, grad_gate_out, out_rows, gains = hold(
        (grad_normed, grad_pair, grad_w_down, grad_gate_out, out_rows, gains)
    )
    hidden_out = (middle + out_rows).astype(BF16)
    grad_mix_norm, gains = scatter_rows(reorder(grad_normed), sum_along(gains, "dp"))
    sums = sum_along(gains, "tensor")
    grad_rows, _ = norm_back(rows_in, mix_gain, grad_mix_norm)
    grad_in = (grad_middle + grad_rows).astype(BF16)
    ends = [model, 2 * model, 2 * model + head_gain.shape[0], 2 * model + head_gain.shape[0] + log_rate.shape[0]]
    grad_mix_gain, grad_ffn_gain, grad_head_gain, grad_log_rate, grad_decay_bias = jnp.split(sums, ends)
    grad_w_query, grad_w_key, grad_w_value = apart(grad_qkv, keys, keys, vals)
    grad_gate_out, grad_pair = grad_gate_out.astype(F32), grad_pair.astype(F32)
    return (
        hidden_out,
        grad_in,
        grad_mix_gain,
        grad_w_query,
        grad_w_key,
        grad_w_value,
        grad_kernels[:, : cut[0]],
        grad_kernels[:, cut[0] : cut[1]],
        grad_kernels[:, cut[1] :],
        grad_narrow[:, :heads],
        grad_narrow[:, heads:],
        grad_log_rate,
        grad_decay_bias,
        grad_gate_out[:, :vals],
        grad_head_gain,
        grad_gate_out[:, vals:].T,
        grad_ffn_gain,
        grad_pair[:, :hidden],
        grad_pair[:, hidden:],
        grad_w_down.astype(F32),
    )


def solution(mesh):
    rows, both, flat = P(("dp", "tensor"), None), P("dp", "tensor"), P(None, ("tensor", "dp"))
    turned = P("tensor", "dp")
    return jax.shard_map(
        local,
        mesh=mesh,
        in_specs=(
            *(rows, rows, P()),
            *(both, both, both, flat, flat, flat, both, both),
            *(P(), P(), both, P(), turned, P(), both, both, turned),
        ),
        out_specs=(
            *(rows, rows, P()),
            *(both, both, both, flat, flat, flat, both, both),
            *(P(), P(), both, P(), turned, P(), both, both, turned),
        ),
        check_vma=False,
    )
```

```python
import jax
import jax.numpy as jnp
from jax import lax
from jax.experimental import pallas as pl
from jax.experimental.pallas import tpu as pltpu
from jax.sharding import PartitionSpec as P

GROUP = 64
TAIL = 8
F32 = jnp.float32
BF16 = jnp.bfloat16
HIGHEST = lax.Precision.HIGHEST


def mm(a, b, dims=((1,), (0,))):
    return lax.dot_general(a.astype(BF16), b.astype(BF16), (dims, ((), ())), preferred_element_type=F32)


NN = ((1,), (0,))
NT = ((1,), (1,))
TN = ((0,), (0,))


def mm_exact(a, b, dims=NN):
    return lax.dot_general(a, b, (dims, ((), ())), precision=HIGHEST, preferred_element_type=F32)


def halves(a):
    high = a.astype(BF16)
    return high, (a - high.astype(F32)).astype(BF16)


def mm_split(a, b, dims=NN):
    a_high, a_low = halves(a)
    b_high, b_low = halves(b)
    return mm(a_high, b_high, dims) + (mm(a_high, b_low, dims) + mm(a_low, b_high, dims))


def sigmoid(x):
    return 1.0 / (1.0 + jnp.exp(-x))


def softplus(x):
    return jnp.maximum(x, 0.0) + jnp.log1p(jnp.exp(-jnp.abs(x)))


def grid_iota(size):
    return (
        lax.broadcasted_iota(jnp.int32, (size, size), 0),
        lax.broadcasted_iota(jnp.int32, (size, size), 1),
    )


def unit_lower_inverses(lowers, row, col):
    size = lowers[0].shape[0]
    base = 16
    eye = jnp.where(row == col, 1.0, 0.0)
    powers = [jnp.where(row // base == col // base, -lower, 0.0) for lower in lowers]
    inverses = [eye + power for power in powers]
    reach = 2
    while reach < base:
        powers = [mm_split(power, power) for power in powers]
        inverses = [inverse + mm_split(inverse, power) for inverse, power in zip(inverses, powers)]
        reach *= 2
    while base < size:
        wide = 2 * base
        off = (row // wide == col // wide) & (row // base > col // base)
        right = [mm_split(jnp.where(off, lower, 0.0), inverse) for lower, inverse in zip(lowers, inverses)]
        inverses = [inverse - mm_split(inverse, r) for inverse, r in zip(inverses, right)]
        base = wide
    return inverses


def gates(p_ab, rate, bias, heads):
    pre = p_ab[:, :heads] + bias
    return sigmoid(p_ab[:, heads:]), -jnp.exp(rate) * softplus(pre), pre


def forward_kernel(
    pqkv, pab, taps, rate, bias,
    n_out, norm_out, conved, u_out, s_out, t_out,
    ext, state,
):
    heads = rate.shape[1]
    vals = n_out.shape[1]
    keys = (pqkv.shape[1] - vals) // 2
    dk, dv = keys // heads, vals // heads

    @pl.when(pl.program_id(0) == 0)
    def _():
        ext[...] = jnp.zeros_like(ext)
        state[...] = jnp.zeros_like(state)

    ext[TAIL:, :] = pqkv[...]
    n_taps = taps.shape[0]
    total = None
    for i in range(n_taps):
        start = TAIL - (n_taps - 1) + i
        term = ext[start : start + GROUP, :] * taps[i : i + 1, :]
        total = term if total is None else total + term
    conved[...] = total
    ext[:TAIL, :] = ext[GROUP:, :]

    row, col = grid_iota(GROUP)
    tri = jnp.where(row >= col, 1.0, 0.0)
    beta, log_decay, _ = gates(pab[...], rate[...], bias[...], heads)
    c_col = mm_exact(tri, log_decay)
    c_row = mm_exact(log_decay, jnp.where(row <= col, 1.0, 0.0), TN)
    start_decay = jnp.exp(c_col)
    end_decay = jnp.exp(c_col[GROUP - 1 :, :] - c_col)
    last_decay = jnp.exp(c_col[GROUP - 1 :, :])

    qs, ks, vs, bs, prods, relatives, lowers = [], [], [], [], [], [], []
    for h in range(heads):
        uq = conved[:, h * dk : (h + 1) * dk]
        uk = conved[:, keys + h * dk : keys + (h + 1) * dk]
        uv = conved[:, 2 * keys + h * dv : 2 * keys + (h + 1) * dv]
        q = uq * sigmoid(uq)
        qs.append(q * (lax.rsqrt(jnp.sum(q * q, -1, keepdims=True) + 1e-6) * dk**-0.5))
        k = uk * sigmoid(uk)
        ks.append(k * lax.rsqrt(jnp.sum(k * k, -1, keepdims=True) + 1e-6))
        vs.append(uv * sigmoid(uv))
        bs.append(beta[:, h : h + 1])
    for h in range(heads):
        prods.append(mm_split(jnp.concatenate([ks[h], qs[h]], 0), ks[h], NT))
    for h in range(heads):
        differ = jnp.minimum(c_col[:, h : h + 1] - c_row[h : h + 1, :], 0.0)
        relatives.append(jnp.where(row >= col, jnp.exp(differ), 0.0))
        lowers.append(jnp.where(row > col, bs[h] * relatives[h] * prods[h][:GROUP], 0.0))
    invs = [inverse for inverse in unit_lower_inverses(lowers, row, col)]
    states = [state[h] for h in range(heads)]
    lows = states
    reads = []
    for h in range(heads):
        e = start_decay[:, h : h + 1]
        reads.append(mm_split(jnp.concatenate([ks[h] * e, qs[h] * e], 0), lows[h]))
    us = [mm_split(invs[h], bs[h] * (vs[h] - reads[h][:GROUP])) for h in range(heads)]
    outs = [reads[h][GROUP:] + mm_split(relatives[h] * prods[h][GROUP:], us[h]) for h in range(heads)]
    nexts = [
        last_decay[:, h : h + 1] * states[h] + mm_split(ks[h] * end_decay[:, h : h + 1], us[h], TN) for h in range(heads)
    ]
    for h in range(heads):
        cols = slice(h * dv, (h + 1) * dv)
        state[h] = nexts[h]
        t_out[0, h] = invs[h].astype(t_out.dtype)
        s_out[0, h] = lows[h].astype(s_out.dtype)
        u_out[:, cols] = us[h].astype(u_out.dtype)
        o = outs[h]
        norm = lax.rsqrt(jnp.mean(o * o, -1, keepdims=True) + 1e-5)
        n_out[:, cols] = (o * norm).astype(n_out.dtype)
        norm_out[:, h : h + 1] = norm


def core_forward(pqkv, pab, taps, rate, bias, keys):
    rows, width = pqkv.shape
    vals = width - 2 * keys
    heads = rate.shape[1]
    dk, dv = keys // heads, vals // heads
    blocks = rows // GROUP
    tokens = lambda width: pl.BlockSpec((GROUP, width), lambda n: (n, 0))
    fixed = lambda a: pl.BlockSpec(a.shape, lambda n: (0, 0))
    return pl.pallas_call(
        forward_kernel,
        grid=(blocks,),
        in_specs=[tokens(a.shape[1]) for a in (pqkv, pab)] + [fixed(a) for a in (taps, rate, bias)],
        out_specs=[
            tokens(vals),
            tokens(heads),
            tokens(width),
            tokens(vals),
            pl.BlockSpec((1, heads, dk, dv), lambda n: (n, 0, 0, 0)),
            pl.BlockSpec((1, heads, GROUP, GROUP), lambda n: (n, 0, 0, 0)),
        ],
        out_shape=[
            jax.ShapeDtypeStruct((rows, vals), BF16),
            jax.ShapeDtypeStruct((rows, heads), F32),
            jax.ShapeDtypeStruct((rows, width), F32),
            jax.ShapeDtypeStruct((rows, vals), BF16),
            jax.ShapeDtypeStruct((blocks, heads, dk, dv), BF16),
            jax.ShapeDtypeStruct((blocks, heads, GROUP, GROUP), BF16),
        ],
        scratch_shapes=[
            pltpu.VMEM((GROUP + TAIL, 2 * keys + vals), F32),
            pltpu.VMEM((heads, dk, dv), F32),
        ],
        compiler_params=pltpu.CompilerParams(dimension_semantics=("arbitrary",), vmem_limit_bytes=40 * 2**20),
        cost_estimate=pl.CostEstimate(flops=8 * 10**9, bytes_accessed=32 * 2**20, transcendentals=10**7),
        name="core_forward",
    )(pqkv, pab, taps, rate, bias)


def backward_kernel(
    dn_in, pqkv, pab, n_in, norm_in, conved, u_in, s_in, t_in, taps, rate, bias,
    dpqkv, dpab, dtaps, dsmall, dgain,
    ext, dstate,
):
    heads = rate.shape[1]
    vals = dn_in.shape[1]
    keys = (pqkv.shape[1] - vals) // 2
    dk, dv = keys // heads, vals // heads

    @pl.when(pl.program_id(0) == 0)
    def _():
        ext[...] = jnp.zeros_like(ext)
        dstate[...] = jnp.zeros_like(dstate)
        for ref in (dtaps, dsmall, dgain):
            ref[...] = jnp.zeros_like(ref)

    row, col = grid_iota(GROUP)
    tri = jnp.where(row >= col, 1.0, 0.0)
    upper = jnp.where(row <= col, 1.0, 0.0)
    beta, log_decay, pre = gates(pab[...], rate[...], bias[...], heads)
    c_col = mm_exact(tri, log_decay)
    c_row = mm_exact(log_decay, upper, TN)
    start_decay = jnp.exp(c_col)
    end_decay = jnp.exp(c_col[GROUP - 1 :, :] - c_col)
    last_decay = jnp.exp(c_col[GROUP - 1 :, :])
    lane = lax.broadcasted_iota(jnp.int32, (1, heads), 1)
    d_beta = jnp.zeros((GROUP, heads), F32)
    after = jnp.zeros((GROUP, heads), F32)
    before = jnp.zeros((GROUP, heads), F32)
    d_log = jnp.zeros((GROUP, heads), F32)
    gain_sum = jnp.zeros((1, dv), F32)

    for h in range(heads):
        ks, vs = slice(h * dk, (h + 1) * dk), slice(h * dv, (h + 1) * dv)
        kx, vx = slice(keys + h * dk, keys + (h + 1) * dk), slice(2 * keys + h * dv, 2 * keys + (h + 1) * dv)
        here = lane == h
        uq, uk, uv = conved[:, ks], conved[:, kx], conved[:, vx]
        sq, sk, sv = sigmoid(uq), sigmoid(uk), sigmoid(uv)
        q = uq * sq
        q_norm = lax.rsqrt(jnp.sum(q * q, -1, keepdims=True) + 1e-6)
        q = q * q_norm
        k = uk * sk
        k_norm = lax.rsqrt(jnp.sum(k * k, -1, keepdims=True) + 1e-6)
        k = k * k_norm
        v = uv * sv
        qs = q * dk**-0.5
        b = beta[:, h : h + 1]
        e = start_decay[:, h : h + 1]
        f = end_decay[:, h : h + 1]
        kb = k.astype(BF16)
        qb = qs.astype(BF16)

        n = n_in[:, vs].astype(F32)
        dn = dn_in[:, vs]
        dnn = dn * n
        gain_sum = gain_sum + jnp.sum(dnn, 0, keepdims=True)
        do = norm_in[:, h : h + 1] * (dn - n * jnp.mean(dnn, -1, keepdims=True))

        prod = mm(jnp.concatenate([kb, qb], 0), kb, NT)
        relative = jnp.where(row >= col, jnp.exp(jnp.minimum(c_col[:, h : h + 1] - c_row[h : h + 1, :], 0.0)), 0.0)
        kk, qk = prod[:GROUP], prod[GROUP:]
        strict = jnp.where(row > col, relative, 0.0)
        mix = relative * qk
        s_prev = s_in[0, h]
        u = u_in[:, vs]
        inv = t_in[0, h]
        ds = dstate[h]
        ds_low = ds.astype(BF16)
        dob = do.astype(BF16)
        ke, qe, kd = k * e, qs * e, k * f
        du = mm_split(mix, do, TN) + mm_split(kd, ds)
        du_hi, du_lo = halves(du)
        dr = mm(inv, du_hi, TN) + mm(inv, du_lo, TN)
        pair = jnp.concatenate([dob, dr.astype(BF16)], 0)
        dstate[h] = last_decay[:, h : h + 1] * ds + mm(jnp.concatenate([qe, -(b * ke)], 0), pair, TN)
        rest = jnp.concatenate([halves(do)[1], halves(dr)[1]], 0)
        cross = mm(pair, u, NT) + mm(rest, u, NT)
        dmix = jnp.where(row >= col, cross[:GROUP], 0.0)
        dlow = jnp.where(row > col, -cross[GROUP:], 0.0)
        back = mm(pair, s_prev, NT) + mm(rest, s_prev, NT)
        dqe, x = back[:GROUP], back[GROUP:]
        dkd = mm(u, ds_low, NT)
        dke = -(b * x)
        rk = strict * kk
        d_beta = d_beta + jnp.where(
            here,
            jnp.sum(dr * v, -1, keepdims=True) - jnp.sum(x * ke, -1, keepdims=True) + jnp.sum(dlow * rk, -1, keepdims=True),
            0.0,
        )
        dpair = dlow * (b * rk) + dmix * mix
        spread = mm(upper, dpair)
        last_part = last_decay[:, h : h + 1] * jnp.sum(ds * s_prev.astype(F32), keepdims=True)
        d_log = d_log + jnp.where(here, jnp.sum(jnp.where(row > col, spread, 0.0), -1, keepdims=True) + last_part, 0.0)
        after = after + jnp.where(here, jnp.sum(dqe * qe + dke * ke, -1, keepdims=True), 0.0)
        before = before + jnp.where(here, jnp.sum(dkd * kd, -1, keepdims=True), 0.0)
        dqk = dmix * relative
        dkk = dlow * (b * strict)
        first = mm(jnp.concatenate([dqk, dkk], 0), kb)
        dq = e * dqe + first[:GROUP]
        dk_ = e * dke + f * dkd + first[GROUP:] + mm(jnp.concatenate([dkk, dqk], 0), jnp.concatenate([kb, qb], 0), TN)
        dq = dq * dk**-0.5
        dq = q_norm * (dq - q * jnp.sum(dq * q, -1, keepdims=True))
        dk_ = k_norm * (dk_ - k * jnp.sum(dk_ * k, -1, keepdims=True))
        ext[:GROUP, ks] = dq * (sq * (1.0 + uq * (1.0 - sq)))
        ext[:GROUP, kx] = dk_ * (sk * (1.0 + uk * (1.0 - sk)))
        ext[:GROUP, vx] = (b * dr) * (sv * (1.0 + uv * (1.0 - sv)))

    d_log = d_log + mm_exact(upper, after) + mm_exact(jnp.where(row > col, 1.0, 0.0), before)
    d_pre = d_log * (-jnp.exp(rate[...])) * sigmoid(pre)
    dpab[:, :heads] = d_pre
    dpab[:, heads:] = d_beta * beta * (1.0 - beta)
    dsmall[0:1, :heads] += jnp.sum(d_log * log_decay, 0, keepdims=True)
    dsmall[0:1, heads:] += jnp.sum(d_pre, 0, keepdims=True)
    dgain[...] += gain_sum

    n_taps = taps.shape[0]
    rows_in = pqkv[...]
    total = None
    for i in range(n_taps):
        start = n_taps - 1 - i
        piece = ext[start : start + GROUP, :]
        term = piece * taps[i : i + 1, :]
        total = term if total is None else total + term
        dtaps[i : i + 1, :] += jnp.sum(piece * rows_in, 0, keepdims=True)
    dpqkv[...] = total.astype(dpqkv.dtype)
    ext[GROUP:, :] = ext[:TAIL, :]


def core_backward(dn, pqkv, pab, kept, taps, rate, bias):
    n_in, norm_in, conved, u_in, s_in, t_in = kept
    rows, width = pqkv.shape
    vals = dn.shape[1]
    keys = (width - vals) // 2
    heads = rate.shape[1]
    dk, dv = keys // heads, vals // heads
    blocks = rows // GROUP
    tokens = lambda width: pl.BlockSpec((GROUP, width), lambda n: (blocks - 1 - n, 0))
    stacked = lambda a: pl.BlockSpec((1,) + a.shape[1:], lambda n: (blocks - 1 - n, 0, 0, 0))
    fixed = lambda shape: pl.BlockSpec(shape, lambda n: (0, 0))
    small = (1, 2 * heads)
    return pl.pallas_call(
        backward_kernel,
        grid=(blocks,),
        in_specs=[tokens(a.shape[1]) for a in (dn, pqkv, pab, n_in, norm_in, conved, u_in)]
        + [stacked(s_in), stacked(t_in)]
        + [fixed(a.shape) for a in (taps, rate, bias)],
        out_specs=[tokens(a.shape[1]) for a in (pqkv, pab)]
        + [fixed(taps.shape), fixed(small), fixed((1, dv))],
        out_shape=[jax.ShapeDtypeStruct(pqkv.shape, BF16), jax.ShapeDtypeStruct(pab.shape, F32)]
        + [jax.ShapeDtypeStruct(s, F32) for s in (taps.shape, small, (1, dv))],
        scratch_shapes=[
            pltpu.VMEM((GROUP + TAIL, 2 * keys + vals), F32),
            pltpu.VMEM((heads, dk, dv), F32),
        ],
        compiler_params=pltpu.CompilerParams(dimension_semantics=("arbitrary",), vmem_limit_bytes=40 * 2**20),
        cost_estimate=pl.CostEstimate(flops=20 * 10**9, bytes_accessed=48 * 2**20, transcendentals=10**7),
        name="core_backward",
    )(dn, pqkv, pab, n_in, norm_in, conved, u_in, s_in, t_in, taps, rate, bias)


def projections_kernel(dqkv, dpo, dab, w_qkv, w_out, w_ab, normed, out, sums):
    grad = (
        mm(dqkv[...], w_qkv[...], NT)
        + mm(dpo[...], w_out[...], NT)
        + mm(dab[...], w_ab[...])
    )
    out[...] = grad.astype(out.dtype)
    sums[...] = jnp.sum(grad * normed[...].astype(F32), 0, keepdims=True)


def projections_back(dqkv, dpo, dab, w_qkv, w_out, w_ab, normed):
    rows, model = normed.shape
    tile = 512
    whole = lambda a: pl.BlockSpec(a.shape, lambda n: (0, 0), pipeline_mode=pl.Buffered(1))
    return pl.pallas_call(
        projections_kernel,
        grid=(model // tile,),
        in_specs=[
            whole(dqkv),
            whole(dpo),
            whole(dab),
            pl.BlockSpec((tile, dqkv.shape[1]), lambda n: (n, 0)),
            pl.BlockSpec((tile, dpo.shape[1]), lambda n: (n, 0)),
            pl.BlockSpec((dab.shape[1], tile), lambda n: (0, n)),
            pl.BlockSpec((rows, tile), lambda n: (0, n)),
        ],
        out_specs=[pl.BlockSpec((rows, tile), lambda n: (0, n)), pl.BlockSpec((1, tile), lambda n: (0, n))],
        out_shape=[jax.ShapeDtypeStruct((rows, model), BF16), jax.ShapeDtypeStruct((1, model), F32)],
        compiler_params=pltpu.CompilerParams(dimension_semantics=("arbitrary",), vmem_limit_bytes=40 * 2**20),
        cost_estimate=pl.CostEstimate(
            flops=2 * rows * model * (dqkv.shape[1] + dpo.shape[1]), bytes_accessed=32 * 2**20, transcendentals=0
        ),
        name="projections_back",
    )(dqkv, dpo, dab, w_qkv, w_out, w_ab, normed)


def side_by_side_kernel(*refs):
    *parts, out = refs
    at = 0
    for part in parts:
        out[:, at : at + part.shape[1]] = part[...].astype(out.dtype)
        at += part.shape[1]


def side_by_side(*parts):
    rows = parts[0].shape[0]
    step = rows // 2
    width = sum(a.shape[1] for a in parts)
    band = lambda columns: pl.BlockSpec((step, columns), lambda n: (n, 0))
    return pl.pallas_call(
        side_by_side_kernel,
        grid=(2,),
        in_specs=[band(a.shape[1]) for a in parts],
        out_specs=band(width),
        out_shape=jax.ShapeDtypeStruct((rows, width), BF16),
        name="side_by_side",
    )(*parts)


def apart_kernel(whole, *outs):
    at = 0
    for out in outs:
        out[...] = whole[:, at : at + out.shape[1]].astype(out.dtype)
        at += out.shape[1]


def apart(whole, *widths):
    rows = whole.shape[0]
    step = rows // 2
    band = lambda columns: pl.BlockSpec((step, columns), lambda n: (n, 0))
    return pl.pallas_call(
        apart_kernel,
        grid=(2,),
        in_specs=[band(whole.shape[1])],
        out_specs=[band(width) for width in widths],
        out_shape=[jax.ShapeDtypeStruct((rows, width), F32) for width in widths],
        name="apart",
    )(whole)


def rms_norm(values, gain_vec):
    return values * lax.rsqrt(jnp.mean(values * values, -1, keepdims=True) + 1e-05) * gain_vec


def dot(a, b, dims=NN):
    return lax.dot_general(a, b, (dims, ((), ())), preferred_element_type=F32)


def swap(piece, mask):
    return lax.ppermute(piece, "tensor", [(i, i ^ mask) for i in range(4)])


def gather_rows(own, beside=None):
    if lax.axis_size("tensor") != 4:
        full = lax.all_gather(own, "tensor", axis=0, tiled=True)
        return full if beside is None else (full, beside)
    half = own.shape[0] // 2
    first, second = swap(own, 1), swap(own, 2)
    if beside is not None:
        first, second, beside = lax.optimization_barrier((first, second, beside))
    full = jnp.concatenate([own, first, second, swap(second[:half], 1), swap(first[half:], 2)], 0)
    return full if beside is None else (full, beside)


def scatter_rows(part, beside=None):
    if lax.axis_size("tensor") != 4:
        total = lax.psum_scatter(part, "tensor", scatter_dimension=0, tiled=True).astype(F32)
        return total if beside is None else (total, beside)
    rows, half = part.shape[0] // 4, part.shape[1] // 2

    def chunk(k, columns):
        return part[k * rows : (k + 1) * rows, columns]

    plans = ((slice(0, half), 1, 2), (slice(half, 2 * half), 2, 1))
    arrived = [swap(jnp.concatenate([chunk(one, columns), chunk(3, columns)], 0), one) for columns, one, _ in plans]
    if beside is not None:
        arrived, beside = lax.optimization_barrier((arrived, beside))
    owns, passed = [], []
    for (columns, _, two), got in zip(plans, arrived):
        got = got.astype(F32)
        owns.append(chunk(0, columns).astype(F32) + got[:rows])
        passed.append((chunk(two, columns).astype(F32) + got[rows:]).astype(BF16))
    passed = lax.optimization_barrier(passed)
    sums = [own + swap(piece, two).astype(F32) for own, piece, (_, _, two) in zip(owns, passed, plans)]
    total = jnp.concatenate(sums, 1)
    return total if beside is None else (total, beside)


def scatter_direct(part, beside):
    if lax.axis_size("tensor") != 4:
        return lax.psum_scatter(part, "tensor", scatter_dimension=0, tiled=True).astype(F32), beside
    chunks = jnp.split(part, 4)
    arrived, beside = lax.optimization_barrier(([swap(chunks[k], k) for k in range(1, 4)], beside))
    return sum((piece.astype(F32) for piece in arrived), chunks[0].astype(F32)), beside


def sum_along(values, axis):
    size = lax.axis_size(axis)
    if size & (size - 1):
        return lax.psum(values, axis)
    mask = 1
    while mask < size:
        values = values + lax.ppermute(values, axis, [(i, i ^ mask) for i in range(size)])
        mask *= 2
    return values


def reorder(rows_in):
    if lax.axis_size("tensor") != 4:
        return rows_in
    rows = rows_in.shape[0] // 4
    me = lax.axis_index("tensor")
    return jnp.concatenate([lax.dynamic_slice_in_dim(rows_in, (me ^ k) * rows, rows, 0) for k in range(4)], 0)


def norm_back(values, gain_vec, grad):
    factor = lax.rsqrt(jnp.mean(values * values, -1, keepdims=True) + 1e-05)
    normal = values * factor
    scaled = grad * gain_vec
    return (
        factor * (scaled - normal * jnp.mean(scaled * normal, -1, keepdims=True)),
        jnp.sum(grad * normal, 0),
    )


def gather_dp(shard, axis):
    return lax.all_gather(shard.astype(BF16), "dp", axis=axis, tiled=True)


def sibling(piece):
    return lax.ppermute(piece, "dp", [(i, i ^ 1) for i in range(lax.axis_size("dp"))])


def split_blocks(full):
    size = lax.axis_size("dp")
    width = full.shape[1] // size
    core = lax.axis_index("dp") % 2

    def pick(c):
        return jnp.concatenate(
            [lax.dynamic_slice_in_dim(full, (2 * i + c) * width, width, 1) for i in range(size // 2)], 1
        )

    return pick(core), pick(1 - core)


def scatter_chips(part, axis):
    size = lax.axis_size("dp")
    groups = [list(range(core, size, 2)) for core in range(2)]
    return lax.psum_scatter(part, "dp", scatter_dimension=axis, tiled=True, axis_index_groups=groups)


def local(
    hidden_in,
    grad_out,
    mix_gain,
    w_query,
    w_key,
    w_value,
    conv_query,
    conv_key,
    conv_value,
    w_decay,
    w_beta,
    log_rate,
    decay_bias,
    w_outgate,
    head_gain,
    w_output,
    ffn_gain,
    w_gate,
    w_up,
    w_down,
):
    dp = lax.axis_size("dp")
    model = hidden_in.shape[1]
    keys, vals, hidden = w_query.shape[1], w_value.shape[1], w_gate.shape[1]
    heads = w_decay.shape[1]
    first_head = lax.axis_index("tensor") * heads
    rate = lax.dynamic_slice_in_dim(log_rate, first_head, heads)[None]
    bias = lax.dynamic_slice_in_dim(decay_bias, first_head, heads)[None]
    gain = jnp.tile(head_gain, heads)

    narrow = jnp.concatenate([w_decay, w_beta], 1).T
    kernels = jnp.concatenate([conv_query, conv_key, conv_value], 1)
    wide = max(narrow.shape[1], kernels.shape[1])
    pad = lambda a: jnp.pad(a, ((0, 0), (0, wide - a.shape[1])))
    few = lax.all_gather(jnp.concatenate([pad(narrow), pad(kernels)], 0).astype(BF16), "dp")
    unroll = lambda a: jnp.swapaxes(a, 0, 1).reshape(a.shape[1], -1)
    full_narrow = unroll(few[:, : 2 * heads, : narrow.shape[1]])
    pieces = few[:, 2 * heads :, : kernels.shape[1]]
    cut = (conv_query.shape[1], conv_query.shape[1] + conv_key.shape[1])
    taps = jnp.concatenate(
        [unroll(pieces[:, :, : cut[0]]), unroll(pieces[:, :, cut[0] : cut[1]]), unroll(pieces[:, :, cut[1] :])], 1
    ).astype(F32)

    full_qkv = gather_dp(side_by_side(w_query, w_key, w_value), 0)
    full_gate_out = gather_dp(jnp.concatenate([w_outgate, w_output.T], 1), 0)
    full_outgate, full_output = full_gate_out[:, :vals], full_gate_out[:, vals:]
    full_pair = gather_dp(jnp.concatenate([w_gate, w_up], 1), 0)
    full_down = gather_dp(w_down, 1)

    hold = lax.optimization_barrier
    rows_in = hidden_in.astype(F32)
    normed = reorder(gather_rows(rms_norm(rows_in, mix_gain).astype(BF16)))
    cot_own, _ = hold((grad_out, normed))
    cot = gather_rows(cot_own)
    pqkv = dot(normed, full_qkv)
    pab = dot(normed, full_narrow, NT)
    pqkv, cot, normed_here, normed_there = hold((pqkv, cot, *split_blocks(normed)))
    kept = core_forward(pqkv, pab, taps, rate, bias, keys)
    po = dot(normed, full_outgate)
    po_sig = jax.nn.sigmoid(po)
    mixed = (kept[0].astype(F32) * gain * (po * po_sig)).astype(BF16)
    middle = rows_in + scatter_rows(reorder(dot(mixed, full_output, NT).astype(BF16)))

    ffn_rows = gather_rows(rms_norm(middle, ffn_gain).astype(BF16))
    pre = dot(ffn_rows, full_pair)
    gate_pre, up_pre = pre[:, :hidden], pre[:, hidden:]
    gate_sig = jax.nn.sigmoid(gate_pre)
    activ = (gate_pre * gate_sig * up_pre).astype(BF16)
    cot, part_down = hold((cot, dot(activ, cot, TN).astype(BF16)))
    grad_w_down = lax.psum_scatter(part_down, "dp", scatter_dimension=1, tiled=True)
    grad_activ = dot(cot, full_down, NT)
    grad_gate_pre = (grad_activ * up_pre * gate_sig * (1.0 + gate_pre * (1.0 - gate_sig))).astype(BF16)
    grad_up_pre = (grad_activ * (gate_pre * gate_sig)).astype(BF16)
    grad_pre = jnp.concatenate([grad_gate_pre, grad_up_pre], 1)
    ffn_here, ffn_there = split_blocks(ffn_rows)
    grad_pre, sent = hold((grad_pre, dot(ffn_there, grad_pre, TN).astype(BF16)))
    got = sibling(sent)
    grad_ffn_rows, got = hold((dot(grad_pre, full_pair, NT).astype(BF16), got))
    part_pair = (dot(ffn_here, grad_pre, TN) + got.astype(F32)).astype(BF16)
    grad_ffn_norm, part_pair = scatter_rows(grad_ffn_rows, part_pair)
    grad_pair = scatter_chips(part_pair, 0)
    grad_middle_norm, ffn_gain_part = norm_back(middle, ffn_gain, grad_ffn_norm)
    grad_middle = grad_out.astype(F32) + grad_middle_norm

    activ_late, mix_low = hold((activ, grad_middle.astype(BF16)))
    mix_cot, out_part = gather_rows(mix_low, dot(activ_late, full_down).astype(BF16))
    mix_cot = reorder(mix_cot)
    mix_here, mix_there = split_blocks(mix_cot)
    mix_cot, sent_output = hold((mix_cot, dot(mix_there, mixed, TN).astype(BF16)))
    grad_mixed = dot(mix_cot, full_output)
    grad_po = grad_mixed * kept[0].astype(F32) * gain * (po_sig * (1.0 + po * (1.0 - po_sig)))
    grad_po = grad_po.astype(BF16)
    grad_n = grad_mixed * gain * (po * po_sig)
    sent_outgate = dot(normed_there, grad_po, TN).astype(BF16)
    got_output, got_outgate = sibling(sent_output), sibling(sent_outgate)
    part_output = (dot(mix_here, mixed, TN) + got_output.astype(F32)).astype(BF16)
    part_outgate = (dot(normed_here, grad_po, TN) + got_outgate.astype(F32)).astype(BF16)
    part_gate_out = jnp.concatenate([part_outgate, part_output], 1)
    grad_n, grad_w_down, part_gate_out = hold((grad_n, grad_w_down, part_gate_out))
    grad_gate_out = scatter_chips(part_gate_out, 0)
    grad_pqkv, grad_pab, grad_taps, grad_small, grad_gain = core_backward(grad_n, pqkv, pab, kept, taps, rate, bias)
    grad_pqkv, grad_pair = hold((grad_pqkv, grad_pair))
    out_rows, grad_pqkv = scatter_direct(out_part, grad_pqkv)
    grad_pqkv, sent = hold((grad_pqkv, dot(normed_there, grad_pqkv, TN).astype(BF16)))
    got = sibling(sent)
    part_qkv = (dot(normed_here, grad_pqkv, TN) + got.astype(F32)).astype(BF16)
    grad_pqkv, grad_pab, grad_taps, part_qkv = hold((grad_pqkv, grad_pab, grad_taps, part_qkv))
    grad_qkv = scatter_chips(part_qkv, 0)
    low_pab = grad_pab.astype(BF16)
    grad_normed, gain_sum = projections_back(grad_pqkv, grad_po, low_pab, full_qkv, full_gate_out, full_narrow, normed)
    mix_gain_part = gain_sum[0] / mix_gain
    grad_narrow = dot(low_pab, normed, TN)
    roll = lambda a: jnp.swapaxes(a.reshape(a.shape[0], dp, -1), 0, 1)
    grad_kernels = jnp.concatenate(
        [roll(grad_taps[:, :keys]), roll(grad_taps[:, keys : 2 * keys]), roll(grad_taps[:, 2 * keys :])], 2
    )
    pad3 = lambda a: jnp.pad(a, ((0, 0), (0, 0), (0, wide - a.shape[2])))
    few_parts = jnp.concatenate([pad3(roll(grad_narrow)), pad3(grad_kernels)], 1)
    few_grads = jnp.sum(lax.all_to_all(few_parts, "dp", 0, 0, tiled=True), 0)
    grad_narrow = few_grads[: 2 * heads, : narrow.shape[1]].T
    grad_kernels = few_grads[2 * heads :, : kernels.shape[1]]

    place = lambda a: lax.dynamic_update_slice_in_dim(jnp.zeros_like(log_rate), a, first_head, 0)
    gains = jnp.concatenate(
        [
            mix_gain_part,
            ffn_gain_part,
            grad_gain[0] / head_gain,
            place(grad_small[0, :heads]),
            place(grad_small[0, heads:]),
        ]
    )
    grad_normed, grad_pair, grad_w_down, grad_gate_out, out_rows, gains = hold(
        (grad_normed, grad_pair, grad_w_down, grad_gate_out, out_rows, gains)
    )
    hidden_out = (middle + out_rows).astype(BF16)
    grad_mix_norm, gains = scatter_rows(reorder(grad_normed), sum_along(gains, "dp"))
    sums = sum_along(gains, "tensor")
    grad_rows, _ = norm_back(rows_in, mix_gain, grad_mix_norm)
    grad_in = (grad_middle + grad_rows).astype(BF16)
    ends = [model, 2 * model, 2 * model + head_gain.shape[0], 2 * model + head_gain.shape[0] + log_rate.shape[0]]
    grad_mix_gain, grad_ffn_gain, grad_head_gain, grad_log_rate, grad_decay_bias = jnp.split(sums, ends)
    grad_w_query, grad_w_key, grad_w_value = apart(grad_qkv, keys, keys, vals)
    grad_gate_out, grad_pair = grad_gate_out.astype(F32), grad_pair.astype(F32)
    return (
        hidden_out,
        grad_in,
        grad_mix_gain,
        grad_w_query,
        grad_w_key,
        grad_w_value,
        grad_kernels[:, : cut[0]],
        grad_kernels[:, cut[0] : cut[1]],
        grad_kernels[:, cut[1] :],
        grad_narrow[:, :heads],
        grad_narrow[:, heads:],
        grad_log_rate,
        grad_decay_bias,
        grad_gate_out[:, :vals],
        grad_head_gain,
        grad_gate_out[:, vals:].T,
        grad_ffn_gain,
        grad_pair[:, :hidden],
        grad_pair[:, hidden:],
        grad_w_down.astype(F32),
    )


def solution(mesh):
    rows, both, flat = P(("dp", "tensor"), None), P("dp", "tensor"), P(None, ("tensor", "dp"))
    turned = P("tensor", "dp")
    return jax.shard_map(
        local,
        mesh=mesh,
        in_specs=(
            *(rows, rows, P()),
            *(both, both, both, flat, flat, flat, both, both),
            *(P(), P(), both, P(), turned, P(), both, both, turned),
        ),
        out_specs=(
            *(rows, rows, P()),
            *(both, both, both, flat, flat, flat, both, both),
            *(P(), P(), both, P(), turned, P(), both, both, turned),
        ),
        check_vma=False,
    )
```
